512 devices in a mesh: tm: 16 (over z), space: 32 (over x, y, core).
Axes of the slice: x: 4, y: 4, z: 16, core: 2. Of those that a mesh axis runs over, the one named last changes fastest.
Arguments:
- right_side: float32 [64, 256, 16, 128], P('tm', 'space'), may hold values from -7 to 7, as said below
- state: float32 [64, 256, 16, 128], P('tm', 'space'), may hold values from -1 to 1
Outputs:
- correction: float32 [64, 256, 16, 128], P('tm', 'space')
The draws below stay inside these ranges and needn't reach their ends.
Inputs may be any that keep to these rules, and one draw needn't show every extreme that they name: `right_side`: a rough field plus a smooth part.
All inputs are finite; a program needn't handle non-finite values.
Results may differ from the reference program's by a relative error of at most 0.0003.
Values sent between devices are 32-bit elements; how exact they have to be, the bound alone decides.
No kernel may reach another device: no remote copies, remote signals or barrier semaphores. Data moves between devices by JAX's collectives and lax.ppermute only.
A program may use at most 64 MiB of HBM per device.

```python
import jax
import jax.numpy as jnp
from jax import lax

CX = 16
CY = 128
CT = 4
CZ = 8
OV = 2
OT = 2
SWEEPS = 4
CHEB = 8
NT = 64
NZ = 256
NTC = 8
NZC = 64
N_TM = 16
N_SPACE = 32


def draw_right_side(key, part):
    key = jax.random.fold_in(key, 11)
    rough_key, amp_key, phase_key = jax.random.split(key, 3)
    shape = (NT, NZ, CX, CY)
    tpos = jnp.arange(NT, dtype=jnp.float32)[:, None, None, None]
    zpos = jnp.arange(NZ, dtype=jnp.float32)[None, :, None, None]
    xpos = jnp.arange(CX, dtype=jnp.float32)[None, None, :, None]
    ypos = jnp.arange(CY, dtype=jnp.float32)[None, None, None, :]
    amps = jax.random.uniform(amp_key, (3,), jnp.float32, 0.5, 1.0)
    phases = jax.random.uniform(phase_key, (4,), jnp.float32, 0.0, 6.2831853)
    smooth = (0.8 * amps[0] + 0.8) * jnp.sin(6.2831853 * zpos / NZ + phases[0]) * jnp.cos(3.1415927 * tpos / NT + phases[1])
    smooth = smooth + 0.5 * amps[2] * jnp.sin(6.2831853 * xpos / CX + phases[2])
    smooth = smooth + jnp.sin(6.2831853 * ypos / CY + phases[3])
    rough = jnp.clip(jax.random.normal(rough_key, shape, jnp.float32), -3.9, 3.9)
    return rough + smooth


def level_of(key, extent, cuts, least, high):
    def one(position, shards_of):
        steps = jax.random.uniform(jax.random.fold_in(jax.random.fold_in(key, 6), position), (shards_of,), jnp.float32, least / len(cuts), high / len(cuts))
        return jnp.repeat(jnp.exp(steps), extent[position] // shards_of).reshape((-1,) + (1,) * (len(extent) - position - 1))

    loudness = one(*cuts[0])
    for cut in cuts[1:]:
        loudness = loudness * one(*cut)
    return loudness


def setup_inputs(seed: int = 0) -> dict:
    arg_keys = jax.random.split(jax.random.key(seed), 3)
    return {
        "right_side": draw_right_side(jax.random.fold_in(arg_keys[2], 71), 0),
        "state": jnp.clip(jax.random.uniform(arg_keys[1], (NT, NZ, CX, CY), jnp.float32, -1.0, 1.0) * level_of(arg_keys[1], (NT, NZ, CX, CY), ((0, 16), (1, 32)), -0.4, 0.0), -1.0, 1.0),
    }


rate = 8.0
react = 0.5
damp = 0.9


def spatial_sum(padded_z, field):
    total = padded_z[:, 2:] + padded_z[:, :-2]
    total = total + jnp.roll(field, 1, axis=2) + jnp.roll(field, -1, axis=2)
    total = total + jnp.roll(field, 1, axis=3) + jnp.roll(field, -1, axis=3)
    return total


def sweep_block(rhs, coef, tmask):
    diag = rate + 6.0 + react * coef
    field = jnp.zeros_like(rhs)
    for sweep in range(SWEEPS):
        padded_z = jnp.pad(field, ((0, 0), (1, 1), (0, 0), (0, 0)))
        before = jnp.pad(field, ((1, 0), (0, 0), (0, 0), (0, 0)))[:-1]
        applied = diag * field - rate * before - spatial_sum(padded_z, field)
        field = (field + damp * (rhs - applied) / diag) * tmask[:, None, None, None]
    return field


def coarse_apply(field, coarse_coef):
    width = CY // 4
    yidx = jnp.arange(field.shape[-1], dtype=jnp.int32) % width
    yplus = jnp.where(yidx == width - 1, jnp.roll(field, width - 1, axis=-1), jnp.roll(field, -1, axis=-1))
    yminus = jnp.where(yidx == 0, jnp.roll(field, -(width - 1), axis=-1), jnp.roll(field, 1, axis=-1))
    beside = jnp.roll(field, 1, axis=1) + jnp.roll(field, -1, axis=1)
    beside = beside + jnp.roll(field, width, axis=2) + jnp.roll(field, -width, axis=2)
    beside = beside + yplus + yminus
    before = jnp.pad(field, ((1, 0), (0, 0), (0, 0)))[:-1]
    return 1.0 * (field - before) + (6.0 * field - beside) / 16.0 + react * coarse_coef * field


def coarse_solve(coarse_rhs, coarse_coef):
    theta = 0.8
    delta = 0.6
    diag = 1.375 + react * coarse_coef
    sol = jnp.zeros_like(coarse_rhs)
    resid = coarse_rhs
    step_dir = resid / (diag * theta)
    rho = delta / theta
    for step in range(CHEB):
        sol = sol + step_dir
        if step + 1 < CHEB:
            resid = resid - coarse_apply(step_dir, coarse_coef)
            rho_next = 1.0 / (2.0 * theta / delta - rho)
            step_dir = rho_next * rho * step_dir + (2.0 * rho_next / delta) * (resid / diag)
            rho = rho_next
    return sol


def reference(right_side, state):
    coef = 3.0 * state * state - 1.0
    stacked = jnp.stack([right_side, coef])
    stacked = jnp.concatenate([stacked[:, :, NZ - OV:], stacked, stacked[:, :, :OV]], axis=2)
    stacked = jnp.pad(stacked, ((0, 0), (OT, 0), (0, 0), (0, 0), (0, 0)))

    def one_block(index):
        slab = index // N_SPACE
        plane = index % N_SPACE
        zero = jnp.int32(0)
        block = lax.dynamic_slice(stacked, (zero, (slab * CT).astype(jnp.int32), (plane * CZ).astype(jnp.int32), zero, zero), (2, CT + OT, CZ + 2 * OV, CX, CY))
        first = (slab > 0).astype(jnp.float32)
        tmask = jnp.concatenate([jnp.zeros((OT,), jnp.float32) + first, jnp.ones((CT,), jnp.float32)])
        field = sweep_block(block[0], block[1], tmask)
        return field[OT:, OV:OV + CZ]

    blocks = lax.map(one_block, jnp.arange(N_TM * N_SPACE, dtype=jnp.int32))
    blocks = blocks.reshape(N_TM, N_SPACE, CT, CZ, CX, CY).transpose(0, 2, 1, 3, 4, 5)
    local_part = blocks.reshape(NT, NZ, CX, CY)
    padded_z = jnp.concatenate([local_part[:, NZ - 1:], local_part, local_part[:, :1]], axis=1)
    before = jnp.pad(local_part, ((1, 0), (0, 0), (0, 0), (0, 0)))[:-1]
    applied = (rate + 6.0 + react * coef) * local_part - rate * before - spatial_sum(padded_z, local_part)
    after = right_side - applied
    both = jnp.stack([after, coef]).reshape(2, NTC, 8, NZC, 4, CX // 4, 4, CY // 4, 4)
    coarse = jnp.sum(both, axis=(2, 4, 6, 8)) * (1.0 / 512.0)
    coarse = coarse.reshape(2, NTC, NZC, (CX // 4) * (CY // 4))
    coarse_solution = coarse_solve(coarse[0], coarse[1])
    spread = coarse_solution.reshape(NTC, 1, NZC, 1, CX // 4, 1, CY // 4, 1)
    spread = jnp.broadcast_to(spread, (NTC, 8, NZC, 4, CX // 4, 4, CY // 4, 4)).reshape(NT, NZ, CX, CY)
    return local_part + spread
```

```python
import functools

import jax
import jax.numpy as jnp
from jax import lax
from jax.experimental import pallas as pl
from jax.experimental.pallas import tpu as pltpu
from jax.sharding import PartitionSpec as P

CX = 16
CY = 128
CT = 4
CZ = 8
OV = 2
SWEEPS = 4
CHEB = 8
LANES = 128
SLOTS = 8
NEAR = 4
GROUP = 2 * NEAR

rate = 8.0
react = 0.5
damp = 0.9
theta = 0.8
delta = 0.6

F32 = jnp.float32
PLANE = (CX, CY)
VMEM = pl.BlockSpec(memory_space=pltpu.VMEM)
SMEM = pl.BlockSpec(memory_space=pltpu.SMEM)


def params():
    return pltpu.CompilerParams(vmem_limit_bytes=32 * 1024 * 1024)


def beside(v):
    total = pltpu.roll(v, 1, 0) + pltpu.roll(v, CX - 1, 0)
    return total + (pltpu.roll(v, 1, 1) + pltpu.roll(v, CY - 1, 1))


def swept(v, first, scale, near, before):
    total = beside(v)
    for plane in near:
        if plane is not None:
            total = total + plane
    if before is not None:
        total = total + rate * before
    return (1.0 - damp) * v + first + scale * total


def first_kernel(rhs_ref, state_ref, both_ref, up_ref, down_ref):
    for t in range(CT):
        for z in range(CZ):
            s = state_ref[t, z]
            diag = (rate + 6.0 - react) + (3.0 * react) * (s * s)
            scale = damp / diag
            first = scale * rhs_ref[t, z]
            both_ref[0, t, z] = scale
            both_ref[1, t, z] = first
            if z >= CZ - OV:
                up_ref[0, t, z - (CZ - OV)] = scale
                up_ref[1, t, z - (CZ - OV)] = first
            if z < OV:
                down_ref[0, t, z] = scale
                down_ref[1, t, z] = first


def reader(which, both_ref, low_ref, high_ref):
    def read(t, z):
        if z < 0:
            return low_ref[which, t, z + OV]
        if z >= CZ:
            return high_ref[which, t, z - CZ]
        return both_ref[which, t, z]

    return read


def later_kernel(both_ref, low_ref, high_ref, out_ref):
    scale = reader(0, both_ref, low_ref, high_ref)
    first = reader(1, both_ref, low_ref, high_ref)
    a, b = CT - 2, CT - 1
    off2 = CZ
    off1 = off2 + CZ + 2
    for z in range(-2, CZ + 2):
        out_ref[off1 + z + 2] = first(b, z)
    for z in range(-1, CZ + 1):
        v = first(b, z)
        out_ref[off2 + z + 1] = swept(
            v, v, scale(b, z), (first(b, z - 1), first(b, z + 1)), first(a, z)
        )
    for z in range(CZ):
        v = first(a, z)
        second = swept(v, v, scale(a, z), (first(a, z - 1), first(a, z + 1)), None)
        out_ref[z] = swept(
            out_ref[off2 + z + 1],
            first(b, z),
            scale(b, z),
            (out_ref[off2 + z], out_ref[off2 + z + 2]),
            second,
        )


def fold_matrix(rows, columns, fine_first):
    i = lax.broadcasted_iota(jnp.int32, (rows, columns), 0)
    k = lax.broadcasted_iota(jnp.int32, (rows, columns), 1)
    fine, lane = (i, k) if fine_first else (k, i)
    return jnp.where(lax.shift_right_logical(fine, 2) == (lane & (CY // 4 - 1)), 1.0, 0.0)


def x_mask():
    x = lax.broadcasted_iota(jnp.int32, PLANE, 0)
    lane = lax.broadcasted_iota(jnp.int32, PLANE, 1)
    return jnp.where(lax.shift_right_logical(x, 2) == lax.shift_right_logical(lane, 5), 1.0, 0.0)


def main_kernel(
    rhs_ref, state_ref, both_ref, low_ref, high_ref, prev_ref, lp_ref, sums_ref, v2, v3, stack
):
    scale = reader(0, both_ref, low_ref, high_ref)
    own = reader(1, both_ref, low_ref, high_ref)
    off2 = CZ
    off1 = off2 + CZ + 2

    def first(t, z):
        return prev_ref[off1 + z + 2] if t < 0 else own(t, z)

    def second(t, z):
        return prev_ref[off2 + z + 1] if t < 0 else v2[t, z + 2]

    def third(t, z):
        return prev_ref[z] if t < 0 else v3[t, z + 1]

    for t in range(CT):
        for z in range(-2, CZ + 2):
            v = own(t, z)
            near = [own(t, q) for q in (z - 1, z + 1) if -2 <= q < CZ + 2]
            v2[t, z + 2] = swept(v, v, scale(t, z), near, first(t - 1, z))
        for z in range(-1, CZ + 1):
            near = (second(t, z - 1), second(t, z + 1))
            v3[t, z + 1] = swept(second(t, z), own(t, z), scale(t, z), near, second(t - 1, z))
        for z in range(CZ):
            near = (third(t, z - 1), third(t, z + 1))
            lp_ref[t, z] = swept(third(t, z), own(t, z), scale(t, z), near, third(t - 1, z))

    rest = []
    planes = []
    coefs = []
    for z in range(CZ):
        part = None
        square = None
        for t in range(CT):
            s = state_ref[t, z]
            q = s * s
            diag = (rate + 6.0 - react) + (3.0 * react) * q
            term = rhs_ref[t, z] - diag * lp_ref[t, z]
            part = term if part is None else part + term
            square = q if square is None else square + q
        early = lp_ref[0, z]
        for t in range(1, CT - 1):
            early = early + lp_ref[t, z]
        rest.append(part + rate * early)
        planes.append(early + lp_ref[CT - 1, z])
        coefs.append(3.0 * square - float(CT))
    for b in range(2):
        z = 4 * b
        total = planes[z] + planes[z + 1] + planes[z + 2] + planes[z + 3]
        inner = planes[z] + planes[z + 3] + 2.0 * (planes[z + 1] + planes[z + 2])
        inner = inner + (planes[4] if b == 0 else planes[3])
        value = rest[z] + rest[z + 1] + rest[z + 2] + rest[z + 3]
        stack[b] = value + beside(total) + inner
        last = lp_ref[CT - 1, z] + lp_ref[CT - 1, z + 1]
        last = last + (lp_ref[CT - 1, z + 2] + lp_ref[CT - 1, z + 3])
        stack[4 + b] = rate * last
        stack[6 + b] = coefs[z] + coefs[z + 1] + coefs[z + 2] + coefs[z + 3]
    stack[2] = planes[0]
    stack[3] = planes[CZ - 1]
    folded = jnp.dot(
        stack[...].reshape(8 * CX, CY),
        fold_matrix(CY, LANES, True),
        precision=lax.Precision.HIGHEST,
        preferred_element_type=F32,
    )
    sums = jnp.sum(folded.reshape(8, CX, LANES) * x_mask()[None], axis=1)
    sums_ref[...] = jnp.broadcast_to(sums[None], sums_ref.shape)


def slots_kernel(all_ref, out_ref):
    def row(r):
        return all_ref[:, 0, r, :] + all_ref[:, 1, r, :]

    slot = lax.broadcasted_iota(jnp.int32, (SLOTS, LANES), 0)
    rows = []
    for b in range(2):
        odd = jnp.where(slot == 0, 0.0, pltpu.roll(all_ref[:, 1, 4 + b, :], 1, 0))
        rows.append(row(b) + all_ref[:, 0, 4 + b, :] + odd)
    rows += [row(2), row(3), row(6), row(7)]
    for r, value in enumerate(rows):
        value = value * (1.0 / 512.0)
        for k in range(out_ref.shape[0]):
            out_ref[k, r] = value


def coarse_kernel(at_ref, lp_ref, here_ref, beside_ref, out_ref, found):
    index = at_ref[0]
    slot = at_ref[1]
    place = index & (GROUP - 1)
    late = place >= NEAR
    start = place & (NEAR - 1)
    devices = 3 * NEAR
    low = [beside_ref[k] for k in range(NEAR)]
    parts = []
    for k in range(devices):
        early_part = beside_ref[k] if k < NEAR else here_ref[k - NEAR]
        late_part = here_ref[k] if k < GROUP else beside_ref[k - NEAR]
        parts.append(jnp.where(late, late_part, early_part))
    n = 2 * devices
    rhs = []
    diag = []
    for k in range(devices):
        a0, a1, c0, c1 = parts[k][0], parts[k][1], parts[k][4], parts[k][5]
        if k > 0:
            a0 = a0 + parts[k - 1][3]
        if k + 1 < devices:
            a1 = a1 + parts[k + 1][2]
        rhs += [a0, a1]
        diag += [1.375 + react * c0, 1.375 + react * c1]
    lane = lax.broadcasted_iota(jnp.int32, (SLOTS, LANES), 1) & (CY // 4 - 1)
    slots = lax.broadcasted_iota(jnp.int32, (SLOTS, LANES), 0)
    width = CY // 4
    is_first, is_last, is_start = lane == 0, lane == width - 1, slots == 0

    def around(f):
        total = pltpu.roll(f, width, 1) + pltpu.roll(f, LANES - width, 1)
        after = jnp.where(is_last, pltpu.roll(f, width - 1, 1), pltpu.roll(f, LANES - 1, 1))
        before = jnp.where(is_first, pltpu.roll(f, LANES - width + 1, 1), pltpu.roll(f, 1, 1))
        return total + (after + before)

    def earlier(f):
        return jnp.where(is_start, 0.0, pltpu.roll(f, 1, 0))

    inverse = [1.0 / d for d in diag]
    resid = [r * i for r, i in zip(rhs, inverse)]
    step = [r * (1.0 / theta) for r in resid]
    mine = range(2 * NEAR, 4 * NEAR)
    sol = {r: step[r] for r in mine}
    rho = delta / theta
    for k in range(1, CHEB):
        nxt = 1.0 / (2.0 * theta / delta - rho)
        new_resid = list(resid)
        new_step = list(step)
        for r in range(1 + k, n - 1 - k):
            spread = around(step[r]) + (step[r - 1] + step[r + 1])
            flow = earlier(step[r]) + spread * (1.0 / 16.0)
            new_resid[r] = resid[r] - step[r] + flow * inverse[r]
            new_step[r] = (nxt * rho) * step[r] + (2.0 * nxt / delta) * new_resid[r]
        resid, step, rho = new_resid, new_step, nxt
        for r in mine:
            sol[r] = sol[r] + step[r]
    for r in mine:
        found[r - 2 * NEAR] = sol[r]
    mask = x_mask()
    spread = [found[2 * start + b, pl.ds(slot, 1), :] * mask for b in range(2)]
    fine = jnp.dot(
        jnp.concatenate(spread, axis=0),
        fold_matrix(LANES, CY, False),
        precision=lax.Precision.HIGHEST,
        preferred_element_type=F32,
    )
    for b in range(2):
        value = fine[b * CX : (b + 1) * CX]
        for t in range(CT):
            for z in range(4):
                out_ref[t, 4 * b + z] = lp_ref[t, 4 * b + z] + value


def call(kernel, shapes, n_in, scratch=(), smem=0):
    single = not isinstance(shapes, (list, tuple))
    outs = [shapes] if single else list(shapes)
    specs = [VMEM] * len(outs)
    return pl.pallas_call(
        kernel,
        out_shape=shapes if single else outs,
        in_specs=[SMEM] * smem + [VMEM] * n_in,
        out_specs=VMEM if single else specs,
        scratch_shapes=list(scratch),
        compiler_params=params(),
    )


def arr(*shape):
    return jax.ShapeDtypeStruct(shape, F32)


def local(right_side, state):
    slabs = lax.axis_size("tm")
    planes = lax.axis_size("space")
    slab = lax.axis_index("tm")
    plane = lax.axis_index("space")
    up = [(i, (i + 1) % planes) for i in range(planes)]
    down = [(j, i) for i, j in up]
    onward = [(i, i + 1) for i in range(slabs - 1)]

    edge = arr(2, CT, OV, CX, CY)
    both, top, bottom = call(first_kernel, [arr(2, CT, CZ, CX, CY), edge, edge], 2)(
        right_side, state
    )
    low = lax.ppermute(top, "space", up)
    high = lax.ppermute(bottom, "space", down)
    count = 3 * CZ + 6
    sent = call(later_kernel, arr(count, CX, CY), 3)(both, low, high)
    prev = lax.ppermute(sent, "tm", onward)
    lp, sums = call(
        main_kernel,
        [arr(CT, CZ, CX, CY), arr(slabs, 8, LANES)],
        6,
        [
            pltpu.VMEM((CT, CZ + 4, CX, CY), F32),
            pltpu.VMEM((CT, CZ + 2, CX, CY), F32),
            pltpu.VMEM((8, CX, CY), F32),
        ],
    )(right_side, state, both, low, high, prev)
    every = lax.all_to_all(sums, "tm", 0, 0)
    slots = call(slots_kernel, arr(GROUP, 6, SLOTS, LANES), 1)(
        every.reshape(slabs // 2, 2, 8, LANES)
    )
    groups = [[GROUP * g + k for k in range(GROUP)] for g in range(planes // GROUP)]
    shifted = [[(q + NEAR) % planes for q in group] for group in groups]
    here = lax.all_to_all(slots, "space", 0, 0, axis_index_groups=groups)
    other = lax.all_to_all(slots, "space", 0, 0, axis_index_groups=shifted)
    at = jnp.stack([plane, slab // 2]).astype(jnp.int32)
    return call(
        coarse_kernel,
        arr(CT, CZ, CX, CY),
        3,
        [pltpu.VMEM((2 * NEAR, SLOTS, LANES), F32)],
        smem=1,
    )(at, lp, here, other)


def solution(mesh):
    return jax.shard_map(
        local,
        mesh=mesh,
        in_specs=(P("tm", "space", None, None), P("tm", "space", None, None)),
        out_specs=P("tm", "space", None, None),
        check_vma=False,
    )
```

```python
import jax
import jax.numpy as jnp
from jax import lax
from jax.experimental import pallas as pl
from jax.experimental.pallas import tpu as pltpu
from jax.sharding import PartitionSpec as P

CX = 16
CY = 128
CT = 4
CZ = 8
OV = 2
SWEEPS = 4
CHEB = 8
LANES = 128
NEAR = 4
WINDOW = 16

rate = 8.0
react = 0.5
damp = 0.9
theta = 0.8
delta = 0.6

F32 = jnp.float32
PLANE = (CX, CY)
VMEM = pl.BlockSpec(memory_space=pltpu.VMEM)


def beside(v):
    total = pltpu.roll(v, 1, 0) + pltpu.roll(v, CX - 1, 0)
    return total + (pltpu.roll(v, 1, 1) + pltpu.roll(v, CY - 1, 1))


def swept(v, first, scale, near, before):
    total = beside(v)
    for plane in near:
        if plane is not None:
            total = total + plane
    if before is not None:
        total = total + rate * before
    return (1.0 - damp) * v + first + scale * total


def by_parity(body, first, second):
    odd = at_ref[0] & 1

    @pl.when(odd == 0)
    def _():
        body(first, second)

    @pl.when(odd == 1)
    def _():
        body(second, first)


def by_parity(body, first, second):
    odd = lax.axis_index("space") & 1

    @pl.when(odd == 0)
    def _():
        body(first, second)

    @pl.when(odd == 1)
    def _():
        body(second, first)


def first_kernel(rhs_ref, state_ref, own_ref, outer_ref, inner_ref):
    def body(low_ref, high_ref):
        for t in range(CT):
            for z in range(CZ):
                rhs, s = rhs_ref[t, z], state_ref[t, z]
                diag = (rate + 6.0 - react) + (3.0 * react) * (s * s)
                scale = damp / diag
                first = scale * rhs
                for which, value in enumerate((scale, first, diag, rhs)):
                    own_ref[which, t, z] = value
                if z < OV:
                    low_ref[0, t, z], low_ref[1, t, z] = scale, first
                if z >= CZ - OV:
                    high_ref[0, t, z - (CZ - OV)] = scale
                    high_ref[1, t, z - (CZ - OV)] = first

    by_parity(body, outer_ref, inner_ref)


def reader(which, own_ref, low_ref, high_ref):
    def read(t, z):
        if z < 0:
            return low_ref[which, t, z + OV]
        if z >= CZ:
            return high_ref[which, t, z - CZ]
        return own_ref[which, t, z]

    return read


def later_kernel(own_ref, outer_ref, inner_ref, out_ref):
    off2 = CZ
    off1 = off2 + CZ + 2
    a, b = CT - 2, CT - 1

    def body(low_ref, high_ref):
        scale = reader(0, own_ref, low_ref, high_ref)
        first = reader(1, own_ref, low_ref, high_ref)
        for z in range(-2, CZ + 2):
            out_ref[off1 + z + 2] = first(b, z)
        for z in range(-1, CZ + 1):
            v = first(b, z)
            near = (first(b, z - 1), first(b, z + 1))
            out_ref[off2 + z + 1] = swept(v, v, scale(b, z), near, first(a, z))
        for z in range(CZ):
            v = first(a, z)
            second = swept(v, v, scale(a, z), (first(a, z - 1), first(a, z + 1)), None)
            near = (out_ref[off2 + z], out_ref[off2 + z + 2])
            out_ref[z] = swept(out_ref[off2 + z + 1], first(b, z), scale(b, z), near, second)

    by_parity(body, outer_ref, inner_ref)


def fold_matrix(rows, columns, fine_first):
    i = lax.broadcasted_iota(jnp.int32, (rows, columns), 0)
    k = lax.broadcasted_iota(jnp.int32, (rows, columns), 1)
    fine, lane = (i, k) if fine_first else (k, i)
    return jnp.where(lax.shift_right_logical(fine, 2) == (lane & (CY // 4 - 1)), 1.0, 0.0)


def x_mask():
    x = lax.broadcasted_iota(jnp.int32, PLANE, 0)
    lane = lax.broadcasted_iota(jnp.int32, PLANE, 1)
    return jnp.where(lax.shift_right_logical(x, 2) == lax.shift_right_logical(lane, 5), 1.0, 0.0)


def main_kernel(
    own_ref,
    outer_ref,
    inner_ref,
    prev_ref,
    lp_ref,
    sums_ref,
    v2,
    v3,
    stack,
):
    off2 = CZ
    off1 = off2 + CZ + 2

    def body(low_ref, high_ref):
        scale = reader(0, own_ref, low_ref, high_ref)
        own = reader(1, own_ref, low_ref, high_ref)

        def first(t, z):
            return prev_ref[off1 + z + 2] if t < 0 else own(t, z)

        def second(t, z):
            return prev_ref[off2 + z + 1] if t < 0 else v2[t, z + 2]

        def third(t, z):
            return prev_ref[z] if t < 0 else v3[t, z + 1]

        for t in range(CT):
            for z in range(-2, CZ + 2):
                v = own(t, z)
                near = [own(t, q) for q in (z - 1, z + 1) if -2 <= q < CZ + 2]
                v2[t, z + 2] = swept(v, v, scale(t, z), near, first(t - 1, z))
            for z in range(-1, CZ + 1):
                near = (second(t, z - 1), second(t, z + 1))
                v3[t, z + 1] = swept(second(t, z), own(t, z), scale(t, z), near, second(t - 1, z))
            for z in range(CZ):
                near = (third(t, z - 1), third(t, z + 1))
                lp_ref[t, z] = swept(third(t, z), own(t, z), scale(t, z), near, third(t - 1, z))

    by_parity(body, outer_ref, inner_ref)

    rest = []
    planes = []
    coefs = []
    for z in range(CZ):
        part = None
        diags = None
        for t in range(CT):
            diag = own_ref[2, t, z]
            term = own_ref[3, t, z] - diag * lp_ref[t, z]
            part = term if part is None else part + term
            diags = diag if diags is None else diags + diag
        early = lp_ref[0, z]
        for t in range(1, CT - 1):
            early = early + lp_ref[t, z]
        rest.append(part + rate * early)
        planes.append(early + lp_ref[CT - 1, z])
        coefs.append((diags - CT * (rate + 6.0)) * (1.0 / react))
    for b in range(2):
        z = 4 * b
        total = planes[z] + planes[z + 1] + planes[z + 2] + planes[z + 3]
        inner = planes[z] + planes[z + 3] + 2.0 * (planes[z + 1] + planes[z + 2])
        inner = inner + (planes[4] if b == 0 else planes[3])
        value = rest[z] + rest[z + 1] + rest[z + 2] + rest[z + 3]
        stack[b] = value + beside(total) + inner
        last = lp_ref[CT - 1, z] + lp_ref[CT - 1, z + 1]
        last = last + (lp_ref[CT - 1, z + 2] + lp_ref[CT - 1, z + 3])
        stack[4 + b] = rate * last
        stack[6 + b] = coefs[z] + coefs[z + 1] + coefs[z + 2] + coefs[z + 3]
    stack[2] = planes[0]
    stack[3] = planes[CZ - 1]
    folded = jnp.dot(
        stack[...].reshape(8 * CX, CY),
        fold_matrix(CY, LANES, True),
        precision=lax.Precision.HIGHEST,
        preferred_element_type=F32,
    )
    sums = jnp.sum(folded.reshape(8, CX, LANES) * x_mask()[None], axis=1)
    sums_ref[...] = jnp.broadcast_to(sums[None], sums_ref.shape)


def window_kernel(all_ref, out_ref, rows):
    plane = lax.axis_index("space")
    count = all_ref.shape[0]
    parts = [all_ref[lax.rem(plane + (count - NEAR + k), count)] for k in range(2 * NEAR + 1)]
    for k, part in enumerate(parts):
        low, high = part[0:1], part[1:2]
        if k > 0:
            low = low + parts[k - 1][3:4]
        if k < 2 * NEAR:
            high = high + parts[k + 1][2:3]
        if k > 0:
            rows[0, 2 * k - 1 : 2 * k] = low
            rows[1, 2 * k - 1 : 2 * k] = part[4:5]
            rows[2, 2 * k - 1 : 2 * k] = part[6:7]
        if k < 2 * NEAR:
            rows[0, 2 * k : 2 * k + 1] = high
            rows[1, 2 * k : 2 * k + 1] = part[5:6]
            rows[2, 2 * k : 2 * k + 1] = part[7:8]
    value = rows[...]
    for k in range(out_ref.shape[0]):
        out_ref[k] = value


def coarse_steps(all_ref, bound_ref):
    shape = (WINDOW, LANES)
    lane = lax.broadcasted_iota(jnp.int32, shape, 1) & (CY // 4 - 1)
    row = lax.broadcasted_iota(jnp.int32, shape, 0)
    width = CY // 4
    is_first, is_last = lane == 0, lane == width - 1
    bottom, top = row == 0, row == WINDOW - 1

    def around(f):
        total = pltpu.roll(f, width, 1) + pltpu.roll(f, LANES - width, 1)
        after = jnp.where(is_last, pltpu.roll(f, width - 1, 1), pltpu.roll(f, LANES - 1, 1))
        before = jnp.where(is_first, pltpu.roll(f, LANES - width + 1, 1), pltpu.roll(f, 1, 1))
        below = jnp.where(bottom, 0.0, pltpu.roll(f, 1, 0))
        above = jnp.where(top, 0.0, pltpu.roll(f, WINDOW - 1, 0))
        return total + (after + before) + (below + above)

    slots = all_ref.shape[0] // 2
    inverse = []
    resid = []
    for k in range(slots):
        rhs = all_ref[2 * k, 0] + all_ref[2 * k, 1] + all_ref[2 * k + 1, 0]
        if k > 0:
            rhs = rhs + all_ref[2 * k - 1, 1]
        elif bound_ref is not None:
            rhs = rhs + bound_ref[4]
        coef = all_ref[2 * k, 2] + all_ref[2 * k + 1, 2]
        inv = 1.0 / (1.375 + (react / 512.0) * coef)
        inverse.append(inv)
        resid.append((rhs * (1.0 / 512.0)) * inv)
    step = [r * (1.0 / theta) for r in resid]
    sol = list(step)
    rho = delta / theta
    last = []
    for m in range(1, CHEB):
        nxt = 1.0 / (2.0 * theta / delta - rho)
        last.append(step[-1])
        flows = []
        for k in range(slots):
            flow = around(step[k]) * (1.0 / 16.0)
            if k > 0:
                flow = flow + step[k - 1]
            elif bound_ref is not None:
                flow = flow + (bound_ref[m - 1] if m <= 4 else swapped(bound_ref[7 - m]))
            flows.append(flow)
        for k in range(slots):
            resid[k] = resid[k] - step[k] + flows[k] * inverse[k]
            step[k] = (nxt * rho) * step[k] + (2.0 * nxt / delta) * resid[k]
            sol[k] = sol[k] + step[k]
        rho = nxt
    return sol, last


def swapped(v):
    return jnp.concatenate([v[WINDOW // 2 :], v[: WINDOW // 2]], axis=0)


def bound_kernel(all_ref, out_ref):
    _, last = coarse_steps(all_ref, None)
    row = lax.broadcasted_iota(jnp.int32, (WINDOW, LANES), 0)
    for m in range(3):
        used = (row > m) & (row < WINDOW - 1 - m)
        out_ref[m] = jnp.where(used, last[m], swapped(last[6 - m]))
    out_ref[3] = last[3]
    out_ref[4] = all_ref[all_ref.shape[0] - 1, 1]


def coarse_kernel(lp_ref, all_ref, bound_ref, out_ref, found):
    sol, _ = coarse_steps(all_ref, bound_ref)
    for k, value in enumerate(sol):
        found[k] = value
    slot = lax.rem(lax.axis_index("tm"), all_ref.shape[0]) // 2
    mask = x_mask()
    mine = 2 * NEAR - 1
    spread = [found[slot, mine + b : mine + b + 1] * mask for b in range(2)]
    fine = jnp.dot(
        jnp.concatenate(spread, axis=0),
        fold_matrix(LANES, CY, False),
        precision=lax.Precision.HIGHEST,
        preferred_element_type=F32,
    )
    for b in range(2):
        value = fine[b * CX : (b + 1) * CX]
        for t in range(CT):
            for z in range(4):
                out_ref[t, 4 * b + z] = lp_ref[t, 4 * b + z] + value


def call(kernel, shapes, count, scratch=()):
    single = not isinstance(shapes, (list, tuple))
    return pl.pallas_call(
        kernel,
        out_shape=shapes if single else list(shapes),
        in_specs=[VMEM] * count,
        out_specs=VMEM if single else [VMEM] * len(shapes),
        scratch_shapes=list(scratch),
        compiler_params=pltpu.CompilerParams(vmem_limit_bytes=32 << 20),
    )


def arr(*shape):
    return jax.ShapeDtypeStruct(shape, F32)


def local(right_side, state):
    slabs = lax.axis_size("tm")
    planes = lax.axis_size("space")
    half = slabs // 2
    across = [(k, (k + 1) % planes) for k in range(1, planes, 2)]
    across += [(b, a) for a, b in across]
    within = [(k, k + 1) for k in range(0, planes, 2)]
    within += [(b, a) for a, b in within]
    onward = [(i, i + 1) for i in range(slabs - 1)]

    edge = arr(2, CT, OV, CX, CY)
    own, outer, inner = call(first_kernel, [arr(4, CT, CZ, CX, CY), edge, edge], 2)(
        right_side, state
    )
    outer = lax.ppermute(outer, "space", across)
    inner = lax.ppermute(inner, "space", within)
    sent = call(later_kernel, arr(3 * CZ + 6, CX, CY), 3)(own, outer, inner)
    prev = lax.ppermute(sent, "tm", onward)
    lp, sums = call(
        main_kernel,
        [arr(CT, CZ, CX, CY), arr(planes, 8, LANES)],
        4,
        [
            pltpu.VMEM((CT, CZ + 4, CX, CY), F32),
            pltpu.VMEM((CT, CZ + 2, CX, CY), F32),
            pltpu.VMEM((8, CX, CY), F32),
        ],
    )(own, outer, inner, prev)
    column = lax.all_to_all(sums, "space", 0, 0)
    window = call(
        window_kernel,
        arr(half, 3, WINDOW, LANES),
        1,
        [pltpu.VMEM((3, WINDOW, LANES), F32)],
    )(column)
    halves = [list(range(half)), list(range(half, slabs))]
    every = lax.all_to_all(window, "tm", 0, 0, axis_index_groups=halves)
    last = call(bound_kernel, arr(5, WINDOW, LANES), 1)(every)
    quarter = half // 2
    serve = [(i, i + quarter) for i in range(quarter, half)]
    serve += [(i, i + half + quarter) for i in range(quarter)]
    bound = lax.ppermute(last, "tm", serve)
    return call(
        coarse_kernel,
        arr(CT, CZ, CX, CY),
        3,
        [pltpu.VMEM((half // 2, WINDOW, LANES), F32)],
    )(lp, every, bound)


def solution(mesh):
    return jax.shard_map(
        local,
        mesh=mesh,
        in_specs=(P("tm", "space", None, None), P("tm", "space", None, None)),
        out_specs=P("tm", "space", None, None),
        check_vma=False,
    )
```

```python
import jax
import jax.numpy as jnp
from jax import lax
from jax.experimental import pallas as pl
from jax.experimental.pallas import tpu as pltpu
from jax.sharding import PartitionSpec as P

CX = 16
CY = 128
CT = 4
CZ = 8
OV = 2
SWEEPS = 4
CHEB = 8
LANES = 128
NEAR = 4
WINDOW = 16

rate = 8.0
react = 0.5
damp = 0.9
theta = 0.8
delta = 0.6

F32 = jnp.float32
PLANE = (CX, CY)
VMEM = pl.BlockSpec(memory_space=pltpu.VMEM)


def beside(v):
    total = pltpu.roll(v, 1, 0) + pltpu.roll(v, CX - 1, 0)
    return total + (pltpu.roll(v, 1, 1) + pltpu.roll(v, CY - 1, 1))


def swept(v, first, scale, near, before):
    total = beside(v)
    for plane in near:
        if plane is not None:
            total = total + plane
    if before is not None:
        total = total + rate * before
    return (1.0 - damp) * v + first + scale * total


def by_parity(body, first, second):
    odd = at_ref[0] & 1

    @pl.when(odd == 0)
    def _():
        body(first, second)

    @pl.when(odd == 1)
    def _():
        body(second, first)


def by_parity(body, first, second):
    odd = lax.axis_index("space") & 1

    @pl.when(odd == 0)
    def _():
        body(first, second)

    @pl.when(odd == 1)
    def _():
        body(second, first)


def first_kernel(rhs_ref, state_ref, own_ref, outer_ref, inner_ref):
    def body(low_ref, high_ref):
        for t in range(CT):
            for z in range(CZ):
                rhs, s = rhs_ref[t, z], state_ref[t, z]
                diag = (rate + 6.0 - react) + (3.0 * react) * (s * s)
                scale = damp / diag
                first = scale * rhs
                for which, value in enumerate((scale, first, diag, rhs)):
                    own_ref[which, t, z] = value
                if z < OV:
                    low_ref[0, t, z], low_ref[1, t, z] = scale, first
                if z >= CZ - OV:
                    high_ref[0, t, z - (CZ - OV)] = scale
                    high_ref[1, t, z - (CZ - OV)] = first

    by_parity(body, outer_ref, inner_ref)


def reader(which, own_ref, low_ref, high_ref):
    def read(t, z):
        if z < 0:
            return low_ref[which, t, z + OV]
        if z >= CZ:
            return high_ref[which, t, z - CZ]
        return own_ref[which, t, z]

    return read


def later_kernel(own_ref, outer_ref, inner_ref, out_ref):
    off2 = CZ
    off1 = off2 + CZ + 2
    a, b = CT - 2, CT - 1

    def body(low_ref, high_ref):
        scale = reader(0, own_ref, low_ref, high_ref)
        first = reader(1, own_ref, low_ref, high_ref)
        for z in range(-2, CZ + 2):
            out_ref[off1 + z + 2] = first(b, z)
        for z in range(-1, CZ + 1):
            v = first(b, z)
            near = (first(b, z - 1), first(b, z + 1))
            out_ref[off2 + z + 1] = swept(v, v, scale(b, z), near, first(a, z))
        for z in range(CZ):
            v = first(a, z)
            second = swept(v, v, scale(a, z), (first(a, z - 1), first(a, z + 1)), None)
            near = (out_ref[off2 + z], out_ref[off2 + z + 2])
            out_ref[z] = swept(out_ref[off2 + z + 1], first(b, z), scale(b, z), near, second)

    by_parity(body, outer_ref, inner_ref)


def fold_matrix(rows, columns, fine_first):
    i = lax.broadcasted_iota(jnp.int32, (rows, columns), 0)
    k = lax.broadcasted_iota(jnp.int32, (rows, columns), 1)
    fine, lane = (i, k) if fine_first else (k, i)
    return jnp.where(lax.shift_right_logical(fine, 2) == (lane & (CY // 4 - 1)), 1.0, 0.0)


def x_mask():
    x = lax.broadcasted_iota(jnp.int32, PLANE, 0)
    lane = lax.broadcasted_iota(jnp.int32, PLANE, 1)
    return jnp.where(lax.shift_right_logical(x, 2) == lax.shift_right_logical(lane, 5), 1.0, 0.0)


def early_kernel(own_ref, outer_ref, inner_ref, v2_ref, v3_ref, v4_ref):
    def body(low_ref, high_ref):
        scale = reader(0, own_ref, low_ref, high_ref)
        first = reader(1, own_ref, low_ref, high_ref)
        for t in range(1, CT):
            for z in range(-2, CZ + 2):
                v = first(t, z)
                near = [first(t, q) for q in (z - 1, z + 1) if -2 <= q < CZ + 2]
                v2_ref[t - 1, z + 2] = swept(v, v, scale(t, z), near, first(t - 1, z))
        for t in range(2, CT):
            for z in range(-1, CZ + 1):
                near = (v2_ref[t - 1, z + 1], v2_ref[t - 1, z + 3])
                v3_ref[t - 2, z + 1] = swept(
                    v2_ref[t - 1, z + 2], first(t, z), scale(t, z), near, v2_ref[t - 2, z + 2]
                )
        t = CT - 1
        for z in range(CZ):
            near = (v3_ref[t - 2, z], v3_ref[t - 2, z + 2])
            v4_ref[z] = swept(
                v3_ref[t - 2, z + 1], first(t, z), scale(t, z), near, v3_ref[t - 3, z + 1]
            )

    by_parity(body, outer_ref, inner_ref)


def fold(planes):
    folded = jnp.dot(
        planes.reshape(-1, CY),
        fold_matrix(CY, LANES, True),
        precision=lax.Precision.HIGHEST,
        preferred_element_type=F32,
    )
    return jnp.sum(folded.reshape(-1, CX, LANES) * x_mask()[None], axis=1)


def coef_kernel(own_ref, out_ref, stack):
    stack[...] = jnp.zeros_like(stack)
    for b in range(2):
        total = None
        for t in range(CT):
            for z in range(4 * b, 4 * b + 4):
                diag = own_ref[2, t, z]
                total = diag if total is None else total + diag
        stack[4 + b] = (total - 4 * CT * (rate + 6.0)) * (1.0 / react)
    out_ref[...] = fold(stack[...])


def main_kernel(
    own_ref,
    outer_ref,
    inner_ref,
    v2_ref,
    v3_ref,
    v4_ref,
    prev_ref,
    coef_ref,
    other_coef_ref,
    lp_ref,
    sums_ref,
    v2,
    v3,
    stack,
):
    off2 = CZ
    off1 = off2 + CZ + 2

    def body(low_ref, high_ref):
        scale = reader(0, own_ref, low_ref, high_ref)
        own = reader(1, own_ref, low_ref, high_ref)

        def second(t, z):
            if t < 0:
                return prev_ref[off2 + z + 1]
            return v2[z + 2] if t == 0 else v2_ref[t - 1, z + 2]

        def third(t, z):
            if t < 0:
                return prev_ref[z]
            return v3[t, z + 1] if t < 2 else v3_ref[t - 2, z + 1]

        for z in range(-2, CZ + 2):
            v = own(0, z)
            near = [own(0, q) for q in (z - 1, z + 1) if -2 <= q < CZ + 2]
            v2[z + 2] = swept(v, v, scale(0, z), near, prev_ref[off1 + z + 2])
        for t in range(2):
            for z in range(-1, CZ + 1):
                near = (second(t, z - 1), second(t, z + 1))
                v3[t, z + 1] = swept(second(t, z), own(t, z), scale(t, z), near, second(t - 1, z))
        for t in range(CT - 1):
            for z in range(CZ):
                near = (third(t, z - 1), third(t, z + 1))
                lp_ref[t, z] = swept(third(t, z), own(t, z), scale(t, z), near, third(t - 1, z))

    by_parity(body, outer_ref, inner_ref)
    for z in range(CZ):
        lp_ref[CT - 1, z] = v4_ref[z]

    rest = []
    planes = []
    for z in range(CZ):
        part = None
        for t in range(CT):
            term = own_ref[3, t, z] - own_ref[2, t, z] * lp_ref[t, z]
            part = term if part is None else part + term
        early = lp_ref[0, z]
        for t in range(1, CT - 1):
            early = early + lp_ref[t, z]
        rest.append(part + rate * early)
        planes.append(early + lp_ref[CT - 1, z])
    odd = (lax.axis_index("tm") & 1) == 1
    for b in range(2):
        z = 4 * b
        total = planes[z] + planes[z + 1] + planes[z + 2] + planes[z + 3]
        inner = planes[z] + planes[z + 3] + 2.0 * (planes[z + 1] + planes[z + 2])
        inner = inner + (planes[4] if b == 0 else planes[3])
        value = rest[z] + rest[z + 1] + rest[z + 2] + rest[z + 3]
        value = value + beside(total) + inner
        last = lp_ref[CT - 1, z] + lp_ref[CT - 1, z + 1]
        last = rate * (last + (lp_ref[CT - 1, z + 2] + lp_ref[CT - 1, z + 3]))
        stack[b] = jnp.where(odd, value, value + last)
        stack[4 + b] = jnp.where(odd, last, 0.0)
    stack[2] = planes[0]
    stack[3] = planes[CZ - 1]
    stack[6] = jnp.zeros(PLANE, F32)
    stack[7] = jnp.zeros(PLANE, F32)
    coef = coef_ref[...] + other_coef_ref[...]
    sums = fold(stack[...]) + jnp.where(odd, 0.0, coef)
    sums_ref[...] = jnp.broadcast_to(sums[None], sums_ref.shape)


def window_kernel(all_ref, out_ref, rows):
    plane = lax.axis_index("space")
    count = all_ref.shape[0]
    parts = [all_ref[lax.rem(plane + (count - NEAR + k), count)] for k in range(2 * NEAR + 1)]
    for k, part in enumerate(parts):
        low, high = part[0:1], part[1:2]
        if k > 0:
            low = low + parts[k - 1][3:4]
        if k < 2 * NEAR:
            high = high + parts[k + 1][2:3]
        if k > 0:
            rows[0, 2 * k - 1 : 2 * k] = low
            rows[1, 2 * k - 1 : 2 * k] = part[4:5]
        if k < 2 * NEAR:
            rows[0, 2 * k : 2 * k + 1] = high
            rows[1, 2 * k : 2 * k + 1] = part[5:6]
    value = rows[...]
    for k in range(out_ref.shape[0]):
        out_ref[k] = value


def coarse_steps(all_ref, bound_ref):
    shape = (WINDOW, LANES)
    lane = lax.broadcasted_iota(jnp.int32, shape, 1) & (CY // 4 - 1)
    row = lax.broadcasted_iota(jnp.int32, shape, 0)
    width = CY // 4
    is_first, is_last = lane == 0, lane == width - 1
    bottom, top = row == 0, row == WINDOW - 1

    def around(f):
        total = pltpu.roll(f, width, 1) + pltpu.roll(f, LANES - width, 1)
        after = jnp.where(is_last, pltpu.roll(f, width - 1, 1), pltpu.roll(f, LANES - 1, 1))
        before = jnp.where(is_first, pltpu.roll(f, LANES - width + 1, 1), pltpu.roll(f, 1, 1))
        below = jnp.where(bottom, 0.0, pltpu.roll(f, 1, 0))
        above = jnp.where(top, 0.0, pltpu.roll(f, WINDOW - 1, 0))
        return total + (after + before) + (below + above)

    slots = all_ref.shape[0] // 2
    inverse = []
    resid = []
    for k in range(slots):
        rhs = all_ref[2 * k, 0] + all_ref[2 * k + 1, 0]
        if k > 0:
            rhs = rhs + all_ref[2 * k - 1, 1]
        elif bound_ref is not None:
            rhs = rhs + bound_ref[4]
        coef = all_ref[2 * k, 1]
        inv = 1.0 / (1.375 + (react / 512.0) * coef)
        inverse.append(inv)
        resid.append((rhs * (1.0 / 512.0)) * inv)
    step = [r * (1.0 / theta) for r in resid]
    sol = list(step)
    rho = delta / theta
    last = []
    for m in range(1, CHEB):
        nxt = 1.0 / (2.0 * theta / delta - rho)
        last.append(step[-1])
        flows = []
        for k in range(slots):
            flow = around(step[k]) * (1.0 / 16.0)
            if k > 0:
                flow = flow + step[k - 1]
            elif bound_ref is not None:
                flow = flow + (bound_ref[m - 1] if m <= 4 else swapped(bound_ref[7 - m]))
            flows.append(flow)
        for k in range(slots):
            resid[k] = resid[k] - step[k] + flows[k] * inverse[k]
            step[k] = (nxt * rho) * step[k] + (2.0 * nxt / delta) * resid[k]
            sol[k] = sol[k] + step[k]
        rho = nxt
    return sol, last


def swapped(v):
    return jnp.concatenate([v[WINDOW // 2 :], v[: WINDOW // 2]], axis=0)


def bound_kernel(all_ref, out_ref, mine_ref, found):
    @pl.when(lax.axis_index("tm") < all_ref.shape[0])
    def _():
        sol, last = coarse_steps(all_ref, None)
        row = lax.broadcasted_iota(jnp.int32, (WINDOW, LANES), 0)
        for m in range(3):
            used = (row > m) & (row < WINDOW - 1 - m)
            out_ref[m] = jnp.where(used, last[m], swapped(last[6 - m]))
        out_ref[3] = last[3]
        out_ref[4] = all_ref[all_ref.shape[0] - 1, 1]
        mine_ref[...] = own_slot(sol, found)


def own_slot(sol, found):
    for k, value in enumerate(sol):
        found[k] = value
    return found[lax.rem(lax.axis_index("tm"), 2 * len(sol)) // 2]


def spread(window):
    mask = x_mask()
    mine = 2 * NEAR - 1
    both = [window[mine + b : mine + b + 1] * mask for b in range(2)]
    fine = jnp.dot(
        jnp.concatenate(both, axis=0),
        fold_matrix(LANES, CY, False),
        precision=lax.Precision.HIGHEST,
        preferred_element_type=F32,
    )
    return [fine[b * CX : (b + 1) * CX] for b in range(2)]


def result_kernel(lp_ref, mine_ref, out_ref):
    for b, value in enumerate(spread(mine_ref[...])):
        for t in range(CT):
            for z in range(4 * b, 4 * b + 4):
                out_ref[t, z] = lp_ref[t, z] + value


def second_half_kernel(lp_ref, all_ref, bound_ref, _, out_ref, found, result, sems):
    @pl.when(lax.axis_index("tm") >= all_ref.shape[0])
    def _():
        sol, _ = coarse_steps(all_ref, bound_ref)
        values = spread(own_slot(sol, found))
        copies = []
        for t in range(CT):
            for b, value in enumerate(values):
                for z in range(4 * b, 4 * b + 4):
                    result[t, z] = lp_ref[t, z] + value
                part = pl.ds(4 * b, 4)
                copy = pltpu.make_async_copy(
                    result.at[t, part], out_ref.at[t, part], sems.at[2 * t + b]
                )
                copy.start()
                copies.append(copy)
        for copy in copies:
            copy.wait()


def call(kernel, shapes, count, scratch=()):
    single = not isinstance(shapes, (list, tuple))
    return pl.pallas_call(
        kernel,
        out_shape=shapes if single else list(shapes),
        in_specs=[VMEM] * count,
        out_specs=VMEM if single else [VMEM] * len(shapes),
        scratch_shapes=list(scratch),
        compiler_params=pltpu.CompilerParams(vmem_limit_bytes=32 << 20),
    )


def arr(*shape):
    return jax.ShapeDtypeStruct(shape, F32)


def local(right_side, state):
    slabs = lax.axis_size("tm")
    planes = lax.axis_size("space")
    half = slabs // 2
    across = [(k, (k + 1) % planes) for k in range(1, planes, 2)]
    across += [(b, a) for a, b in across]
    within = [(k, k + 1) for k in range(0, planes, 2)]
    within += [(b, a) for a, b in within]
    onward = [(i, i + 1) for i in range(slabs - 1)]

    edge = arr(2, CT, OV, CX, CY)
    own, outer, inner = call(first_kernel, [arr(4, CT, CZ, CX, CY), edge, edge], 2)(
        right_side, state
    )
    outer = lax.ppermute(outer, "space", across)
    inner = lax.ppermute(inner, "space", within)
    sent = call(later_kernel, arr(3 * CZ + 6, CX, CY), 3)(own, outer, inner)
    prev = lax.ppermute(sent, "tm", onward)
    v2, v3, v4 = call(
        early_kernel,
        [arr(CT - 1, CZ + 4, CX, CY), arr(CT - 2, CZ + 2, CX, CY), arr(CZ, CX, CY)],
        3,
    )(own, outer, inner)
    coef = call(coef_kernel, arr(8, LANES), 1, [pltpu.VMEM((8, CX, CY), F32)])(own)
    other_coef = lax.ppermute(coef, "tm", [(i, i - 1) for i in range(1, slabs, 2)])
    lp, sums = call(
        main_kernel,
        [arr(CT, CZ, CX, CY), arr(planes, 8, LANES)],
        9,
        [
            pltpu.VMEM((CZ + 4, CX, CY), F32),
            pltpu.VMEM((2, CZ + 2, CX, CY), F32),
            pltpu.VMEM((8, CX, CY), F32),
        ],
    )(own, outer, inner, v2, v3, v4, prev, coef, other_coef)
    column = lax.all_to_all(sums, "space", 0, 0)
    window = call(
        window_kernel,
        arr(half, 2, WINDOW, LANES),
        1,
        [pltpu.VMEM((2, WINDOW, LANES), F32)],
    )(column)
    halves = [list(range(half)), list(range(half, slabs))]
    every = lax.all_to_all(window, "tm", 0, 0, axis_index_groups=halves)
    found = pltpu.VMEM((half // 2, WINDOW, LANES), F32)
    last, mine = call(bound_kernel, [arr(5, WINDOW, LANES), arr(WINDOW, LANES)], 1, [found])(every)
    quarter = half // 2
    serve = [(i, i + quarter) for i in range(quarter, half)]
    serve += [(i, i + half + quarter) for i in range(quarter)]
    bound = lax.ppermute(last, "tm", serve)
    shape = arr(CT, CZ, CX, CY)
    result = call(result_kernel, shape, 2)(lp, mine)
    anywhere = pl.BlockSpec(memory_space=pl.ANY)
    return pl.pallas_call(
        second_half_kernel,
        out_shape=shape,
        in_specs=[VMEM, VMEM, VMEM, anywhere],
        out_specs=anywhere,
        scratch_shapes=[
            found,
            pltpu.VMEM((CT, CZ, CX, CY), F32),
            pltpu.SemaphoreType.DMA((2 * CT,)),
        ],
        input_output_aliases={3: 0},
        compiler_params=pltpu.CompilerParams(vmem_limit_bytes=32 << 20),
    )(lp, every, bound, result)


def solution(mesh):
    return jax.shard_map(
        local,
        mesh=mesh,
        in_specs=(P("tm", "space", None, None), P("tm", "space", None, None)),
        out_specs=P("tm", "space", None, None),
        check_vma=False,
    )
```

```python
import jax
import jax.numpy as jnp
from jax import lax
from jax.experimental import pallas as pl
from jax.experimental.pallas import tpu as pltpu
from jax.sharding import PartitionSpec as P

CX = 16
CY = 128
CT = 4
CZ = 8
OV = 2
SWEEPS = 4
CHEB = 8
LANES = 128
NEAR = 4
WINDOW = 16

rate = 8.0
react = 0.5
damp = 0.9
theta = 0.8
delta = 0.6

F32 = jnp.float32
PLANE = (CX, CY)
VMEM = pl.BlockSpec(memory_space=pltpu.VMEM)


def beside(v):
    total = pltpu.roll(v, 1, 0) + pltpu.roll(v, CX - 1, 0)
    return total + (pltpu.roll(v, 1, 1) + pltpu.roll(v, CY - 1, 1))


def swept(v, first, scale, near, before):
    total = beside(v)
    for plane in near:
        if plane is not None:
            total = total + plane
    if before is not None:
        total = total + rate * before
    return (1.0 - damp) * v + first + scale * total


def by_parity(body, first, second):
    odd = at_ref[0] & 1

    @pl.when(odd == 0)
    def _():
        body(first, second)

    @pl.when(odd == 1)
    def _():
        body(second, first)


def by_parity(body, first, second):
    odd = lax.axis_index("space") & 1

    @pl.when(odd == 0)
    def _():
        body(first, second)

    @pl.when(odd == 1)
    def _():
        body(second, first)


def first_kernel(loaded_ref, own_ref, outer_ref, inner_ref):
    def body(low_ref, high_ref):
        for t in range(CT):
            for z in range(CZ):
                rhs, s = loaded_ref[0, t, z], loaded_ref[1, t, z]
                diag = (rate + 6.0 - react) + (3.0 * react) * (s * s)
                scale = damp / diag
                first = scale * rhs
                for which, value in enumerate((scale, first, diag, rhs)):
                    own_ref[which, t, z] = value
                if z < OV:
                    low_ref[0, t, z], low_ref[1, t, z] = scale, first
                if z >= CZ - OV:
                    high_ref[0, t, z - (CZ - OV)] = scale
                    high_ref[1, t, z - (CZ - OV)] = first

    by_parity(body, outer_ref, inner_ref)


def reader(which, own_ref, low_ref, high_ref):
    def read(t, z):
        if z < 0:
            return low_ref[which, t, z + OV]
        if z >= CZ:
            return high_ref[which, t, z - CZ]
        return own_ref[which, t, z]

    return read


def later_kernel(own_ref, outer_ref, inner_ref, out_ref):
    off2 = CZ
    off1 = off2 + CZ + 2
    a, b = CT - 2, CT - 1

    def body(low_ref, high_ref):
        scale = reader(0, own_ref, low_ref, high_ref)
        first = reader(1, own_ref, low_ref, high_ref)
        for z in range(-2, CZ + 2):
            out_ref[off1 + z + 2] = first(b, z)
        for z in range(-1, CZ + 1):
            v = first(b, z)
            near = (first(b, z - 1), first(b, z + 1))
            out_ref[off2 + z + 1] = swept(v, v, scale(b, z), near, first(a, z))
        for z in range(CZ):
            v = first(a, z)
            second = swept(v, v, scale(a, z), (first(a, z - 1), first(a, z + 1)), None)
            near = (out_ref[off2 + z], out_ref[off2 + z + 2])
            out_ref[z] = swept(out_ref[off2 + z + 1], first(b, z), scale(b, z), near, second)

    by_parity(body, outer_ref, inner_ref)


def fold_matrix(rows, columns, fine_first):
    i = lax.broadcasted_iota(jnp.int32, (rows, columns), 0)
    k = lax.broadcasted_iota(jnp.int32, (rows, columns), 1)
    fine, lane = (i, k) if fine_first else (k, i)
    return jnp.where(lax.shift_right_logical(fine, 2) == (lane & (CY // 4 - 1)), 1.0, 0.0)


def x_mask():
    x = lax.broadcasted_iota(jnp.int32, PLANE, 0)
    lane = lax.broadcasted_iota(jnp.int32, PLANE, 1)
    return jnp.where(lax.shift_right_logical(x, 2) == lax.shift_right_logical(lane, 5), 1.0, 0.0)


def early_kernel(own_ref, outer_ref, inner_ref, v2_ref, v3_ref, v4_ref):
    def body(low_ref, high_ref):
        scale = reader(0, own_ref, low_ref, high_ref)
        first = reader(1, own_ref, low_ref, high_ref)
        for t in range(1, CT):
            for z in range(-2, CZ + 2):
                v = first(t, z)
                near = [first(t, q) for q in (z - 1, z + 1) if -2 <= q < CZ + 2]
                v2_ref[t - 1, z + 2] = swept(v, v, scale(t, z), near, first(t - 1, z))
        for t in range(2, CT):
            for z in range(-1, CZ + 1):
                near = (v2_ref[t - 1, z + 1], v2_ref[t - 1, z + 3])
                v3_ref[t - 2, z + 1] = swept(
                    v2_ref[t - 1, z + 2], first(t, z), scale(t, z), near, v2_ref[t - 2, z + 2]
                )
        t = CT - 1
        for z in range(CZ):
            near = (v3_ref[t - 2, z], v3_ref[t - 2, z + 2])
            v4_ref[z] = swept(
                v3_ref[t - 2, z + 1], first(t, z), scale(t, z), near, v3_ref[t - 3, z + 1]
            )

    by_parity(body, outer_ref, inner_ref)


def fold(planes):
    folded = jnp.dot(
        planes.reshape(-1, CY),
        fold_matrix(CY, LANES, True),
        precision=lax.Precision.HIGHEST,
        preferred_element_type=F32,
    )
    return jnp.sum(folded.reshape(-1, CX, LANES) * x_mask()[None], axis=1)


def coef_kernel(own_ref, out_ref, stack):
    stack[...] = jnp.zeros_like(stack)
    for b in range(2):
        total = None
        for t in range(CT):
            for z in range(4 * b, 4 * b + 4):
                diag = own_ref[2, t, z]
                total = diag if total is None else total + diag
        stack[4 + b] = (total - 4 * CT * (rate + 6.0)) * (1.0 / react)
    out_ref[...] = fold(stack[...])


def main_kernel(
    own_ref,
    outer_ref,
    inner_ref,
    v2_ref,
    v3_ref,
    v4_ref,
    prev_ref,
    coef_ref,
    other_coef_ref,
    lp_ref,
    sums_ref,
    v2,
    v3,
    stack,
):
    off2 = CZ
    off1 = off2 + CZ + 2

    def body(low_ref, high_ref):
        scale = reader(0, own_ref, low_ref, high_ref)
        own = reader(1, own_ref, low_ref, high_ref)

        def second(t, z):
            if t < 0:
                return prev_ref[off2 + z + 1]
            return v2[z + 2] if t == 0 else v2_ref[t - 1, z + 2]

        def third(t, z):
            if t < 0:
                return prev_ref[z]
            return v3[t, z + 1] if t < 2 else v3_ref[t - 2, z + 1]

        for z in range(-2, CZ + 2):
            v = own(0, z)
            near = [own(0, q) for q in (z - 1, z + 1) if -2 <= q < CZ + 2]
            v2[z + 2] = swept(v, v, scale(0, z), near, prev_ref[off1 + z + 2])
        for t in range(2):
            for z in range(-1, CZ + 1):
                near = (second(t, z - 1), second(t, z + 1))
                v3[t, z + 1] = swept(second(t, z), own(t, z), scale(t, z), near, second(t - 1, z))
        for t in range(CT - 1):
            for z in range(CZ):
                near = (third(t, z - 1), third(t, z + 1))
                lp_ref[t, z] = swept(third(t, z), own(t, z), scale(t, z), near, third(t - 1, z))

    by_parity(body, outer_ref, inner_ref)
    for z in range(CZ):
        lp_ref[CT - 1, z] = v4_ref[z]

    rest = []
    planes = []
    for z in range(CZ):
        part = None
        for t in range(CT):
            term = own_ref[3, t, z] - own_ref[2, t, z] * lp_ref[t, z]
            part = term if part is None else part + term
        early = lp_ref[0, z]
        for t in range(1, CT - 1):
            early = early + lp_ref[t, z]
        rest.append(part + rate * early)
        planes.append(early + lp_ref[CT - 1, z])
    odd = (lax.axis_index("tm") & 1) == 1
    for b in range(2):
        z = 4 * b
        total = planes[z] + planes[z + 1] + planes[z + 2] + planes[z + 3]
        inner = planes[z] + planes[z + 3] + 2.0 * (planes[z + 1] + planes[z + 2])
        inner = inner + (planes[4] if b == 0 else planes[3])
        value = rest[z] + rest[z + 1] + rest[z + 2] + rest[z + 3]
        value = value + beside(total) + inner
        last = lp_ref[CT - 1, z] + lp_ref[CT - 1, z + 1]
        last = rate * (last + (lp_ref[CT - 1, z + 2] + lp_ref[CT - 1, z + 3]))
        stack[b] = jnp.where(odd, value, value + last)
        stack[4 + b] = jnp.where(odd, last, 0.0)
    stack[2] = planes[0]
    stack[3] = planes[CZ - 1]
    stack[6] = jnp.zeros(PLANE, F32)
    stack[7] = jnp.zeros(PLANE, F32)
    coef = coef_ref[...] + other_coef_ref[...]
    sums = fold(stack[...]) + jnp.where(odd, 0.0, coef)
    sums_ref[...] = jnp.broadcast_to(sums[None], sums_ref.shape)


def window_kernel(all_ref, out_ref, rows):
    plane = lax.axis_index("space")
    count = all_ref.shape[0]
    parts = [all_ref[lax.rem(plane + (count - NEAR + k), count)] for k in range(2 * NEAR + 1)]
    for k, part in enumerate(parts):
        low, high = part[0:1], part[1:2]
        if k > 0:
            low = low + parts[k - 1][3:4]
        if k < 2 * NEAR:
            high = high + parts[k + 1][2:3]
        if k > 0:
            rows[0, 2 * k - 1 : 2 * k] = low
            rows[1, 2 * k - 1 : 2 * k] = part[4:5]
        if k < 2 * NEAR:
            rows[0, 2 * k : 2 * k + 1] = high
            rows[1, 2 * k : 2 * k + 1] = part[5:6]
    value = rows[...]
    for k in range(out_ref.shape[0]):
        out_ref[k] = value


def coarse_steps(all_ref, bound_ref):
    shape = (WINDOW, LANES)
    lane = lax.broadcasted_iota(jnp.int32, shape, 1) & (CY // 4 - 1)
    row = lax.broadcasted_iota(jnp.int32, shape, 0)
    width = CY // 4
    is_first, is_last = lane == 0, lane == width - 1
    bottom, top = row == 0, row == WINDOW - 1

    def around(f):
        total = pltpu.roll(f, width, 1) + pltpu.roll(f, LANES - width, 1)
        after = jnp.where(is_last, pltpu.roll(f, width - 1, 1), pltpu.roll(f, LANES - 1, 1))
        before = jnp.where(is_first, pltpu.roll(f, LANES - width + 1, 1), pltpu.roll(f, 1, 1))
        below = jnp.where(bottom, 0.0, pltpu.roll(f, 1, 0))
        above = jnp.where(top, 0.0, pltpu.roll(f, WINDOW - 1, 0))
        return total + (after + before) + (below + above)

    slots = all_ref.shape[0] // 2
    inverse = []
    resid = []
    for k in range(slots):
        rhs = all_ref[2 * k, 0] + all_ref[2 * k + 1, 0]
        if k > 0:
            rhs = rhs + all_ref[2 * k - 1, 1]
        elif bound_ref is not None:
            rhs = rhs + bound_ref[4]
        coef = all_ref[2 * k, 1]
        inv = 1.0 / (1.375 + (react / 512.0) * coef)
        inverse.append(inv)
        resid.append((rhs * (1.0 / 512.0)) * inv)
    step = [r * (1.0 / theta) for r in resid]
    sol = list(step)
    rho = delta / theta
    last = []
    for m in range(1, CHEB):
        nxt = 1.0 / (2.0 * theta / delta - rho)
        last.append(step[-1])
        flows = []
        for k in range(slots):
            flow = around(step[k]) * (1.0 / 16.0)
            if k > 0:
                flow = flow + step[k - 1]
            elif bound_ref is not None:
                flow = flow + (bound_ref[m - 1] if m <= 4 else swapped(bound_ref[7 - m]))
            flows.append(flow)
        for k in range(slots):
            resid[k] = resid[k] - step[k] + flows[k] * inverse[k]
            step[k] = (nxt * rho) * step[k] + (2.0 * nxt / delta) * resid[k]
            sol[k] = sol[k] + step[k]
        rho = nxt
    return sol, last


def swapped(v):
    return jnp.concatenate([v[WINDOW // 2 :], v[: WINDOW // 2]], axis=0)


def bound_kernel(all_ref, out_ref, mine_ref, found):
    @pl.when(lax.axis_index("tm") < all_ref.shape[0])
    def _():
        sol, last = coarse_steps(all_ref, None)
        row = lax.broadcasted_iota(jnp.int32, (WINDOW, LANES), 0)
        for m in range(3):
            used = (row > m) & (row < WINDOW - 1 - m)
            out_ref[m] = jnp.where(used, last[m], swapped(last[6 - m]))
        out_ref[3] = last[3]
        out_ref[4] = all_ref[all_ref.shape[0] - 1, 1]
        mine_ref[...] = own_slot(sol, found)


def own_slot(sol, found):
    for k, value in enumerate(sol):
        found[k] = value
    return found[lax.rem(lax.axis_index("tm"), 2 * len(sol)) // 2]


def spread(window):
    mask = x_mask()
    mine = 2 * NEAR - 1
    both = [window[mine + b : mine + b + 1] * mask for b in range(2)]
    fine = jnp.dot(
        jnp.concatenate(both, axis=0),
        fold_matrix(LANES, CY, False),
        precision=lax.Precision.HIGHEST,
        preferred_element_type=F32,
    )
    return [fine[b * CX : (b + 1) * CX] for b in range(2)]


def result_kernel(lp_ref, mine_ref, out_ref):
    for b, value in enumerate(spread(mine_ref[...])):
        for t in range(CT):
            for z in range(4 * b, 4 * b + 4):
                out_ref[t, z] = lp_ref[t, z] + value


def second_half_kernel(lp_ref, all_ref, bound_ref, _, out_ref, found, result, sems):
    @pl.when(lax.axis_index("tm") >= all_ref.shape[0])
    def _():
        sol, _ = coarse_steps(all_ref, bound_ref)
        values = spread(own_slot(sol, found))
        copies = []
        for t in range(CT):
            for b, value in enumerate(values):
                for z in range(4 * b, 4 * b + 4):
                    result[t, z] = lp_ref[t, z] + value
                part = pl.ds(4 * b, 4)
                copy = pltpu.make_async_copy(
                    result.at[t, part], out_ref.at[t, part], sems.at[2 * t + b]
                )
                copy.start()
                copies.append(copy)
        for copy in copies:
            copy.wait()


def call(kernel, shapes, count, scratch=()):
    single = not isinstance(shapes, (list, tuple))
    return pl.pallas_call(
        kernel,
        out_shape=shapes if single else list(shapes),
        in_specs=[VMEM] * count,
        out_specs=VMEM if single else [VMEM] * len(shapes),
        scratch_shapes=list(scratch),
        compiler_params=pltpu.CompilerParams(vmem_limit_bytes=32 << 20),
    )


def arr(*shape):
    return jax.ShapeDtypeStruct(shape, F32)


def local(right_side, state):
    slabs = lax.axis_size("tm")
    planes = lax.axis_size("space")
    half = slabs // 2
    across = [(k, (k + 1) % planes) for k in range(1, planes, 2)]
    across += [(b, a) for a, b in across]
    within = [(k, k + 1) for k in range(0, planes, 2)]
    within += [(b, a) for a, b in within]
    onward = [(i, i + 1) for i in range(slabs - 1)]

    edge = arr(2, CT, OV, CX, CY)
    own, outer, inner = call(first_kernel, [arr(4, CT, CZ, CX, CY), edge, edge], 1)(
        jnp.stack([right_side, state])
    )
    outer = lax.ppermute(outer, "space", across)
    inner = lax.ppermute(inner, "space", within)
    sent = call(later_kernel, arr(3 * CZ + 6, CX, CY), 3)(own, outer, inner)
    prev = lax.ppermute(sent, "tm", onward)
    v2, v3, v4 = call(
        early_kernel,
        [arr(CT - 1, CZ + 4, CX, CY), arr(CT - 2, CZ + 2, CX, CY), arr(CZ, CX, CY)],
        3,
    )(own, outer, inner)
    coef = call(coef_kernel, arr(8, LANES), 1, [pltpu.VMEM((8, CX, CY), F32)])(own)
    other_coef = lax.ppermute(coef, "tm", [(i, i - 1) for i in range(1, slabs, 2)])
    lp, sums = call(
        main_kernel,
        [arr(CT, CZ, CX, CY), arr(planes, 8, LANES)],
        9,
        [
            pltpu.VMEM((CZ + 4, CX, CY), F32),
            pltpu.VMEM((2, CZ + 2, CX, CY), F32),
            pltpu.VMEM((8, CX, CY), F32),
        ],
    )(own, outer, inner, v2, v3, v4, prev, coef, other_coef)
    column = lax.all_to_all(sums, "space", 0, 0)
    window = call(
        window_kernel,
        arr(half, 2, WINDOW, LANES),
        1,
        [pltpu.VMEM((2, WINDOW, LANES), F32)],
    )(column)
    halves = [list(range(half)), list(range(half, slabs))]
    every = lax.all_to_all(window, "tm", 0, 0, axis_index_groups=halves)
    found = pltpu.VMEM((half // 2, WINDOW, LANES), F32)
    last, mine = call(bound_kernel, [arr(5, WINDOW, LANES), arr(WINDOW, LANES)], 1, [found])(every)
    quarter = half // 2
    serve = [(i, i + quarter) for i in range(quarter, half)] + [(0, slabs - 1), (1, slabs - 2)]
    serve += [(i, half + quarter + i - 2) for i in range(2, quarter)]
    bound = lax.ppermute(last, "tm", serve)
    shape = arr(CT, CZ, CX, CY)
    result = call(result_kernel, shape, 2)(lp, mine)
    anywhere = pl.BlockSpec(memory_space=pl.ANY)
    return pl.pallas_call(
        second_half_kernel,
        out_shape=shape,
        in_specs=[VMEM, VMEM, VMEM, anywhere],
        out_specs=anywhere,
        scratch_shapes=[
            found,
            pltpu.VMEM((CT, CZ, CX, CY), F32),
            pltpu.SemaphoreType.DMA((2 * CT,)),
        ],
        input_output_aliases={3: 0},
        compiler_params=pltpu.CompilerParams(vmem_limit_bytes=32 << 20),
    )(lp, every, bound, result)


def solution(mesh):
    return jax.shard_map(
        local,
        mesh=mesh,
        in_specs=(P("tm", "space", None, None), P("tm", "space", None, None)),
        out_specs=P("tm", "space", None, None),
        check_vma=False,
    )
```

```python
import jax
import jax.numpy as jnp
from jax import lax
from jax.experimental import pallas as pl
from jax.experimental.pallas import tpu as pltpu
from jax.sharding import PartitionSpec as P

CX = 16
CY = 128
CT = 4
CZ = 8
OV = 2
SWEEPS = 4
CHEB = 8
LANES = 128
NEAR = 4
WINDOW = 16

rate = 8.0
react = 0.5
damp = 0.9
theta = 0.8
delta = 0.6

F32 = jnp.float32
PLANE = (CX, CY)
VMEM = pl.BlockSpec(memory_space=pltpu.VMEM)


def beside(v):
    total = pltpu.roll(v, 1, 0) + pltpu.roll(v, CX - 1, 0)
    return total + (pltpu.roll(v, 1, 1) + pltpu.roll(v, CY - 1, 1))


def swept(v, first, scale, near, before):
    total = beside(v)
    for plane in near:
        if plane is not None:
            total = total + plane
    if before is not None:
        total = total + rate * before
    return (1.0 - damp) * v + first + scale * total


def by_parity(body, first, second):
    odd = at_ref[0] & 1

    @pl.when(odd == 0)
    def _():
        body(first, second)

    @pl.when(odd == 1)
    def _():
        body(second, first)


def by_parity(body, first, second):
    odd = lax.axis_index("space") & 1

    @pl.when(odd == 0)
    def _():
        body(first, second)

    @pl.when(odd == 1)
    def _():
        body(second, first)


def first_kernel(loaded_ref, own_ref, outer_ref, inner_ref):
    def body(low_ref, high_ref):
        for t in range(CT):
            for z in range(CZ):
                rhs, s = loaded_ref[0, t, z], loaded_ref[1, t, z]
                diag = (rate + 6.0 - react) + (3.0 * react) * (s * s)
                scale = damp / diag
                first = scale * rhs
                for which, value in enumerate((scale, first, diag, rhs)):
                    own_ref[which, t, z] = value
                if z < OV:
                    low_ref[0, t, z], low_ref[1, t, z] = scale, first
                if z >= CZ - OV:
                    high_ref[0, t, z - (CZ - OV)] = scale
                    high_ref[1, t, z - (CZ - OV)] = first

    by_parity(body, outer_ref, inner_ref)


def reader(which, own_ref, low_ref, high_ref):
    def read(t, z):
        if z < 0:
            return low_ref[which, t, z + OV]
        if z >= CZ:
            return high_ref[which, t, z - CZ]
        return own_ref[which, t, z]

    return read


def later_kernel(own_ref, outer_ref, inner_ref, out_ref):
    off2 = CZ
    off1 = off2 + CZ + 2
    a, b = CT - 2, CT - 1

    def body(low_ref, high_ref):
        scale = reader(0, own_ref, low_ref, high_ref)
        first = reader(1, own_ref, low_ref, high_ref)
        for z in range(-2, CZ + 2):
            out_ref[off1 + z + 2] = first(b, z)
        for z in range(-1, CZ + 1):
            v = first(b, z)
            near = (first(b, z - 1), first(b, z + 1))
            out_ref[off2 + z + 1] = swept(v, v, scale(b, z), near, first(a, z))
        for z in range(CZ):
            v = first(a, z)
            second = swept(v, v, scale(a, z), (first(a, z - 1), first(a, z + 1)), None)
            near = (out_ref[off2 + z], out_ref[off2 + z + 2])
            out_ref[z] = swept(out_ref[off2 + z + 1], first(b, z), scale(b, z), near, second)

    by_parity(body, outer_ref, inner_ref)


def fold_matrix(rows, columns, fine_first):
    i = lax.broadcasted_iota(jnp.int32, (rows, columns), 0)
    k = lax.broadcasted_iota(jnp.int32, (rows, columns), 1)
    fine, lane = (i, k) if fine_first else (k, i)
    return jnp.where(lax.shift_right_logical(fine, 2) == (lane & (CY // 4 - 1)), 1.0, 0.0)


def x_mask():
    x = lax.broadcasted_iota(jnp.int32, PLANE, 0)
    lane = lax.broadcasted_iota(jnp.int32, PLANE, 1)
    return jnp.where(lax.shift_right_logical(x, 2) == lax.shift_right_logical(lane, 5), 1.0, 0.0)


def early_kernel(own_ref, outer_ref, inner_ref, v2_ref, v3_ref, v4_ref, rest_ref):
    def body(low_ref, high_ref):
        scale = reader(0, own_ref, low_ref, high_ref)
        first = reader(1, own_ref, low_ref, high_ref)
        for t in range(CT):
            for z in range(-2, CZ + 2):
                v = first(t, z)
                near = [first(t, q) for q in (z - 1, z + 1) if -2 <= q < CZ + 2]
                before = first(t - 1, z) if t > 0 else None
                v2_ref[t, z + 2] = swept(v, v, scale(t, z), near, before)
        for t in range(1, CT):
            for z in range(-1, CZ + 1):
                near = (v2_ref[t, z + 1], v2_ref[t, z + 3])
                before = v2_ref[t - 1, z + 2] if t > 1 else None
                v3_ref[t - 1, z + 1] = swept(
                    v2_ref[t, z + 2], first(t, z), scale(t, z), near, before
                )
        for t in range(2, CT):
            for z in range(CZ):
                near = (v3_ref[t - 1, z], v3_ref[t - 1, z + 2])
                before = v3_ref[t - 2, z + 1] if t > 2 else None
                v4_ref[t - 2, z] = swept(
                    v3_ref[t - 1, z + 1], first(t, z), scale(t, z), near, before
                )

    by_parity(body, outer_ref, inner_ref)
    for z in range(CZ):
        rest = own_ref[3, 0, z] - own_ref[2, CT - 1, z] * v4_ref[1, z]
        for t in range(1, CT):
            rest = rest + own_ref[3, t, z]
        rest_ref[z] = rest


def exact_dot(x, ones):
    parts = []
    for _ in range(3):
        part = x.astype(jnp.bfloat16)
        parts.append(part)
        x = x - part.astype(F32)
    ones = ones.astype(jnp.bfloat16)
    high, mid, low = (jnp.dot(part, ones, preferred_element_type=F32) for part in parts)
    return high + (mid + low)


def fold(planes):
    folded = exact_dot(planes.reshape(-1, CY), fold_matrix(CY, LANES, True))
    return jnp.sum(folded.reshape(-1, CX, LANES) * x_mask()[None], axis=1)


def coef_kernel(own_ref, out_ref, stack):
    stack[...] = jnp.zeros_like(stack)
    for b in range(2):
        total = None
        for t in range(CT):
            for z in range(4 * b, 4 * b + 4):
                diag = own_ref[2, t, z]
                total = diag if total is None else total + diag
        stack[4 + b] = (total - 4 * CT * (rate + 6.0)) * (1.0 / react)
    out_ref[...] = fold(stack[...])


def main_kernel(
    own_ref,
    outer_ref,
    inner_ref,
    v2_ref,
    v3_ref,
    v4_ref,
    rest_ref,
    prev_ref,
    coef_ref,
    other_coef_ref,
    lp_ref,
    sums_ref,
    v2,
    v3,
    stack,
):
    off2 = CZ
    off1 = off2 + CZ + 2

    def body(low_ref, high_ref):
        scale = reader(0, own_ref, low_ref, high_ref)
        own = reader(1, own_ref, low_ref, high_ref)
        for z in range(-2, CZ + 2):
            v2[z + 2] = v2_ref[0, z + 2] + rate * scale(0, z) * prev_ref[off1 + z + 2]
        for z in range(-1, CZ + 1):
            near = (v2[z + 1], v2[z + 3])
            before = prev_ref[off2 + z + 1]
            v3[0, z + 1] = swept(v2[z + 2], own(0, z), scale(0, z), near, before)
            v3[1, z + 1] = v3_ref[0, z + 1] + rate * scale(1, z) * v2[z + 2]

    by_parity(body, outer_ref, inner_ref)

    rest = []
    planes = []
    for z in range(CZ):
        part = rest_ref[z]
        early = None
        for t in range(CT - 1):
            scale = own_ref[0, t, z]
            if t < 2:
                before = prev_ref[z] if t == 0 else v3[0, z + 1]
                near = (v3[t, z], v3[t, z + 2])
                value = swept(v3[t, z + 1], own_ref[1, t, z], scale, near, before)
            else:
                value = v4_ref[0, z] + rate * scale * v3[1, z + 1]
            lp_ref[t, z] = value
            part = part - own_ref[2, t, z] * value
            early = value if early is None else early + value
        value = v4_ref[1, z]
        lp_ref[CT - 1, z] = value
        rest.append(part + rate * early)
        planes.append(early + value)
    odd = (lax.axis_index("tm") & 1) == 1
    for b in range(2):
        z = 4 * b
        total = planes[z] + planes[z + 1] + planes[z + 2] + planes[z + 3]
        inner = planes[z] + planes[z + 3] + 2.0 * (planes[z + 1] + planes[z + 2])
        inner = inner + (planes[4] if b == 0 else planes[3])
        value = rest[z] + rest[z + 1] + rest[z + 2] + rest[z + 3]
        value = value + beside(total) + inner
        last = v4_ref[1, z] + v4_ref[1, z + 1]
        last = rate * (last + (v4_ref[1, z + 2] + v4_ref[1, z + 3]))
        stack[b] = jnp.where(odd, value, value + last)
        stack[4 + b] = jnp.where(odd, last, 0.0)
    stack[2] = planes[0]
    stack[3] = planes[CZ - 1]
    coef = coef_ref[...] + other_coef_ref[...]
    none = jnp.zeros((2, LANES), F32)
    sums = jnp.concatenate([fold(stack[...]), none], axis=0) + jnp.where(odd, 0.0, coef)
    sums_ref[...] = jnp.broadcast_to(sums[None], sums_ref.shape)


def window_kernel(all_ref, out_ref, rows):
    plane = lax.axis_index("space")
    count = all_ref.shape[0]
    parts = [all_ref[lax.rem(plane + (count - NEAR + k), count)] for k in range(2 * NEAR + 1)]
    for k, part in enumerate(parts):
        low, high = part[0:1], part[1:2]
        if k > 0:
            low = low + parts[k - 1][3:4]
        if k < 2 * NEAR:
            high = high + parts[k + 1][2:3]
        if k > 0:
            rows[0, 2 * k - 1 : 2 * k] = low
            rows[1, 2 * k - 1 : 2 * k] = part[4:5]
        if k < 2 * NEAR:
            rows[0, 2 * k : 2 * k + 1] = high
            rows[1, 2 * k : 2 * k + 1] = part[5:6]
    value = rows[...]
    for k in range(out_ref.shape[0]):
        out_ref[k] = value


def coarse_steps(all_ref, bound_ref):
    shape = (WINDOW, LANES)
    lane = lax.broadcasted_iota(jnp.int32, shape, 1) & (CY // 4 - 1)
    row = lax.broadcasted_iota(jnp.int32, shape, 0)
    width = CY // 4
    is_first, is_last = lane == 0, lane == width - 1
    bottom, top = row == 0, row == WINDOW - 1

    def around(f):
        total = pltpu.roll(f, width, 1) + pltpu.roll(f, LANES - width, 1)
        after = jnp.where(is_last, pltpu.roll(f, width - 1, 1), pltpu.roll(f, LANES - 1, 1))
        before = jnp.where(is_first, pltpu.roll(f, LANES - width + 1, 1), pltpu.roll(f, 1, 1))
        below = jnp.where(bottom, 0.0, pltpu.roll(f, 1, 0))
        above = jnp.where(top, 0.0, pltpu.roll(f, WINDOW - 1, 0))
        return total + (after + before) + (below + above)

    slots = all_ref.shape[0] // 2
    inverse = []
    resid = []
    for k in range(slots):
        rhs = all_ref[2 * k, 0] + all_ref[2 * k + 1, 0]
        if k > 0:
            rhs = rhs + all_ref[2 * k - 1, 1]
        elif bound_ref is not None:
            rhs = rhs + handed(bound_ref, 4)
        coef = all_ref[2 * k, 1]
        inv = 1.0 / (1.375 + (react / 512.0) * coef)
        inverse.append(inv)
        resid.append((rhs * (1.0 / 512.0)) * inv)
    step = [r * (1.0 / theta) for r in resid]
    sol = list(step)
    rho = delta / theta
    last = []
    for m in range(1, CHEB):
        nxt = 1.0 / (2.0 * theta / delta - rho)
        last.append(step[-1])
        flows = []
        for k in range(slots):
            flow = around(step[k]) * (1.0 / 16.0)
            if k > 0:
                flow = flow + step[k - 1]
            elif bound_ref is not None:
                flow = flow + handed(bound_ref, m - 1 if m <= 4 else m)
            flows.append(flow)
        for k in range(slots):
            resid[k] = resid[k] - step[k] + flows[k] * inverse[k]
            step[k] = (nxt * rho) * step[k] + (2.0 * nxt / delta) * resid[k]
            sol[k] = sol[k] + step[k]
        rho = nxt
    return sol, last


def swapped(v):
    return jnp.concatenate([v[WINDOW // 2 :], v[: WINDOW // 2]], axis=0)


def handed(bound_ref, k):
    if k == 3:
        none = jnp.zeros((WINDOW // 4, LANES), F32)
        return jnp.concatenate([none, bound_ref[6], none], axis=0)
    at = (0, 2, 4, None, 7, 4, 2, 0)[k]
    both = (bound_ref[at], bound_ref[at + 1])
    return jnp.concatenate(both if k <= 4 else both[::-1], axis=0)


def bound_kernel(all_ref, out_ref, mine_ref, found):
    @pl.when(lax.axis_index("tm") < all_ref.shape[0])
    def _():
        sol, last = coarse_steps(all_ref, None)
        row = lax.broadcasted_iota(jnp.int32, (WINDOW, LANES), 0)
        for m in range(3):
            used = (row > m) & (row < WINDOW - 1 - m)
            block = jnp.where(used, last[m], swapped(last[6 - m]))
            out_ref[2 * m], out_ref[2 * m + 1] = block[: WINDOW // 2], block[WINDOW // 2 :]
        out_ref[6] = last[3][WINDOW // 4 : 3 * WINDOW // 4]
        for h in range(2):
            half = pl.ds(h * WINDOW // 2, WINDOW // 2)
            out_ref[7 + h] = all_ref[all_ref.shape[0] - 1, 1, half]
        mine_ref[...] = own_slot(sol, found)


def own_slot(sol, found):
    for k, value in enumerate(sol):
        found[k] = value
    return found[lax.rem(lax.axis_index("tm"), 2 * len(sol)) // 2]


def spread(window):
    mask = x_mask()
    mine = 2 * NEAR - 1
    both = [window[mine + b : mine + b + 1] * mask for b in range(2)]
    fine = exact_dot(jnp.concatenate(both, axis=0), fold_matrix(LANES, CY, False))
    return [fine[b * CX : (b + 1) * CX] for b in range(2)]


def result_kernel(lp_ref, mine_ref, out_ref):
    for b, value in enumerate(spread(mine_ref[...])):
        for t in range(CT):
            for z in range(4 * b, 4 * b + 4):
                out_ref[t, z] = lp_ref[t, z] + value


def second_half_kernel(lp_ref, all_ref, bound_ref, _, out_ref, found, result, sems):
    @pl.when(lax.axis_index("tm") >= all_ref.shape[0])
    def _():
        sol, _ = coarse_steps(all_ref, bound_ref)
        values = spread(own_slot(sol, found))
        copies = []
        for t in range(CT):
            for b, value in enumerate(values):
                for z in range(4 * b, 4 * b + 4):
                    result[t, z] = lp_ref[t, z] + value
                part = pl.ds(4 * b, 4)
                copy = pltpu.make_async_copy(
                    result.at[t, part], out_ref.at[t, part], sems.at[2 * t + b]
                )
                copy.start()
                copies.append(copy)
        for copy in copies:
            copy.wait()


def call(kernel, shapes, count, scratch=()):
    single = not isinstance(shapes, (list, tuple))
    return pl.pallas_call(
        kernel,
        out_shape=shapes if single else list(shapes),
        in_specs=[VMEM] * count,
        out_specs=VMEM if single else [VMEM] * len(shapes),
        scratch_shapes=list(scratch),
        compiler_params=pltpu.CompilerParams(vmem_limit_bytes=32 << 20),
    )


def arr(*shape):
    return jax.ShapeDtypeStruct(shape, F32)


def local(right_side, state):
    slabs = lax.axis_size("tm")
    planes = lax.axis_size("space")
    half = slabs // 2
    across = [(k, (k + 1) % planes) for k in range(1, planes, 2)]
    across += [(b, a) for a, b in across]
    within = [(k, k + 1) for k in range(0, planes, 2)]
    within += [(b, a) for a, b in within]
    onward = [(i, i + 1) for i in range(slabs - 1)]

    edge = arr(2, CT, OV, CX, CY)
    own, outer, inner = call(first_kernel, [arr(4, CT, CZ, CX, CY), edge, edge], 1)(
        jnp.stack([right_side, state])
    )
    outer = lax.ppermute(outer, "space", across)
    inner = lax.ppermute(inner, "space", within)
    sent = call(later_kernel, arr(3 * CZ + 6, CX, CY), 3)(own, outer, inner)
    prev = lax.ppermute(sent, "tm", onward)
    v2, v3, v4, rest = call(
        early_kernel,
        [
            arr(CT, CZ + 4, CX, CY),
            arr(CT - 1, CZ + 2, CX, CY),
            arr(CT - 2, CZ, CX, CY),
            arr(CZ, CX, CY),
        ],
        3,
    )(own, outer, inner)
    coef = call(coef_kernel, arr(8, LANES), 1, [pltpu.VMEM((8, CX, CY), F32)])(own)
    other_coef = lax.ppermute(coef, "tm", [(i, i - 1) for i in range(1, slabs, 2)])
    lp, sums = call(
        main_kernel,
        [arr(CT, CZ, CX, CY), arr(planes, 8, LANES)],
        10,
        [
            pltpu.VMEM((CZ + 4, CX, CY), F32),
            pltpu.VMEM((2, CZ + 2, CX, CY), F32),
            pltpu.VMEM((6, CX, CY), F32),
        ],
    )(own, outer, inner, v2, v3, v4, rest, prev, coef, other_coef)
    column = lax.all_to_all(sums, "space", 0, 0)
    window = call(
        window_kernel,
        arr(half, 2, WINDOW, LANES),
        1,
        [pltpu.VMEM((2, WINDOW, LANES), F32)],
    )(column)
    halves = [list(range(half)), list(range(half, slabs))]
    every = lax.all_to_all(window, "tm", 0, 0, axis_index_groups=halves)
    found = pltpu.VMEM((half // 2, WINDOW, LANES), F32)
    last, mine = call(bound_kernel, [arr(9, WINDOW // 2, LANES), arr(WINDOW, LANES)], 1, [found])(every)
    quarter = half // 2
    order = (0, 2, 1, 3, 5, 6, 4, 7) if half == 8 else tuple(range(half))
    serve = [((quarter + k) % half, half + order[k]) for k in range(half)]
    bound = lax.ppermute(last, "tm", serve)
    shape = arr(CT, CZ, CX, CY)
    result = call(result_kernel, shape, 2)(lp, mine)
    anywhere = pl.BlockSpec(memory_space=pl.ANY)
    return pl.pallas_call(
        second_half_kernel,
        out_shape=shape,
        in_specs=[VMEM, VMEM, VMEM, anywhere],
        out_specs=anywhere,
        scratch_shapes=[
            found,
            pltpu.VMEM((CT, CZ, CX, CY), F32),
            pltpu.SemaphoreType.DMA((2 * CT,)),
        ],
        input_output_aliases={3: 0},
        compiler_params=pltpu.CompilerParams(vmem_limit_bytes=32 << 20),
    )(lp, every, bound, result)


def solution(mesh):
    return jax.shard_map(
        local,
        mesh=mesh,
        in_specs=(P("tm", "space", None, None), P("tm", "space", None, None)),
        out_specs=P("tm", "space", None, None),
        check_vma=False,
    )
```

```python
import jax
import jax.numpy as jnp
from jax import lax
from jax.experimental import pallas as pl
from jax.experimental.pallas import tpu as pltpu
from jax.sharding import PartitionSpec as P

CX = 16
CY = 128
CT = 4
CZ = 8
OV = 2
SWEEPS = 4
CHEB = 8
LANES = 128
NEAR = 4
WINDOW = 16
TURN = 20
EARLY = (7, 6, 5, 4, 3, 2, 1, 0)
LATE = (3, 0, 1, 2, 4, 5, 6, 7)

rate = 8.0
react = 0.5
damp = 0.9
theta = 0.8
delta = 0.6

F32 = jnp.float32
PLANE = (CX, CY)
VMEM = pl.BlockSpec(memory_space=pltpu.VMEM)


def beside(v):
    total = pltpu.roll(v, 1, 0) + pltpu.roll(v, CX - 1, 0)
    return total + (pltpu.roll(v, 1, 1) + pltpu.roll(v, CY - 1, 1))


def swept(v, first, scale, near, before):
    total = beside(v)
    for plane in near:
        if plane is not None:
            total = total + plane
    if before is not None:
        total = total + rate * before
    return (1.0 - damp) * v + first + scale * total


def by_parity(body, first, second):
    odd = at_ref[0] & 1

    @pl.when(odd == 0)
    def _():
        body(first, second)

    @pl.when(odd == 1)
    def _():
        body(second, first)


def by_parity(body, first, second):
    odd = lax.axis_index("space") & 1

    @pl.when(odd == 0)
    def _():
        body(first, second)

    @pl.when(odd == 1)
    def _():
        body(second, first)


def first_kernel(loaded_ref, own_ref, outer_ref, inner_ref):
    def body(low_ref, high_ref):
        for t in range(CT):
            for z in range(CZ):
                rhs, s = loaded_ref[0, t, z], loaded_ref[1, t, z]
                diag = (rate + 6.0 - react) + (3.0 * react) * (s * s)
                scale = damp / diag
                first = scale * rhs
                for which, value in enumerate((scale, first, diag, rhs)):
                    own_ref[which, t, z] = value
                if z < OV:
                    low_ref[0, t, z], low_ref[1, t, z] = scale, first
                if z >= CZ - OV:
                    high_ref[0, t, z - (CZ - OV)] = scale
                    high_ref[1, t, z - (CZ - OV)] = first

    by_parity(body, outer_ref, inner_ref)


def reader(which, own_ref, low_ref, high_ref):
    def read(t, z):
        if z < 0:
            return low_ref[which, t, z + OV]
        if z >= CZ:
            return high_ref[which, t, z - CZ]
        return own_ref[which, t, z]

    return read


def later_kernel(own_ref, outer_ref, inner_ref, out_ref):
    off2 = CZ
    off1 = off2 + CZ + 2
    a, b = CT - 2, CT - 1

    def body(low_ref, high_ref):
        scale = reader(0, own_ref, low_ref, high_ref)
        first = reader(1, own_ref, low_ref, high_ref)
        for z in range(-2, CZ + 2):
            out_ref[off1 + z + 2] = first(b, z)
        for z in range(-1, CZ + 1):
            v = first(b, z)
            near = (first(b, z - 1), first(b, z + 1))
            out_ref[off2 + z + 1] = swept(v, v, scale(b, z), near, first(a, z))
        for z in range(CZ):
            v = first(a, z)
            second = swept(v, v, scale(a, z), (first(a, z - 1), first(a, z + 1)), None)
            near = (out_ref[off2 + z], out_ref[off2 + z + 2])
            out_ref[z] = swept(out_ref[off2 + z + 1], first(b, z), scale(b, z), near, second)

    by_parity(body, outer_ref, inner_ref)


def fold_matrix(rows, columns, fine_first):
    i = lax.broadcasted_iota(jnp.int32, (rows, columns), 0)
    k = lax.broadcasted_iota(jnp.int32, (rows, columns), 1)
    fine, lane = (i, k) if fine_first else (k, i)
    return jnp.where(lax.shift_right_logical(fine, 2) == (lane & (CY // 4 - 1)), 1.0, 0.0)


def x_mask():
    x = lax.broadcasted_iota(jnp.int32, PLANE, 0)
    lane = lax.broadcasted_iota(jnp.int32, PLANE, 1)
    return jnp.where(lax.shift_right_logical(x, 2) == lax.shift_right_logical(lane, 5), 1.0, 0.0)


def early_kernel(own_ref, outer_ref, inner_ref, v2_ref, v3_ref, v4_ref, rest_ref):
    def body(low_ref, high_ref):
        scale = reader(0, own_ref, low_ref, high_ref)
        first = reader(1, own_ref, low_ref, high_ref)
        for t in range(CT):
            for z in range(-2, CZ + 2):
                v = first(t, z)
                near = [first(t, q) for q in (z - 1, z + 1) if -2 <= q < CZ + 2]
                before = first(t - 1, z) if t > 0 else None
                v2_ref[t, z + 2] = swept(v, v, scale(t, z), near, before)
        for t in range(1, CT):
            for z in range(-1, CZ + 1):
                near = (v2_ref[t, z + 1], v2_ref[t, z + 3])
                before = v2_ref[t - 1, z + 2] if t > 1 else None
                v3_ref[t - 1, z + 1] = swept(
                    v2_ref[t, z + 2], first(t, z), scale(t, z), near, before
                )
        for t in range(2, CT):
            for z in range(CZ):
                near = (v3_ref[t - 1, z], v3_ref[t - 1, z + 2])
                before = v3_ref[t - 2, z + 1] if t > 2 else None
                v4_ref[t - 2, z] = swept(
                    v3_ref[t - 1, z + 1], first(t, z), scale(t, z), near, before
                )

    by_parity(body, outer_ref, inner_ref)
    for z in range(CZ):
        rest = own_ref[3, 0, z] - own_ref[2, CT - 1, z] * v4_ref[1, z]
        for t in range(1, CT):
            rest = rest + own_ref[3, t, z]
        rest_ref[z] = rest


def exact_dot(x, ones):
    parts = []
    for _ in range(3):
        part = x.astype(jnp.bfloat16)
        parts.append(part)
        x = x - part.astype(F32)
    ones = ones.astype(jnp.bfloat16)
    high, mid, low = (jnp.dot(part, ones, preferred_element_type=F32) for part in parts)
    return high + (mid + low)


def fold(planes):
    folded = exact_dot(planes.reshape(-1, CY), fold_matrix(CY, LANES, True))
    return jnp.sum(folded.reshape(-1, CX, LANES) * x_mask()[None], axis=1)


def coef_kernel(own_ref, out_ref, stack):
    stack[...] = jnp.zeros_like(stack)
    for b in range(2):
        total = None
        for t in range(CT):
            for z in range(4 * b, 4 * b + 4):
                diag = own_ref[2, t, z]
                total = diag if total is None else total + diag
        stack[4 + b] = (total - 4 * CT * (rate + 6.0)) * (1.0 / react)
    out_ref[...] = fold(stack[...])


def main_kernel(
    own_ref,
    outer_ref,
    inner_ref,
    v2_ref,
    v3_ref,
    v4_ref,
    rest_ref,
    prev_ref,
    coef_ref,
    other_coef_ref,
    lp_ref,
    sums_ref,
    v2,
    v3,
    stack,
):
    off2 = CZ
    off1 = off2 + CZ + 2

    def body(low_ref, high_ref):
        scale = reader(0, own_ref, low_ref, high_ref)
        own = reader(1, own_ref, low_ref, high_ref)
        for z in range(-2, CZ + 2):
            v2[z + 2] = v2_ref[0, z + 2] + rate * scale(0, z) * prev_ref[off1 + z + 2]
        for z in range(-1, CZ + 1):
            near = (v2[z + 1], v2[z + 3])
            before = prev_ref[off2 + z + 1]
            v3[0, z + 1] = swept(v2[z + 2], own(0, z), scale(0, z), near, before)
            v3[1, z + 1] = v3_ref[0, z + 1] + rate * scale(1, z) * v2[z + 2]

    by_parity(body, outer_ref, inner_ref)

    rest = []
    planes = []
    for z in range(CZ):
        part = rest_ref[z]
        early = None
        for t in range(CT - 1):
            scale = own_ref[0, t, z]
            if t < 2:
                before = prev_ref[z] if t == 0 else v3[0, z + 1]
                near = (v3[t, z], v3[t, z + 2])
                value = swept(v3[t, z + 1], own_ref[1, t, z], scale, near, before)
            else:
                value = v4_ref[0, z] + rate * scale * v3[1, z + 1]
            lp_ref[t, z] = value
            part = part - own_ref[2, t, z] * value
            early = value if early is None else early + value
        value = v4_ref[1, z]
        lp_ref[CT - 1, z] = value
        rest.append(part + rate * early)
        planes.append(early + value)
    odd = (lax.axis_index("tm") & 1) == 1
    for b in range(2):
        z = 4 * b
        total = planes[z] + planes[z + 1] + planes[z + 2] + planes[z + 3]
        inner = planes[z] + planes[z + 3] + 2.0 * (planes[z + 1] + planes[z + 2])
        inner = inner + (planes[4] if b == 0 else planes[3])
        value = rest[z] + rest[z + 1] + rest[z + 2] + rest[z + 3]
        value = value + beside(total) + inner
        last = v4_ref[1, z] + v4_ref[1, z + 1]
        last = rate * (last + (v4_ref[1, z + 2] + v4_ref[1, z + 3]))
        stack[b] = jnp.where(odd, value, value + last)
        stack[4 + b] = jnp.where(odd, last, 0.0)
    stack[2] = planes[0]
    stack[3] = planes[CZ - 1]
    coef = coef_ref[...] + other_coef_ref[...]
    none = jnp.zeros((2, LANES), F32)
    sums = jnp.concatenate([fold(stack[...]), none], axis=0) + jnp.where(odd, 0.0, coef)
    sums_ref[...] = jnp.broadcast_to(sums[None], sums_ref.shape)


def window_kernel(all_ref, out_ref, rows):
    plane = lax.axis_index("space")
    count = all_ref.shape[0]
    parts = [all_ref[lax.rem(plane + (2 * count - TURN - NEAR + k), count)] for k in range(2 * NEAR + 1)]
    for k, part in enumerate(parts):
        low, high = part[0:1], part[1:2]
        if k > 0:
            low = low + parts[k - 1][3:4]
        if k < 2 * NEAR:
            high = high + parts[k + 1][2:3]
        if k > 0:
            rows[0, 2 * k - 1 : 2 * k] = low
            rows[1, 2 * k - 1 : 2 * k] = part[4:5]
        if k < 2 * NEAR:
            rows[0, 2 * k : 2 * k + 1] = high
            rows[1, 2 * k : 2 * k + 1] = part[5:6]
    value = rows[...]
    for k in range(out_ref.shape[0]):
        out_ref[k] = value


def coarse_steps(all_ref, bound_ref):
    lane = lax.broadcasted_iota(jnp.int32, (WINDOW, LANES), 1) & (CY // 4 - 1)
    width = CY // 4
    is_first, is_last = lane == 0, lane == width - 1

    def around(f):
        total = pltpu.roll(f, width, 1) + pltpu.roll(f, LANES - width, 1)
        after = jnp.where(is_last, pltpu.roll(f, width - 1, 1), pltpu.roll(f, LANES - 1, 1))
        before = jnp.where(is_first, pltpu.roll(f, LANES - width + 1, 1), pltpu.roll(f, 1, 1))
        return (total + (pltpu.roll(f, 1, 0) + pltpu.roll(f, WINDOW - 1, 0))) + (after + before)

    slots = all_ref.shape[0] // 2
    order = EARLY if bound_ref is None else LATE

    def slab(k, which):
        return all_ref[order.index(k), which]

    inverse = []
    resid = []
    for k in range(slots):
        rhs = slab(2 * k, 0) + slab(2 * k + 1, 0)
        if k > 0:
            rhs = rhs + slab(2 * k - 1, 1)
        elif bound_ref is not None:
            rhs = rhs + handed(bound_ref, 4)
        coef = slab(2 * k, 1)
        inv = 1.0 / (1.375 + (react / 512.0) * coef)
        inverse.append(inv)
        resid.append((rhs * (1.0 / 512.0)) * inv)
    step = [r * (1.0 / theta) for r in resid]
    sol = list(step)
    rho = delta / theta
    last = []
    beside = [i * (1.0 / 16.0) for i in inverse]
    for m in range(1, CHEB):
        nxt = 1.0 / (2.0 * theta / delta - rho)
        last.append(step[-1])
        known = []
        for k in range(slots):
            value = resid[k] - step[k]
            if k > 0:
                value = value + step[k - 1] * inverse[k]
            elif bound_ref is not None:
                value = value + handed(bound_ref, m - 1 if m <= 4 else m) * inverse[k]
            known.append(value)
        for k in range(slots):
            resid[k] = known[k] + around(step[k]) * beside[k]
        for k in range(slots):
            step[k] = (nxt * rho) * step[k] + (2.0 * nxt / delta) * resid[k]
            sol[k] = sol[k] + step[k]
        rho = nxt
    return sol, last


def swapped(v):
    return jnp.concatenate([v[WINDOW // 2 :], v[: WINDOW // 2]], axis=0)


def handed(bound_ref, k):
    if k == 3:
        none = jnp.zeros((WINDOW // 4, LANES), F32)
        return jnp.concatenate([none, bound_ref[6], none], axis=0)
    at = (0, 2, 4, None, 7, 4, 2, 0)[k]
    both = (bound_ref[at], bound_ref[at + 1])
    return jnp.concatenate(both if k <= 4 else both[::-1], axis=0)


def bound_kernel(all_ref, out_ref, mine_ref, found):
    @pl.when(lax.axis_index("tm") < all_ref.shape[0])
    def _():
        sol, last = coarse_steps(all_ref, None)
        row = lax.broadcasted_iota(jnp.int32, (WINDOW, LANES), 0)
        for m in range(3):
            used = (row > m) & (row < WINDOW - 1 - m)
            block = jnp.where(used, last[m], swapped(last[6 - m]))
            out_ref[2 * m], out_ref[2 * m + 1] = block[: WINDOW // 2], block[WINDOW // 2 :]
        out_ref[6] = last[3][WINDOW // 4 : 3 * WINDOW // 4]
        for h in range(2):
            half = pl.ds(h * WINDOW // 2, WINDOW // 2)
            out_ref[7 + h] = all_ref[EARLY.index(all_ref.shape[0] - 1), 1, half]
        mine_ref[...] = own_slot(sol, found)


def own_slot(sol, found):
    for k, value in enumerate(sol):
        found[k] = value
    return found[lax.rem(lax.axis_index("tm"), 2 * len(sol)) // 2]


def spread(window):
    mask = x_mask()
    mine = 2 * NEAR - 1
    both = [window[mine + b : mine + b + 1] * mask for b in range(2)]
    fine = exact_dot(jnp.concatenate(both, axis=0), fold_matrix(LANES, CY, False))
    return [fine[b * CX : (b + 1) * CX] for b in range(2)]


def result_kernel(lp_ref, mine_ref, out_ref):
    for b, value in enumerate(spread(mine_ref[...])):
        for t in range(CT):
            for z in range(4 * b, 4 * b + 4):
                out_ref[t, z] = lp_ref[t, z] + value


def second_half_kernel(lp_ref, all_ref, bound_ref, _, out_ref, found, result, sems):
    @pl.when(lax.axis_index("tm") >= all_ref.shape[0])
    def _():
        sol, _ = coarse_steps(all_ref, bound_ref)
        values = spread(own_slot(sol, found))
        copies = []
        for t in range(CT):
            for b, value in enumerate(values):
                for z in range(4 * b, 4 * b + 4):
                    result[t, z] = lp_ref[t, z] + value
                part = pl.ds(4 * b, 4)
                copy = pltpu.make_async_copy(
                    result.at[t, part], out_ref.at[t, part], sems.at[2 * t + b]
                )
                copy.start()
                copies.append(copy)
        for copy in copies:
            copy.wait()


def call(kernel, shapes, count, scratch=()):
    single = not isinstance(shapes, (list, tuple))
    return pl.pallas_call(
        kernel,
        out_shape=shapes if single else list(shapes),
        in_specs=[VMEM] * count,
        out_specs=VMEM if single else [VMEM] * len(shapes),
        scratch_shapes=list(scratch),
        compiler_params=pltpu.CompilerParams(vmem_limit_bytes=32 << 20),
    )


def arr(*shape):
    return jax.ShapeDtypeStruct(shape, F32)


def local(right_side, state):
    slabs = lax.axis_size("tm")
    planes = lax.axis_size("space")
    half = slabs // 2
    across = [(k, (k + 1) % planes) for k in range(1, planes, 2)]
    across += [(b, a) for a, b in across]
    within = [(k, k + 1) for k in range(0, planes, 2)]
    within += [(b, a) for a, b in within]
    onward = [(i, i + 1) for i in range(slabs - 1)]

    edge = arr(2, CT, OV, CX, CY)
    own, outer, inner = call(first_kernel, [arr(4, CT, CZ, CX, CY), edge, edge], 1)(
        jnp.stack([right_side, state])
    )
    outer = lax.ppermute(outer, "space", across)
    inner = lax.ppermute(inner, "space", within)
    sent = call(later_kernel, arr(3 * CZ + 6, CX, CY), 3)(own, outer, inner)
    prev = lax.ppermute(sent, "tm", onward)
    v2, v3, v4, rest = call(
        early_kernel,
        [
            arr(CT, CZ + 4, CX, CY),
            arr(CT - 1, CZ + 2, CX, CY),
            arr(CT - 2, CZ, CX, CY),
            arr(CZ, CX, CY),
        ],
        3,
    )(own, outer, inner)
    coef = call(coef_kernel, arr(8, LANES), 1, [pltpu.VMEM((8, CX, CY), F32)])(own)
    other_coef = lax.ppermute(coef, "tm", [(i, i - 1) for i in range(1, slabs, 2)])
    lp, sums = call(
        main_kernel,
        [arr(CT, CZ, CX, CY), arr(planes, 8, LANES)],
        10,
        [
            pltpu.VMEM((CZ + 4, CX, CY), F32),
            pltpu.VMEM((2, CZ + 2, CX, CY), F32),
            pltpu.VMEM((6, CX, CY), F32),
        ],
    )(own, outer, inner, v2, v3, v4, rest, prev, coef, other_coef)
    column = lax.all_to_all(
        sums, "space", 0, 0, axis_index_groups=[[(p + TURN) % planes for p in range(planes)]]
    )
    window = call(
        window_kernel,
        arr(half, 2, WINDOW, LANES),
        1,
        [pltpu.VMEM((2, WINDOW, LANES), F32)],
    )(column)
    halves = [list(EARLY), [half + k for k in LATE]]
    every = lax.all_to_all(window, "tm", 0, 0, axis_index_groups=halves)
    found = pltpu.VMEM((half // 2, WINDOW, LANES), F32)
    last, mine = call(bound_kernel, [arr(9, WINDOW // 2, LANES), arr(WINDOW, LANES)], 1, [found])(every)
    quarter = half // 2
    order = (0, 2, 1, 3, 5, 6, 4, 7) if half == 8 else tuple(range(half))
    serve = [((quarter + k) % half, half + order[k]) for k in range(half)]
    bound = lax.ppermute(last, "tm", serve)
    shape = arr(CT, CZ, CX, CY)
    result = call(result_kernel, shape, 2)(lp, mine)
    anywhere = pl.BlockSpec(memory_space=pl.ANY)
    return pl.pallas_call(
        second_half_kernel,
        out_shape=shape,
        in_specs=[VMEM, VMEM, VMEM, anywhere],
        out_specs=anywhere,
        scratch_shapes=[
            found,
            pltpu.VMEM((CT, CZ, CX, CY), F32),
            pltpu.SemaphoreType.DMA((2 * CT,)),
        ],
        input_output_aliases={3: 0},
        compiler_params=pltpu.CompilerParams(vmem_limit_bytes=32 << 20),
    )(lp, every, bound, result)


def solution(mesh):
    return jax.shard_map(
        local,
        mesh=mesh,
        in_specs=(P("tm", "space", None, None), P("tm", "space", None, None)),
        out_specs=P("tm", "space", None, None),
        check_vma=False,
    )
```

```python
import jax
import jax.numpy as jnp
from jax import lax
from jax.experimental import pallas as pl
from jax.experimental.pallas import tpu as pltpu
from jax.sharding import PartitionSpec as P

CX = 16
CY = 128
CT = 4
CZ = 8
OV = 2
SWEEPS = 4
CHEB = 8
LANES = 128
NEAR = 4
WINDOW = 16
TURN = 20
EARLY = (5, 0, 1, 2, 3, 4, 6, 7)
LATE = (3, 7, 6, 5, 4, 2, 1, 0)

rate = 8.0
react = 0.5
damp = 0.9
theta = 0.8
delta = 0.6

F32 = jnp.float32
PLANE = (CX, CY)
VMEM = pl.BlockSpec(memory_space=pltpu.VMEM)


def beside(v):
    total = pltpu.roll(v, 1, 0) + pltpu.roll(v, CX - 1, 0)
    return total + (pltpu.roll(v, 1, 1) + pltpu.roll(v, CY - 1, 1))


def swept(v, first, scale, near, before):
    total = beside(v)
    for plane in near:
        if plane is not None:
            total = total + plane
    if before is not None:
        total = total + rate * before
    return (1.0 - damp) * v + first + scale * total


def by_parity(body, first, second):
    odd = at_ref[0] & 1

    @pl.when(odd == 0)
    def _():
        body(first, second)

    @pl.when(odd == 1)
    def _():
        body(second, first)


def by_parity(body, first, second):
    odd = lax.axis_index("space") & 1

    @pl.when(odd == 0)
    def _():
        body(first, second)

    @pl.when(odd == 1)
    def _():
        body(second, first)


def first_kernel(loaded_ref, own_ref, outer_ref, inner_ref):
    def body(low_ref, high_ref):
        for t in range(CT):
            for z in range(CZ):
                rhs, s = loaded_ref[0, t, z], loaded_ref[1, t, z]
                diag = (rate + 6.0 - react) + (3.0 * react) * (s * s)
                scale = damp / diag
                first = scale * rhs
                for which, value in enumerate((scale, first, diag, rhs)):
                    own_ref[which, t, z] = value
                if z < OV:
                    low_ref[0, t, z], low_ref[1, t, z] = scale, first
                if z >= CZ - OV:
                    high_ref[0, t, z - (CZ - OV)] = scale
                    high_ref[1, t, z - (CZ - OV)] = first

    by_parity(body, outer_ref, inner_ref)


def reader(which, own_ref, low_ref, high_ref):
    def read(t, z):
        if z < 0:
            return low_ref[which, t, z + OV]
        if z >= CZ:
            return high_ref[which, t, z - CZ]
        return own_ref[which, t, z]

    return read


def inner_kernel(own_ref, out_ref):
    a, b = CT - 2, CT - 1

    def scale(t, z):
        return own_ref[0, t, z]

    def first(t, z):
        return own_ref[1, t, z]

    for z in range(CZ):
        out_ref[z] = first(b, z)
    for z in range(1, CZ - 1):
        v = first(b, z)
        near = (first(b, z - 1), first(b, z + 1))
        out_ref[CZ + z - 1] = swept(v, v, scale(b, z), near, first(a, z))
    for z in range(2, CZ - 2):
        v = first(a, z)
        second = swept(v, v, scale(a, z), (first(a, z - 1), first(a, z + 1)), None)
        near = (out_ref[CZ + z - 2], out_ref[CZ + z])
        out_ref[2 * CZ + z - 4] = swept(
            out_ref[CZ + z - 1], first(b, z), scale(b, z), near, second
        )


FIRST_ENDS = (-2, -1, CZ, CZ + 1)
SECOND_ENDS = (-1, 0, CZ - 1, CZ)
THIRD_ENDS = (0, 1, CZ - 2, CZ - 1)


def earlier_step(inside_ref, ends_ref):
    def first(z):
        return ends_ref[FIRST_ENDS.index(z)] if z in FIRST_ENDS else inside_ref[z]

    def second(z):
        if z in SECOND_ENDS:
            return ends_ref[4 + SECOND_ENDS.index(z)]
        return inside_ref[CZ + z - 1]

    def third(z):
        if z in THIRD_ENDS:
            return ends_ref[8 + THIRD_ENDS.index(z)]
        return inside_ref[2 * CZ + z - 4]

    return first, second, third


def later_kernel(own_ref, outer_ref, inner_ref, inside_ref, out_ref):
    a, b = CT - 2, CT - 1

    def body(low_ref, high_ref):
        scale = reader(0, own_ref, low_ref, high_ref)
        first = reader(1, own_ref, low_ref, high_ref)
        _, second, _ = earlier_step(inside_ref, out_ref)
        for k, z in enumerate(FIRST_ENDS):
            out_ref[k] = first(b, z)
        for k, z in enumerate(SECOND_ENDS):
            v = first(b, z)
            near = (first(b, z - 1), first(b, z + 1))
            out_ref[4 + k] = swept(v, v, scale(b, z), near, first(a, z))
        for k, z in enumerate(THIRD_ENDS):
            v = first(a, z)
            before = swept(v, v, scale(a, z), (first(a, z - 1), first(a, z + 1)), None)
            near = (second(z - 1), second(z + 1))
            out_ref[8 + k] = swept(second(z), first(b, z), scale(b, z), near, before)

    by_parity(body, outer_ref, inner_ref)


def fold_matrix(rows, columns, fine_first):
    i = lax.broadcasted_iota(jnp.int32, (rows, columns), 0)
    k = lax.broadcasted_iota(jnp.int32, (rows, columns), 1)
    fine, lane = (i, k) if fine_first else (k, i)
    return jnp.where(lax.shift_right_logical(fine, 2) == (lane & (CY // 4 - 1)), 1.0, 0.0)


def x_mask():
    x = lax.broadcasted_iota(jnp.int32, PLANE, 0)
    lane = lax.broadcasted_iota(jnp.int32, PLANE, 1)
    return jnp.where(lax.shift_right_logical(x, 2) == lax.shift_right_logical(lane, 5), 1.0, 0.0)


def early_kernel(own_ref, outer_ref, inner_ref, v2_ref, v3_ref, v4_ref, rest_ref):
    def body(low_ref, high_ref):
        scale = reader(0, own_ref, low_ref, high_ref)
        first = reader(1, own_ref, low_ref, high_ref)
        for t in range(CT):
            for z in range(-2, CZ + 2):
                v = first(t, z)
                near = [first(t, q) for q in (z - 1, z + 1) if -2 <= q < CZ + 2]
                before = first(t - 1, z) if t > 0 else None
                v2_ref[t, z + 2] = swept(v, v, scale(t, z), near, before)
        for t in range(1, CT):
            for z in range(-1, CZ + 1):
                near = (v2_ref[t, z + 1], v2_ref[t, z + 3])
                before = v2_ref[t - 1, z + 2] if t > 1 else None
                v3_ref[t - 1, z + 1] = swept(
                    v2_ref[t, z + 2], first(t, z), scale(t, z), near, before
                )
        for t in range(2, CT):
            for z in range(CZ):
                near = (v3_ref[t - 1, z], v3_ref[t - 1, z + 2])
                before = v3_ref[t - 2, z + 1] if t > 2 else None
                v4_ref[t - 2, z] = swept(
                    v3_ref[t - 1, z + 1], first(t, z), scale(t, z), near, before
                )

    by_parity(body, outer_ref, inner_ref)
    for z in range(CZ):
        rest = own_ref[3, 0, z] - own_ref[2, CT - 1, z] * v4_ref[1, z]
        for t in range(1, CT):
            rest = rest + own_ref[3, t, z]
        rest_ref[z] = rest


def exact_dot(x, ones):
    parts = []
    for _ in range(3):
        part = x.astype(jnp.bfloat16)
        parts.append(part)
        x = x - part.astype(F32)
    ones = ones.astype(jnp.bfloat16)
    high, mid, low = (jnp.dot(part, ones, preferred_element_type=F32) for part in parts)
    return high + (mid + low)


def fold(planes):
    folded = exact_dot(planes.reshape(-1, CY), fold_matrix(CY, LANES, True))
    return jnp.sum(folded.reshape(-1, CX, LANES) * x_mask()[None], axis=1)


def coef_kernel(own_ref, out_ref, stack):
    stack[...] = jnp.zeros_like(stack)
    for b in range(2):
        total = None
        for t in range(CT):
            for z in range(4 * b, 4 * b + 4):
                diag = own_ref[2, t, z]
                total = diag if total is None else total + diag
        stack[4 + b] = (total - 4 * CT * (rate + 6.0)) * (1.0 / react)
    out_ref[...] = fold(stack[...])


def main_kernel(
    own_ref,
    outer_ref,
    inner_ref,
    v2_ref,
    v3_ref,
    v4_ref,
    rest_ref,
    inside_ref,
    ends_ref,
    coef_ref,
    other_coef_ref,
    lp_ref,
    sums_ref,
    v2,
    v3,
    stack,
):
    first_before, second_before, third_before = earlier_step(inside_ref, ends_ref)

    def body(low_ref, high_ref):
        scale = reader(0, own_ref, low_ref, high_ref)
        own = reader(1, own_ref, low_ref, high_ref)
        for z in range(-2, CZ + 2):
            v2[z + 2] = v2_ref[0, z + 2] + rate * scale(0, z) * first_before(z)
        for z in range(-1, CZ + 1):
            near = (v2[z + 1], v2[z + 3])
            before = second_before(z)
            v3[0, z + 1] = swept(v2[z + 2], own(0, z), scale(0, z), near, before)
            v3[1, z + 1] = v3_ref[0, z + 1] + rate * scale(1, z) * v2[z + 2]

    by_parity(body, outer_ref, inner_ref)

    rest = []
    planes = []
    for z in range(CZ):
        part = rest_ref[z]
        early = None
        for t in range(CT - 1):
            scale = own_ref[0, t, z]
            if t < 2:
                before = third_before(z) if t == 0 else v3[0, z + 1]
                near = (v3[t, z], v3[t, z + 2])
                value = swept(v3[t, z + 1], own_ref[1, t, z], scale, near, before)
            else:
                value = v4_ref[0, z] + rate * scale * v3[1, z + 1]
            lp_ref[t, z] = value
            part = part - own_ref[2, t, z] * value
            early = value if early is None else early + value
        value = v4_ref[1, z]
        lp_ref[CT - 1, z] = value
        rest.append(part + rate * early)
        planes.append(early + value)
    odd = (lax.axis_index("tm") & 1) == 1
    for b in range(2):
        z = 4 * b
        total = planes[z] + planes[z + 1] + planes[z + 2] + planes[z + 3]
        inner = planes[z] + planes[z + 3] + 2.0 * (planes[z + 1] + planes[z + 2])
        inner = inner + (planes[4] if b == 0 else planes[3])
        value = rest[z] + rest[z + 1] + rest[z + 2] + rest[z + 3]
        value = value + beside(total) + inner
        last = v4_ref[1, z] + v4_ref[1, z + 1]
        last = rate * (last + (v4_ref[1, z + 2] + v4_ref[1, z + 3]))
        stack[b] = jnp.where(odd, value, value + last)
        stack[4 + b] = jnp.where(odd, last, 0.0)
    stack[2] = planes[0]
    stack[3] = planes[CZ - 1]
    coef = coef_ref[...] + other_coef_ref[...]
    none = jnp.zeros((2, LANES), F32)
    sums = jnp.concatenate([fold(stack[...]), none], axis=0) + jnp.where(odd, 0.0, coef)
    sums_ref[...] = jnp.broadcast_to(sums[None], sums_ref.shape)


def window_kernel(all_ref, out_ref, rows):
    plane = lax.axis_index("space")
    count = all_ref.shape[0]
    parts = [all_ref[lax.rem(plane + (2 * count - TURN - NEAR + k), count)] for k in range(2 * NEAR + 1)]
    for k, part in enumerate(parts):
        low, high = part[0:1], part[1:2]
        if k > 0:
            low = low + parts[k - 1][3:4]
        if k < 2 * NEAR:
            high = high + parts[k + 1][2:3]
        if k > 0:
            rows[0, 2 * k - 1 : 2 * k] = low
            rows[1, 2 * k - 1 : 2 * k] = part[4:5]
        if k < 2 * NEAR:
            rows[0, 2 * k : 2 * k + 1] = high
            rows[1, 2 * k : 2 * k + 1] = part[5:6]
    value = rows[...]
    for k in range(out_ref.shape[0]):
        out_ref[k] = value


def coarse_steps(all_ref, bound_ref):
    lane = lax.broadcasted_iota(jnp.int32, (WINDOW, LANES), 1) & (CY // 4 - 1)
    width = CY // 4
    is_first, is_last = lane == 0, lane == width - 1

    def around(f):
        total = pltpu.roll(f, width, 1) + pltpu.roll(f, LANES - width, 1)
        after = jnp.where(is_last, pltpu.roll(f, width - 1, 1), pltpu.roll(f, LANES - 1, 1))
        before = jnp.where(is_first, pltpu.roll(f, LANES - width + 1, 1), pltpu.roll(f, 1, 1))
        return (total + (pltpu.roll(f, 1, 0) + pltpu.roll(f, WINDOW - 1, 0))) + (after + before)

    slots = all_ref.shape[0] // 2
    order = EARLY if bound_ref is None else LATE

    def slab(k, which):
        return all_ref[order.index(k), which]

    inverse = []
    resid = []
    for k in range(slots):
        rhs = slab(2 * k, 0) + slab(2 * k + 1, 0)
        if k > 0:
            rhs = rhs + slab(2 * k - 1, 1)
        elif bound_ref is not None:
            rhs = rhs + handed(bound_ref, 4)
        coef = slab(2 * k, 1)
        inv = 1.0 / (1.375 + (react / 512.0) * coef)
        inverse.append(inv)
        resid.append((rhs * (1.0 / 512.0)) * inv)
    step = [r * (1.0 / theta) for r in resid]
    sol = list(step)
    rho = delta / theta
    last = []
    beside = [i * (1.0 / 16.0) for i in inverse]
    for m in range(1, CHEB):
        nxt = 1.0 / (2.0 * theta / delta - rho)
        last.append(step[-1])
        known = []
        for k in range(slots):
            value = resid[k] - step[k]
            if k > 0:
                value = value + step[k - 1] * inverse[k]
            elif bound_ref is not None:
                value = value + handed(bound_ref, m - 1 if m <= 4 else m) * inverse[k]
            known.append(value)
        for k in range(slots):
            resid[k] = known[k] + around(step[k]) * beside[k]
        for k in range(slots):
            step[k] = (nxt * rho) * step[k] + (2.0 * nxt / delta) * resid[k]
            sol[k] = sol[k] + step[k]
        rho = nxt
    return sol, last


def swapped(v):
    return jnp.concatenate([v[WINDOW // 2 :], v[: WINDOW // 2]], axis=0)


def handed(bound_ref, k):
    if k == 3:
        none = jnp.zeros((WINDOW // 4, LANES), F32)
        return jnp.concatenate([none, bound_ref[6], none], axis=0)
    at = (0, 2, 4, None, 7, 4, 2, 0)[k]
    both = (bound_ref[at], bound_ref[at + 1])
    return jnp.concatenate(both if k <= 4 else both[::-1], axis=0)


def bound_kernel(all_ref, out_ref, mine_ref, found):
    @pl.when(lax.axis_index("tm") < all_ref.shape[0])
    def _():
        sol, last = coarse_steps(all_ref, None)
        row = lax.broadcasted_iota(jnp.int32, (WINDOW, LANES), 0)
        for m in range(3):
            used = (row > m) & (row < WINDOW - 1 - m)
            block = jnp.where(used, last[m], swapped(last[6 - m]))
            out_ref[2 * m], out_ref[2 * m + 1] = block[: WINDOW // 2], block[WINDOW // 2 :]
        out_ref[6] = last[3][WINDOW // 4 : 3 * WINDOW // 4]
        for h in range(2):
            half = pl.ds(h * WINDOW // 2, WINDOW // 2)
            out_ref[7 + h] = all_ref[EARLY.index(all_ref.shape[0] - 1), 1, half]
        mine_ref[...] = own_slot(sol, found)


def own_slot(sol, found):
    for k, value in enumerate(sol):
        found[k] = value
    return found[lax.rem(lax.axis_index("tm"), 2 * len(sol)) // 2]


def spread(window):
    mask = x_mask()
    mine = 2 * NEAR - 1
    both = [window[mine + b : mine + b + 1] * mask for b in range(2)]
    fine = exact_dot(jnp.concatenate(both, axis=0), fold_matrix(LANES, CY, False))
    return [fine[b * CX : (b + 1) * CX] for b in range(2)]


def result_kernel(lp_ref, mine_ref, out_ref):
    for b, value in enumerate(spread(mine_ref[...])):
        for t in range(CT):
            for z in range(4 * b, 4 * b + 4):
                out_ref[t, z] = lp_ref[t, z] + value


def second_half_kernel(lp_ref, all_ref, bound_ref, _, out_ref, found, result, sems):
    @pl.when(lax.axis_index("tm") >= all_ref.shape[0])
    def _():
        sol, _ = coarse_steps(all_ref, bound_ref)
        values = spread(own_slot(sol, found))
        copies = []
        for t in range(CT):
            for b, value in enumerate(values):
                for z in range(4 * b, 4 * b + 4):
                    result[t, z] = lp_ref[t, z] + value
                part = pl.ds(4 * b, 4)
                copy = pltpu.make_async_copy(
                    result.at[t, part], out_ref.at[t, part], sems.at[2 * t + b]
                )
                copy.start()
                copies.append(copy)
        for copy in copies:
            copy.wait()


def call(kernel, shapes, count, scratch=()):
    single = not isinstance(shapes, (list, tuple))
    return pl.pallas_call(
        kernel,
        out_shape=shapes if single else list(shapes),
        in_specs=[VMEM] * count,
        out_specs=VMEM if single else [VMEM] * len(shapes),
        scratch_shapes=list(scratch),
        compiler_params=pltpu.CompilerParams(vmem_limit_bytes=32 << 20),
    )


def arr(*shape):
    return jax.ShapeDtypeStruct(shape, F32)


def local(right_side, state):
    slabs = lax.axis_size("tm")
    planes = lax.axis_size("space")
    half = slabs // 2
    across = [(k, (k + 1) % planes) for k in range(1, planes, 2)]
    across += [(b, a) for a, b in across]
    within = [(k, k + 1) for k in range(0, planes, 2)]
    within += [(b, a) for a, b in within]
    onward = [(i, i + 1) for i in range(slabs - 1)]

    edge = arr(2, CT, OV, CX, CY)
    own, outer, inner = call(first_kernel, [arr(4, CT, CZ, CX, CY), edge, edge], 1)(
        jnp.stack([right_side, state])
    )
    outer = lax.ppermute(outer, "space", across)
    inner = lax.ppermute(inner, "space", within)
    inside = call(inner_kernel, arr(3 * CZ - 6, CX, CY), 1)(own)
    passed = lax.ppermute(inside, "tm", onward)
    sent = call(later_kernel, arr(12, CX, CY), 4)(own, outer, inner, inside)
    ends = lax.ppermute(sent, "tm", onward)
    v2, v3, v4, rest = call(
        early_kernel,
        [
            arr(CT, CZ + 4, CX, CY),
            arr(CT - 1, CZ + 2, CX, CY),
            arr(CT - 2, CZ, CX, CY),
            arr(CZ, CX, CY),
        ],
        3,
    )(own, outer, inner)
    coef = call(coef_kernel, arr(8, LANES), 1, [pltpu.VMEM((8, CX, CY), F32)])(own)
    other_coef = lax.ppermute(coef, "tm", [(i, i - 1) for i in range(1, slabs, 2)])
    lp, sums = call(
        main_kernel,
        [arr(CT, CZ, CX, CY), arr(planes, 8, LANES)],
        11,
        [
            pltpu.VMEM((CZ + 4, CX, CY), F32),
            pltpu.VMEM((2, CZ + 2, CX, CY), F32),
            pltpu.VMEM((6, CX, CY), F32),
        ],
    )(own, outer, inner, v2, v3, v4, rest, passed, ends, coef, other_coef)
    column = lax.all_to_all(
        sums, "space", 0, 0, axis_index_groups=[[(p + TURN) % planes for p in range(planes)]]
    )
    window = call(
        window_kernel,
        arr(half, 2, WINDOW, LANES),
        1,
        [pltpu.VMEM((2, WINDOW, LANES), F32)],
    )(column)
    halves = [list(EARLY), [half + k for k in LATE]]
    every = lax.all_to_all(window, "tm", 0, 0, axis_index_groups=halves)
    found = pltpu.VMEM((half // 2, WINDOW, LANES), F32)
    last, mine = call(bound_kernel, [arr(9, WINDOW // 2, LANES), arr(WINDOW, LANES)], 1, [found])(every)
    quarter = half // 2
    order = (0, 2, 1, 3, 4, 5, 6, 7) if half == 8 else tuple(range(half))
    serve = [((quarter + k) % half, half + order[k]) for k in range(half)]
    bound = lax.ppermute(last, "tm", serve)
    shape = arr(CT, CZ, CX, CY)
    result = call(result_kernel, shape, 2)(lp, mine)
    anywhere = pl.BlockSpec(memory_space=pl.ANY)
    return pl.pallas_call(
        second_half_kernel,
        out_shape=shape,
        in_specs=[VMEM, VMEM, VMEM, anywhere],
        out_specs=anywhere,
        scratch_shapes=[
            found,
            pltpu.VMEM((CT, CZ, CX, CY), F32),
            pltpu.SemaphoreType.DMA((2 * CT,)),
        ],
        input_output_aliases={3: 0},
        compiler_params=pltpu.CompilerParams(vmem_limit_bytes=32 << 20),
    )(lp, every, bound, result)


def solution(mesh):
    return jax.shard_map(
        local,
        mesh=mesh,
        in_specs=(P("tm", "space", None, None), P("tm", "space", None, None)),
        out_specs=P("tm", "space", None, None),
        check_vma=False,
    )
```

```python
import jax
import jax.numpy as jnp
from jax import lax
from jax.experimental import pallas as pl
from jax.experimental.pallas import tpu as pltpu
from jax.sharding import PartitionSpec as P

CX = 16
CY = 128
CT = 4
CZ = 8
OV = 2
SWEEPS = 4
CHEB = 8
LANES = 128
NEAR = 4
WINDOW = 16
TURN = 4
EARLY = (5, 7, 6, 4, 3, 2, 1, 0)
LATE = (2, 7, 6, 5, 4, 3, 1, 0)

rate = 8.0
react = 0.5
damp = 0.9
theta = 0.8
delta = 0.6

F32 = jnp.float32
PLANE = (CX, CY)
VMEM = pl.BlockSpec(memory_space=pltpu.VMEM)


def beside(v):
    total = pltpu.roll(v, 1, 0) + pltpu.roll(v, CX - 1, 0)
    return total + (pltpu.roll(v, 1, 1) + pltpu.roll(v, CY - 1, 1))


def swept(v, first, scale, near, before):
    total = beside(v)
    for plane in near:
        if plane is not None:
            total = total + plane
    if before is not None:
        total = total + rate * before
    return (1.0 - damp) * v + first + scale * total


def by_parity(body, first, second):
    odd = at_ref[0] & 1

    @pl.when(odd == 0)
    def _():
        body(first, second)

    @pl.when(odd == 1)
    def _():
        body(second, first)


def by_parity(body, first, second):
    odd = lax.axis_index("space") & 1

    @pl.when(odd == 0)
    def _():
        body(first, second)

    @pl.when(odd == 1)
    def _():
        body(second, first)


def first_kernel(loaded_ref, own_ref, outer_ref, inner_ref):
    def body(low_ref, high_ref):
        for t in range(CT):
            for z in range(CZ):
                rhs, s = loaded_ref[0, t, z], loaded_ref[1, t, z]
                diag = (rate + 6.0 - react) + (3.0 * react) * (s * s)
                scale = damp / diag
                first = scale * rhs
                for which, value in enumerate((scale, first, diag, rhs)):
                    own_ref[which, t, z] = value
                if z < OV:
                    low_ref[0, t, z], low_ref[1, t, z] = scale, first
                if z >= CZ - OV:
                    high_ref[0, t, z - (CZ - OV)] = scale
                    high_ref[1, t, z - (CZ - OV)] = first

    by_parity(body, outer_ref, inner_ref)


def reader(which, own_ref, low_ref, high_ref):
    def read(t, z):
        if z < 0:
            return low_ref[which, t, z + OV]
        if z >= CZ:
            return high_ref[which, t, z - CZ]
        return own_ref[which, t, z]

    return read


def inner_kernel(own_ref, out_ref):
    a, b = CT - 2, CT - 1

    def scale(t, z):
        return own_ref[0, t, z]

    def first(t, z):
        return own_ref[1, t, z]

    for z in range(CZ):
        out_ref[z] = first(b, z)
    for z in range(1, CZ - 1):
        v = first(b, z)
        near = (first(b, z - 1), first(b, z + 1))
        out_ref[CZ + z - 1] = swept(v, v, scale(b, z), near, first(a, z))
    for z in range(2, CZ - 2):
        v = first(a, z)
        second = swept(v, v, scale(a, z), (first(a, z - 1), first(a, z + 1)), None)
        near = (out_ref[CZ + z - 2], out_ref[CZ + z])
        out_ref[2 * CZ + z - 4] = swept(
            out_ref[CZ + z - 1], first(b, z), scale(b, z), near, second
        )


FIRST_ENDS = (-2, -1, CZ, CZ + 1)
SECOND_ENDS = (-1, 0, CZ - 1, CZ)
THIRD_ENDS = (0, 1, CZ - 2, CZ - 1)


def earlier_step(inside_ref, ends_ref):
    def first(z):
        return ends_ref[FIRST_ENDS.index(z)] if z in FIRST_ENDS else inside_ref[z]

    def second(z):
        if z in SECOND_ENDS:
            return ends_ref[4 + SECOND_ENDS.index(z)]
        return inside_ref[CZ + z - 1]

    def third(z):
        if z in THIRD_ENDS:
            return ends_ref[8 + THIRD_ENDS.index(z)]
        return inside_ref[2 * CZ + z - 4]

    return first, second, third


def later_kernel(own_ref, outer_ref, inner_ref, inside_ref, out_ref):
    a, b = CT - 2, CT - 1

    def body(low_ref, high_ref):
        scale = reader(0, own_ref, low_ref, high_ref)
        first = reader(1, own_ref, low_ref, high_ref)
        _, second, _ = earlier_step(inside_ref, out_ref)
        for k, z in enumerate(FIRST_ENDS):
            out_ref[k] = first(b, z)
        for k, z in enumerate(SECOND_ENDS):
            v = first(b, z)
            near = (first(b, z - 1), first(b, z + 1))
            out_ref[4 + k] = swept(v, v, scale(b, z), near, first(a, z))
        for k, z in enumerate(THIRD_ENDS):
            v = first(a, z)
            before = swept(v, v, scale(a, z), (first(a, z - 1), first(a, z + 1)), None)
            near = (second(z - 1), second(z + 1))
            out_ref[8 + k] = swept(second(z), first(b, z), scale(b, z), near, before)

    by_parity(body, outer_ref, inner_ref)


def fold_matrix(rows, columns, fine_first):
    i = lax.broadcasted_iota(jnp.int32, (rows, columns), 0)
    k = lax.broadcasted_iota(jnp.int32, (rows, columns), 1)
    fine, lane = (i, k) if fine_first else (k, i)
    return jnp.where(lax.shift_right_logical(fine, 2) == (lane & (CY // 4 - 1)), 1.0, 0.0)


def x_mask():
    x = lax.broadcasted_iota(jnp.int32, PLANE, 0)
    lane = lax.broadcasted_iota(jnp.int32, PLANE, 1)
    return jnp.where(lax.shift_right_logical(x, 2) == lax.shift_right_logical(lane, 5), 1.0, 0.0)


def early_kernel(own_ref, outer_ref, inner_ref, v2_ref, v3_ref, v4_ref, rest_ref):
    def body(low_ref, high_ref):
        scale = reader(0, own_ref, low_ref, high_ref)
        first = reader(1, own_ref, low_ref, high_ref)
        for t in range(CT):
            for z in range(-2, CZ + 2):
                v = first(t, z)
                near = [first(t, q) for q in (z - 1, z + 1) if -2 <= q < CZ + 2]
                before = first(t - 1, z) if t > 0 else None
                v2_ref[t, z + 2] = swept(v, v, scale(t, z), near, before)
        for t in range(1, CT):
            for z in range(-1, CZ + 1):
                near = (v2_ref[t, z + 1], v2_ref[t, z + 3])
                before = v2_ref[t - 1, z + 2] if t > 1 else None
                v3_ref[t - 1, z + 1] = swept(
                    v2_ref[t, z + 2], first(t, z), scale(t, z), near, before
                )
        for t in range(2, CT):
            for z in range(CZ):
                near = (v3_ref[t - 1, z], v3_ref[t - 1, z + 2])
                before = v3_ref[t - 2, z + 1] if t > 2 else None
                v4_ref[t - 2, z] = swept(
                    v3_ref[t - 1, z + 1], first(t, z), scale(t, z), near, before
                )

    by_parity(body, outer_ref, inner_ref)
    for z in range(CZ):
        rest = own_ref[3, 0, z] - own_ref[2, CT - 1, z] * v4_ref[1, z]
        for t in range(1, CT):
            rest = rest + own_ref[3, t, z]
        rest_ref[z] = rest


def exact_dot(x, ones):
    parts = []
    for _ in range(3):
        part = x.astype(jnp.bfloat16)
        parts.append(part)
        x = x - part.astype(F32)
    ones = ones.astype(jnp.bfloat16)
    high, mid, low = (jnp.dot(part, ones, preferred_element_type=F32) for part in parts)
    return high + (mid + low)


def fold(planes):
    folded = exact_dot(planes.reshape(-1, CY), fold_matrix(CY, LANES, True))
    return jnp.sum(folded.reshape(-1, CX, LANES) * x_mask()[None], axis=1)


def coef_kernel(own_ref, out_ref, stack):
    stack[...] = jnp.zeros_like(stack)
    for b in range(2):
        total = None
        for t in range(CT):
            for z in range(4 * b, 4 * b + 4):
                diag = own_ref[2, t, z]
                total = diag if total is None else total + diag
        stack[4 + b] = (total - 4 * CT * (rate + 6.0)) * (1.0 / react)
    out_ref[...] = fold(stack[...])


def main_kernel(
    own_ref,
    outer_ref,
    inner_ref,
    v2_ref,
    v3_ref,
    v4_ref,
    rest_ref,
    inside_ref,
    ends_ref,
    coef_ref,
    other_coef_ref,
    lp_ref,
    sums_ref,
    v2,
    v3,
    stack,
):
    first_before, second_before, third_before = earlier_step(inside_ref, ends_ref)

    def body(low_ref, high_ref):
        scale = reader(0, own_ref, low_ref, high_ref)
        own = reader(1, own_ref, low_ref, high_ref)
        for z in range(-2, CZ + 2):
            v2[z + 2] = v2_ref[0, z + 2] + rate * scale(0, z) * first_before(z)
        for z in range(-1, CZ + 1):
            near = (v2[z + 1], v2[z + 3])
            before = second_before(z)
            v3[0, z + 1] = swept(v2[z + 2], own(0, z), scale(0, z), near, before)
            v3[1, z + 1] = v3_ref[0, z + 1] + rate * scale(1, z) * v2[z + 2]

    by_parity(body, outer_ref, inner_ref)

    rest = []
    planes = []
    for z in range(CZ):
        part = rest_ref[z]
        early = None
        for t in range(CT - 1):
            scale = own_ref[0, t, z]
            if t < 2:
                before = third_before(z) if t == 0 else v3[0, z + 1]
                near = (v3[t, z], v3[t, z + 2])
                value = swept(v3[t, z + 1], own_ref[1, t, z], scale, near, before)
            else:
                value = v4_ref[0, z] + rate * scale * v3[1, z + 1]
            lp_ref[t, z] = value
            part = part - own_ref[2, t, z] * value
            early = value if early is None else early + value
        value = v4_ref[1, z]
        lp_ref[CT - 1, z] = value
        rest.append(part + rate * early)
        planes.append(early + value)
    odd = (lax.axis_index("tm") & 1) == 1
    for b in range(2):
        z = 4 * b
        total = planes[z] + planes[z + 1] + planes[z + 2] + planes[z + 3]
        inner = planes[z] + planes[z + 3] + 2.0 * (planes[z + 1] + planes[z + 2])
        inner = inner + (planes[4] if b == 0 else planes[3])
        value = rest[z] + rest[z + 1] + rest[z + 2] + rest[z + 3]
        value = value + beside(total) + inner
        last = v4_ref[1, z] + v4_ref[1, z + 1]
        last = rate * (last + (v4_ref[1, z + 2] + v4_ref[1, z + 3]))
        stack[b] = jnp.where(odd, value, value + last)
        stack[4 + b] = jnp.where(odd, last, 0.0)
    stack[2] = planes[0]
    stack[3] = planes[CZ - 1]
    coef = coef_ref[...] + other_coef_ref[...]
    none = jnp.zeros((2, LANES), F32)
    sums = jnp.concatenate([fold(stack[...]), none], axis=0) + jnp.where(odd, 0.0, coef)
    sums_ref[...] = jnp.broadcast_to(sums[None], sums_ref.shape)


def window_kernel(all_ref, out_ref, rows):
    plane = lax.axis_index("space")
    count = all_ref.shape[0]
    parts = [all_ref[lax.rem(plane + (2 * count - TURN - NEAR + k), count)] for k in range(2 * NEAR + 1)]
    for k, part in enumerate(parts):
        low, high = part[0:1], part[1:2]
        if k > 0:
            low = low + parts[k - 1][3:4]
        if k < 2 * NEAR:
            high = high + parts[k + 1][2:3]
        if k > 0:
            rows[0, 2 * k - 1 : 2 * k] = low
            rows[1, 2 * k - 1 : 2 * k] = part[4:5]
        if k < 2 * NEAR:
            rows[0, 2 * k : 2 * k + 1] = high
            rows[1, 2 * k : 2 * k + 1] = part[5:6]
    value = rows[...]
    for k in range(out_ref.shape[0]):
        out_ref[k] = value


def coarse_steps(all_ref, bound_ref):
    lane = lax.broadcasted_iota(jnp.int32, (WINDOW, LANES), 1) & (CY // 4 - 1)
    width = CY // 4
    is_first, is_last = lane == 0, lane == width - 1

    def around(f):
        total = pltpu.roll(f, width, 1) + pltpu.roll(f, LANES - width, 1)
        after = jnp.where(is_last, pltpu.roll(f, width - 1, 1), pltpu.roll(f, LANES - 1, 1))
        before = jnp.where(is_first, pltpu.roll(f, LANES - width + 1, 1), pltpu.roll(f, 1, 1))
        return (total + (pltpu.roll(f, 1, 0) + pltpu.roll(f, WINDOW - 1, 0))) + (after + before)

    slots = all_ref.shape[0] // 2
    order = EARLY if bound_ref is None else LATE

    def slab(k, which):
        return all_ref[order.index(k), which]

    inverse = []
    resid = []
    for k in range(slots):
        rhs = slab(2 * k, 0) + slab(2 * k + 1, 0)
        if k > 0:
            rhs = rhs + slab(2 * k - 1, 1)
        elif bound_ref is not None:
            rhs = rhs + handed(bound_ref, 4)
        coef = slab(2 * k, 1)
        inv = 1.0 / (1.375 + (react / 512.0) * coef)
        inverse.append(inv)
        resid.append((rhs * (1.0 / 512.0)) * inv)
    step = [r * (1.0 / theta) for r in resid]
    sol = list(step)
    rho = delta / theta
    last = []
    beside = [i * (1.0 / 16.0) for i in inverse]
    for m in range(1, CHEB):
        nxt = 1.0 / (2.0 * theta / delta - rho)
        last.append(step[-1])
        known = []
        for k in range(slots):
            value = resid[k] - step[k]
            if k > 0:
                value = value + step[k - 1] * inverse[k]
            elif bound_ref is not None:
                value = value + handed(bound_ref, m - 1 if m <= 4 else m) * inverse[k]
            known.append(value)
        for k in range(slots):
            resid[k] = known[k] + around(step[k]) * beside[k]
        for k in range(slots):
            step[k] = (nxt * rho) * step[k] + (2.0 * nxt / delta) * resid[k]
            sol[k] = sol[k] + step[k]
        rho = nxt
    return sol, last


def swapped(v):
    return jnp.concatenate([v[WINDOW // 2 :], v[: WINDOW // 2]], axis=0)


def handed(bound_ref, k):
    if k == 3:
        none = jnp.zeros((WINDOW // 4, LANES), F32)
        return jnp.concatenate([none, bound_ref[6], none], axis=0)
    at = (0, 2, 4, None, 7, 4, 2, 0)[k]
    both = (bound_ref[at], bound_ref[at + 1])
    return jnp.concatenate(both if k <= 4 else both[::-1], axis=0)


def bound_kernel(all_ref, out_ref, mine_ref, found):
    @pl.when(lax.axis_index("tm") < all_ref.shape[0])
    def _():
        sol, last = coarse_steps(all_ref, None)
        row = lax.broadcasted_iota(jnp.int32, (WINDOW, LANES), 0)
        for m in range(3):
            used = (row > m) & (row < WINDOW - 1 - m)
            block = jnp.where(used, last[m], swapped(last[6 - m]))
            out_ref[2 * m], out_ref[2 * m + 1] = block[: WINDOW // 2], block[WINDOW // 2 :]
        out_ref[6] = last[3][WINDOW // 4 : 3 * WINDOW // 4]
        for h in range(2):
            half = pl.ds(h * WINDOW // 2, WINDOW // 2)
            out_ref[7 + h] = all_ref[EARLY.index(all_ref.shape[0] - 1), 1, half]
        mine_ref[...] = own_slot(sol, found)


def own_slot(sol, found):
    for k, value in enumerate(sol):
        found[k] = value
    return found[lax.rem(lax.axis_index("tm"), 2 * len(sol)) // 2]


def spread(window):
    mask = x_mask()
    mine = 2 * NEAR - 1
    both = [window[mine + b : mine + b + 1] * mask for b in range(2)]
    fine = exact_dot(jnp.concatenate(both, axis=0), fold_matrix(LANES, CY, False))
    return [fine[b * CX : (b + 1) * CX] for b in range(2)]


def result_kernel(lp_ref, mine_ref, out_ref):
    for b, value in enumerate(spread(mine_ref[...])):
        for t in range(CT):
            for z in range(4 * b, 4 * b + 4):
                out_ref[t, z] = lp_ref[t, z] + value


def second_half_kernel(lp_ref, all_ref, bound_ref, _, out_ref, found, result, sems):
    @pl.when(lax.axis_index("tm") >= all_ref.shape[0])
    def _():
        sol, _ = coarse_steps(all_ref, bound_ref)
        values = spread(own_slot(sol, found))
        copies = []
        for t in range(CT):
            for b, value in enumerate(values):
                for z in range(4 * b, 4 * b + 4):
                    result[t, z] = lp_ref[t, z] + value
                part = pl.ds(4 * b, 4)
                copy = pltpu.make_async_copy(
                    result.at[t, part], out_ref.at[t, part], sems.at[2 * t + b]
                )
                copy.start()
                copies.append(copy)
        for copy in copies:
            copy.wait()


def call(kernel, shapes, count, scratch=()):
    single = not isinstance(shapes, (list, tuple))
    return pl.pallas_call(
        kernel,
        out_shape=shapes if single else list(shapes),
        in_specs=[VMEM] * count,
        out_specs=VMEM if single else [VMEM] * len(shapes),
        scratch_shapes=list(scratch),
        compiler_params=pltpu.CompilerParams(vmem_limit_bytes=32 << 20),
    )


def arr(*shape):
    return jax.ShapeDtypeStruct(shape, F32)


def local(right_side, state):
    slabs = lax.axis_size("tm")
    planes = lax.axis_size("space")
    half = slabs // 2
    across = [(k, (k + 1) % planes) for k in range(1, planes, 2)]
    across += [(b, a) for a, b in across]
    within = [(k, k + 1) for k in range(0, planes, 2)]
    within += [(b, a) for a, b in within]
    onward = [(i, i + 1) for i in range(slabs - 1)]

    edge = arr(2, CT, OV, CX, CY)
    own, outer, inner = call(first_kernel, [arr(4, CT, CZ, CX, CY), edge, edge], 1)(
        jnp.stack([right_side, state])
    )
    outer = lax.ppermute(outer, "space", across)
    inner = lax.ppermute(inner, "space", within)
    inside = call(inner_kernel, arr(3 * CZ - 6, CX, CY), 1)(own)
    passed = lax.ppermute(inside, "tm", onward)
    sent = call(later_kernel, arr(12, CX, CY), 4)(own, outer, inner, inside)
    ends = lax.ppermute(sent, "tm", onward)
    v2, v3, v4, rest = call(
        early_kernel,
        [
            arr(CT, CZ + 4, CX, CY),
            arr(CT - 1, CZ + 2, CX, CY),
            arr(CT - 2, CZ, CX, CY),
            arr(CZ, CX, CY),
        ],
        3,
    )(own, outer, inner)
    coef = call(coef_kernel, arr(8, LANES), 1, [pltpu.VMEM((8, CX, CY), F32)])(own)
    other_coef = lax.ppermute(coef, "tm", [(i, i - 1) for i in range(1, slabs, 2)])
    lp, sums = call(
        main_kernel,
        [arr(CT, CZ, CX, CY), arr(planes, 8, LANES)],
        11,
        [
            pltpu.VMEM((CZ + 4, CX, CY), F32),
            pltpu.VMEM((2, CZ + 2, CX, CY), F32),
            pltpu.VMEM((6, CX, CY), F32),
        ],
    )(own, outer, inner, v2, v3, v4, rest, passed, ends, coef, other_coef)
    column = lax.all_to_all(
        sums, "space", 0, 0, axis_index_groups=[[(p + TURN) % planes for p in range(planes)]]
    )
    window = call(
        window_kernel,
        arr(half, 2, WINDOW, LANES),
        1,
        [pltpu.VMEM((2, WINDOW, LANES), F32)],
    )(column)
    halves = [list(EARLY), [half + k for k in LATE]]
    every = lax.all_to_all(window, "tm", 0, 0, axis_index_groups=halves)
    found = pltpu.VMEM((half // 2, WINDOW, LANES), F32)
    last, mine = call(bound_kernel, [arr(9, WINDOW // 2, LANES), arr(WINDOW, LANES)], 1, [found])(every)
    quarter = half // 2
    order = (0, 2, 1, 3, 6, 5, 4, 7) if half == 8 else tuple(range(half))
    serve = [((quarter + k) % half, half + order[k]) for k in range(half)]
    bound = lax.ppermute(last, "tm", serve)
    shape = arr(CT, CZ, CX, CY)
    result = call(result_kernel, shape, 2)(lp, mine)
    anywhere = pl.BlockSpec(memory_space=pl.ANY)
    return pl.pallas_call(
        second_half_kernel,
        out_shape=shape,
        in_specs=[VMEM, VMEM, VMEM, anywhere],
        out_specs=anywhere,
        scratch_shapes=[
            found,
            pltpu.VMEM((CT, CZ, CX, CY), F32),
            pltpu.SemaphoreType.DMA((2 * CT,)),
        ],
        input_output_aliases={3: 0},
        compiler_params=pltpu.CompilerParams(vmem_limit_bytes=32 << 20),
    )(lp, every, bound, result)


def solution(mesh):
    return jax.shard_map(
        local,
        mesh=mesh,
        in_specs=(P("tm", "space", None, None), P("tm", "space", None, None)),
        out_specs=P("tm", "space", None, None),
        check_vma=False,
    )
```

```python
import jax
import jax.numpy as jnp
from jax import lax
from jax.experimental import pallas as pl
from jax.experimental.pallas import tpu as pltpu
from jax.sharding import PartitionSpec as P

CX = 16
CY = 128
CT = 4
CZ = 8
OV = 2
SWEEPS = 4
CHEB = 8
LANES = 128
NEAR = 4
WINDOW = 16
TURN = 5
EARLY = (5, 7, 6, 4, 3, 2, 1, 0)
LATE = (2, 7, 6, 5, 4, 3, 1, 0)

rate = 8.0
react = 0.5
damp = 0.9
theta = 0.8
delta = 0.6

F32 = jnp.float32
PLANE = (CX, CY)
VMEM = pl.BlockSpec(memory_space=pltpu.VMEM)


def beside(v):
    total = pltpu.roll(v, 1, 0) + pltpu.roll(v, CX - 1, 0)
    return total + (pltpu.roll(v, 1, 1) + pltpu.roll(v, CY - 1, 1))


def swept(v, first, scale, near, before):
    total = beside(v)
    for plane in near:
        if plane is not None:
            total = total + plane
    if before is not None:
        total = total + rate * before
    return (1.0 - damp) * v + first + scale * total


def by_parity(body, first, second):
    odd = at_ref[0] & 1

    @pl.when(odd == 0)
    def _():
        body(first, second)

    @pl.when(odd == 1)
    def _():
        body(second, first)


def by_parity(body, first, second):
    odd = lax.axis_index("space") & 1

    @pl.when(odd == 0)
    def _():
        body(first, second)

    @pl.when(odd == 1)
    def _():
        body(second, first)


def first_kernel(loaded_ref, own_ref, outer_ref, inner_ref):
    def body(low_ref, high_ref):
        for t in range(CT):
            for z in range(CZ):
                rhs, s = loaded_ref[0, t, z], loaded_ref[1, t, z]
                diag = (rate + 6.0 - react) + (3.0 * react) * (s * s)
                scale = damp / diag
                first = scale * rhs
                for which, value in enumerate((scale, first, diag, rhs)):
                    own_ref[which, t, z] = value
                if z < OV:
                    low_ref[0, t, z], low_ref[1, t, z] = scale, first
                if z >= CZ - OV:
                    high_ref[0, t, z - (CZ - OV)] = scale
                    high_ref[1, t, z - (CZ - OV)] = first

    by_parity(body, outer_ref, inner_ref)


def reader(which, own_ref, low_ref, high_ref):
    def read(t, z):
        if z < 0:
            return low_ref[which, t, z + OV]
        if z >= CZ:
            return high_ref[which, t, z - CZ]
        return own_ref[which, t, z]

    return read


def inner_kernel(own_ref, out_ref):
    a, b = CT - 2, CT - 1

    def scale(t, z):
        return own_ref[0, t, z]

    def first(t, z):
        return own_ref[1, t, z]

    for z in range(CZ):
        out_ref[z] = first(b, z)
    for z in range(1, CZ - 1):
        v = first(b, z)
        near = (first(b, z - 1), first(b, z + 1))
        out_ref[CZ + z - 1] = swept(v, v, scale(b, z), near, first(a, z))
    for z in range(2, CZ - 2):
        v = first(a, z)
        second = swept(v, v, scale(a, z), (first(a, z - 1), first(a, z + 1)), None)
        near = (out_ref[CZ + z - 2], out_ref[CZ + z])
        out_ref[2 * CZ + z - 4] = swept(
            out_ref[CZ + z - 1], first(b, z), scale(b, z), near, second
        )


FIRST_ENDS = (-2, -1, CZ, CZ + 1)
SECOND_ENDS = (-1, 0, CZ - 1, CZ)
THIRD_ENDS = (0, 1, CZ - 2, CZ - 1)


def earlier_step(inside_ref, ends_ref):
    def first(z):
        return ends_ref[FIRST_ENDS.index(z)] if z in FIRST_ENDS else inside_ref[z]

    def second(z):
        if z in SECOND_ENDS:
            return ends_ref[4 + SECOND_ENDS.index(z)]
        return inside_ref[CZ + z - 1]

    def third(z):
        if z in THIRD_ENDS:
            return ends_ref[8 + THIRD_ENDS.index(z)]
        return inside_ref[2 * CZ + z - 4]

    return first, second, third


def later_kernel(own_ref, outer_ref, inner_ref, inside_ref, out_ref):
    a, b = CT - 2, CT - 1

    def body(low_ref, high_ref):
        scale = reader(0, own_ref, low_ref, high_ref)
        first = reader(1, own_ref, low_ref, high_ref)
        _, second, _ = earlier_step(inside_ref, out_ref)
        for k, z in enumerate(FIRST_ENDS):
            out_ref[k] = first(b, z)
        for k, z in enumerate(SECOND_ENDS):
            v = first(b, z)
            near = (first(b, z - 1), first(b, z + 1))
            out_ref[4 + k] = swept(v, v, scale(b, z), near, first(a, z))
        for k, z in enumerate(THIRD_ENDS):
            v = first(a, z)
            before = swept(v, v, scale(a, z), (first(a, z - 1), first(a, z + 1)), None)
            near = (second(z - 1), second(z + 1))
            out_ref[8 + k] = swept(second(z), first(b, z), scale(b, z), near, before)

    by_parity(body, outer_ref, inner_ref)


def fold_matrix(rows, columns, fine_first):
    i = lax.broadcasted_iota(jnp.int32, (rows, columns), 0)
    k = lax.broadcasted_iota(jnp.int32, (rows, columns), 1)
    fine, lane = (i, k) if fine_first else (k, i)
    return jnp.where(lax.shift_right_logical(fine, 2) == (lane & (CY // 4 - 1)), 1.0, 0.0)


def x_mask():
    x = lax.broadcasted_iota(jnp.int32, PLANE, 0)
    lane = lax.broadcasted_iota(jnp.int32, PLANE, 1)
    return jnp.where(lax.shift_right_logical(x, 2) == lax.shift_right_logical(lane, 5), 1.0, 0.0)


def early_kernel(own_ref, outer_ref, inner_ref, v2_ref, v3_ref, v4_ref, rest_ref):
    def body(low_ref, high_ref):
        scale = reader(0, own_ref, low_ref, high_ref)
        first = reader(1, own_ref, low_ref, high_ref)
        for t in range(CT):
            for z in range(-2, CZ + 2):
                v = first(t, z)
                near = [first(t, q) for q in (z - 1, z + 1) if -2 <= q < CZ + 2]
                before = first(t - 1, z) if t > 0 else None
                v2_ref[t, z + 2] = swept(v, v, scale(t, z), near, before)
        for t in range(1, CT):
            for z in range(-1, CZ + 1):
                near = (v2_ref[t, z + 1], v2_ref[t, z + 3])
                before = v2_ref[t - 1, z + 2] if t > 1 else None
                v3_ref[t - 1, z + 1] = swept(
                    v2_ref[t, z + 2], first(t, z), scale(t, z), near, before
                )
        for t in range(2, CT):
            for z in range(CZ):
                near = (v3_ref[t - 1, z], v3_ref[t - 1, z + 2])
                before = v3_ref[t - 2, z + 1] if t > 2 else None
                v4_ref[t - 2, z] = swept(
                    v3_ref[t - 1, z + 1], first(t, z), scale(t, z), near, before
                )

    by_parity(body, outer_ref, inner_ref)
    for z in range(CZ):
        rest = own_ref[3, 0, z] - own_ref[2, CT - 1, z] * v4_ref[1, z]
        for t in range(1, CT):
            rest = rest + own_ref[3, t, z]
        rest_ref[z] = rest


def exact_dot(x, ones):
    parts = []
    for _ in range(3):
        part = x.astype(jnp.bfloat16)
        parts.append(part)
        x = x - part.astype(F32)
    ones = ones.astype(jnp.bfloat16)
    high, mid, low = (jnp.dot(part, ones, preferred_element_type=F32) for part in parts)
    return high + (mid + low)


def fold(planes):
    folded = exact_dot(planes.reshape(-1, CY), fold_matrix(CY, LANES, True))
    return jnp.sum(folded.reshape(-1, CX, LANES) * x_mask()[None], axis=1)


def coef_kernel(own_ref, out_ref, stack):
    stack[...] = jnp.zeros_like(stack)
    for b in range(2):
        total = None
        for t in range(CT):
            for z in range(4 * b, 4 * b + 4):
                diag = own_ref[2, t, z]
                total = diag if total is None else total + diag
        stack[4 + b] = (total - 4 * CT * (rate + 6.0)) * (1.0 / react)
    out_ref[...] = fold(stack[...])


def main_kernel(
    own_ref,
    outer_ref,
    inner_ref,
    v2_ref,
    v3_ref,
    v4_ref,
    rest_ref,
    inside_ref,
    ends_ref,
    coef_ref,
    other_coef_ref,
    lp_ref,
    sums_ref,
    v2,
    v3,
    stack,
):
    first_before, second_before, third_before = earlier_step(inside_ref, ends_ref)

    def body(low_ref, high_ref):
        scale = reader(0, own_ref, low_ref, high_ref)
        own = reader(1, own_ref, low_ref, high_ref)
        for z in range(-2, CZ + 2):
            v2[z + 2] = v2_ref[0, z + 2] + rate * scale(0, z) * first_before(z)
        for z in range(-1, CZ + 1):
            near = (v2[z + 1], v2[z + 3])
            before = second_before(z)
            v3[0, z + 1] = swept(v2[z + 2], own(0, z), scale(0, z), near, before)
            v3[1, z + 1] = v3_ref[0, z + 1] + rate * scale(1, z) * v2[z + 2]

    by_parity(body, outer_ref, inner_ref)

    rest = []
    planes = []
    for z in range(CZ):
        part = rest_ref[z]
        early = None
        for t in range(CT - 1):
            scale = own_ref[0, t, z]
            if t < 2:
                before = third_before(z) if t == 0 else v3[0, z + 1]
                near = (v3[t, z], v3[t, z + 2])
                value = swept(v3[t, z + 1], own_ref[1, t, z], scale, near, before)
            else:
                value = v4_ref[0, z] + rate * scale * v3[1, z + 1]
            lp_ref[t, z] = value
            part = part - own_ref[2, t, z] * value
            early = value if early is None else early + value
        value = v4_ref[1, z]
        lp_ref[CT - 1, z] = value
        rest.append(part + rate * early)
        planes.append(early + value)
    odd = (lax.axis_index("tm") & 1) == 1
    for b in range(2):
        z = 4 * b
        total = planes[z] + planes[z + 1] + planes[z + 2] + planes[z + 3]
        inner = planes[z] + planes[z + 3] + 2.0 * (planes[z + 1] + planes[z + 2])
        inner = inner + (planes[4] if b == 0 else planes[3])
        value = rest[z] + rest[z + 1] + rest[z + 2] + rest[z + 3]
        value = value + beside(total) + inner
        last = v4_ref[1, z] + v4_ref[1, z + 1]
        last = rate * (last + (v4_ref[1, z + 2] + v4_ref[1, z + 3]))
        stack[b] = jnp.where(odd, value, value + last)
        stack[4 + b] = jnp.where(odd, last, 0.0)
    stack[2] = planes[0]
    stack[3] = planes[CZ - 1]
    coef = coef_ref[...] + other_coef_ref[...]
    none = jnp.zeros((2, LANES), F32)
    sums = jnp.concatenate([fold(stack[...]), none], axis=0) + jnp.where(odd, 0.0, coef)
    sums_ref[...] = jnp.broadcast_to(sums[None], sums_ref.shape)


def window_kernel(all_ref, out_ref, rows):
    plane = lax.axis_index("space")
    count = all_ref.shape[0]
    parts = [all_ref[lax.rem(plane + (2 * count - TURN - NEAR + k), count)] for k in range(2 * NEAR + 1)]
    for k, part in enumerate(parts):
        low, high = part[0:1], part[1:2]
        if k > 0:
            low = low + parts[k - 1][3:4]
        if k < 2 * NEAR:
            high = high + parts[k + 1][2:3]
        if k > 0:
            rows[0, 2 * k - 1 : 2 * k] = low
            rows[1, 2 * k - 1 : 2 * k] = part[4:5]
        if k < 2 * NEAR:
            rows[0, 2 * k : 2 * k + 1] = high
            rows[1, 2 * k : 2 * k + 1] = part[5:6]
    value = rows[...]
    for k in range(out_ref.shape[0]):
        out_ref[k] = value


def coarse_steps(all_ref, bound_ref):
    lane = lax.broadcasted_iota(jnp.int32, (WINDOW, LANES), 1) & (CY // 4 - 1)
    width = CY // 4
    is_first, is_last = lane == 0, lane == width - 1

    def around(f):
        total = pltpu.roll(f, width, 1) + pltpu.roll(f, LANES - width, 1)
        after = jnp.where(is_last, pltpu.roll(f, width - 1, 1), pltpu.roll(f, LANES - 1, 1))
        before = jnp.where(is_first, pltpu.roll(f, LANES - width + 1, 1), pltpu.roll(f, 1, 1))
        return (total + (pltpu.roll(f, 1, 0) + pltpu.roll(f, WINDOW - 1, 0))) + (after + before)

    slots = all_ref.shape[0] // 2
    order = EARLY if bound_ref is None else LATE

    def slab(k, which):
        return all_ref[order.index(k), which]

    inverse = []
    resid = []
    for k in range(slots):
        rhs = slab(2 * k, 0) + slab(2 * k + 1, 0)
        if k > 0:
            rhs = rhs + slab(2 * k - 1, 1)
        elif bound_ref is not None:
            rhs = rhs + handed(bound_ref, 4)
        coef = slab(2 * k, 1)
        inv = 1.0 / (1.375 + (react / 512.0) * coef)
        inverse.append(inv)
        resid.append((rhs * (1.0 / 512.0)) * inv)
    step = [r * (1.0 / theta) for r in resid]
    sol = list(step)
    rho = delta / theta
    last = []
    beside = [i * (1.0 / 16.0) for i in inverse]
    for m in range(1, CHEB):
        nxt = 1.0 / (2.0 * theta / delta - rho)
        last.append(step[-1])
        known = []
        for k in range(slots):
            value = resid[k] - step[k]
            if k > 0:
                value = value + step[k - 1] * inverse[k]
            elif bound_ref is not None:
                value = value + handed(bound_ref, m - 1 if m <= 4 else m) * inverse[k]
            known.append(value)
        for k in range(slots):
            resid[k] = known[k] + around(step[k]) * beside[k]
        for k in range(slots):
            step[k] = (nxt * rho) * step[k] + (2.0 * nxt / delta) * resid[k]
            sol[k] = sol[k] + step[k]
        rho = nxt
    return sol, last


def swapped(v):
    return jnp.concatenate([v[WINDOW // 2 :], v[: WINDOW // 2]], axis=0)


def handed(bound_ref, k):
    if k == 3:
        none = jnp.zeros((WINDOW // 4, LANES), F32)
        return jnp.concatenate([none, bound_ref[6], none], axis=0)
    at = (0, 2, 4, None, 7, 4, 2, 0)[k]
    both = (bound_ref[at], bound_ref[at + 1])
    return jnp.concatenate(both if k <= 4 else both[::-1], axis=0)


def bound_kernel(all_ref, out_ref, mine_ref, found):
    @pl.when(lax.axis_index("tm") < all_ref.shape[0])
    def _():
        sol, last = coarse_steps(all_ref, None)
        row = lax.broadcasted_iota(jnp.int32, (WINDOW, LANES), 0)
        for m in range(3):
            used = (row > m) & (row < WINDOW - 1 - m)
            block = jnp.where(used, last[m], swapped(last[6 - m]))
            out_ref[2 * m], out_ref[2 * m + 1] = block[: WINDOW // 2], block[WINDOW // 2 :]
        out_ref[6] = last[3][WINDOW // 4 : 3 * WINDOW // 4]
        for h in range(2):
            half = pl.ds(h * WINDOW // 2, WINDOW // 2)
            out_ref[7 + h] = all_ref[EARLY.index(all_ref.shape[0] - 1), 1, half]
        mine_ref[...] = own_slot(sol, found)


def own_slot(sol, found):
    for k, value in enumerate(sol):
        found[k] = value
    return found[lax.rem(lax.axis_index("tm"), 2 * len(sol)) // 2]


def spread(window):
    mask = x_mask()
    mine = 2 * NEAR - 1
    both = [window[mine + b : mine + b + 1] * mask for b in range(2)]
    fine = exact_dot(jnp.concatenate(both, axis=0), fold_matrix(LANES, CY, False))
    return [fine[b * CX : (b + 1) * CX] for b in range(2)]


def result_kernel(lp_ref, mine_ref, out_ref):
    for b, value in enumerate(spread(mine_ref[...])):
        for t in range(CT):
            for z in range(4 * b, 4 * b + 4):
                out_ref[t, z] = lp_ref[t, z] + value


def second_half_kernel(lp_ref, all_ref, bound_ref, _, out_ref, found, result, sems):
    @pl.when(lax.axis_index("tm") >= all_ref.shape[0])
    def _():
        sol, _ = coarse_steps(all_ref, bound_ref)
        values = spread(own_slot(sol, found))
        copies = []
        for t in range(CT):
            for b, value in enumerate(values):
                for z in range(4 * b, 4 * b + 4):
                    result[t, z] = lp_ref[t, z] + value
                part = pl.ds(4 * b, 4)
                copy = pltpu.make_async_copy(
                    result.at[t, part], out_ref.at[t, part], sems.at[2 * t + b]
                )
                copy.start()
                copies.append(copy)
        for copy in copies:
            copy.wait()


def call(kernel, shapes, count, scratch=()):
    single = not isinstance(shapes, (list, tuple))
    return pl.pallas_call(
        kernel,
        out_shape=shapes if single else list(shapes),
        in_specs=[VMEM] * count,
        out_specs=VMEM if single else [VMEM] * len(shapes),
        scratch_shapes=list(scratch),
        compiler_params=pltpu.CompilerParams(vmem_limit_bytes=32 << 20),
    )


def arr(*shape):
    return jax.ShapeDtypeStruct(shape, F32)


def local(right_side, state):
    slabs = lax.axis_size("tm")
    planes = lax.axis_size("space")
    half = slabs // 2
    across = [(k, (k + 1) % planes) for k in range(1, planes, 2)]
    across += [(b, a) for a, b in across]
    within = [(k, k + 1) for k in range(0, planes, 2)]
    within += [(b, a) for a, b in within]
    onward = [(i, i + 1) for i in range(slabs - 1)]

    edge = arr(2, CT, OV, CX, CY)
    own, outer, inner = call(first_kernel, [arr(4, CT, CZ, CX, CY), edge, edge], 1)(
        jnp.stack([right_side, state])
    )
    outer = lax.ppermute(outer, "space", across)
    inner = lax.ppermute(inner, "space", within)
    inside = call(inner_kernel, arr(3 * CZ - 6, CX, CY), 1)(own)
    passed = lax.ppermute(inside, "tm", onward)
    sent = call(later_kernel, arr(12, CX, CY), 4)(own, outer, inner, inside)
    ends = lax.ppermute(sent, "tm", onward)
    v2, v3, v4, rest = call(
        early_kernel,
        [
            arr(CT, CZ + 4, CX, CY),
            arr(CT - 1, CZ + 2, CX, CY),
            arr(CT - 2, CZ, CX, CY),
            arr(CZ, CX, CY),
        ],
        3,
    )(own, outer, inner)
    coef = call(coef_kernel, arr(8, LANES), 1, [pltpu.VMEM((8, CX, CY), F32)])(own)
    other_coef = lax.ppermute(coef, "tm", [(i, i - 1) for i in range(1, slabs, 2)])
    lp, sums = call(
        main_kernel,
        [arr(CT, CZ, CX, CY), arr(planes, 8, LANES)],
        11,
        [
            pltpu.VMEM((CZ + 4, CX, CY), F32),
            pltpu.VMEM((2, CZ + 2, CX, CY), F32),
            pltpu.VMEM((6, CX, CY), F32),
        ],
    )(own, outer, inner, v2, v3, v4, rest, passed, ends, coef, other_coef)
    column = lax.all_to_all(
        sums, "space", 0, 0, axis_index_groups=[[(p + TURN) % planes for p in range(planes)]]
    )
    window = call(
        window_kernel,
        arr(half, 2, WINDOW, LANES),
        1,
        [pltpu.VMEM((2, WINDOW, LANES), F32)],
    )(column)
    halves = [list(EARLY), [half + k for k in LATE]]
    every = lax.all_to_all(window, "tm", 0, 0, axis_index_groups=halves)
    found = pltpu.VMEM((half // 2, WINDOW, LANES), F32)
    last, mine = call(bound_kernel, [arr(9, WINDOW // 2, LANES), arr(WINDOW, LANES)], 1, [found])(every)
    quarter = half // 2
    order = (0, 2, 1, 3, 6, 5, 4, 7) if half == 8 else tuple(range(half))
    serve = [((quarter + k) % half, half + order[k]) for k in range(half)]
    bound = lax.ppermute(last, "tm", serve)
    shape = arr(CT, CZ, CX, CY)
    result = call(result_kernel, shape, 2)(lp, mine)
    anywhere = pl.BlockSpec(memory_space=pl.ANY)
    return pl.pallas_call(
        second_half_kernel,
        out_shape=shape,
        in_specs=[VMEM, VMEM, VMEM, anywhere],
        out_specs=anywhere,
        scratch_shapes=[
            found,
            pltpu.VMEM((CT, CZ, CX, CY), F32),
            pltpu.SemaphoreType.DMA((2 * CT,)),
        ],
        input_output_aliases={3: 0},
        compiler_params=pltpu.CompilerParams(vmem_limit_bytes=32 << 20),
    )(lp, every, bound, result)


def solution(mesh):
    return jax.shard_map(
        local,
        mesh=mesh,
        in_specs=(P("tm", "space", None, None), P("tm", "space", None, None)),
        out_specs=P("tm", "space", None, None),
        check_vma=False,
    )
```

```python
import jax
import jax.numpy as jnp
from jax import lax
from jax.experimental import pallas as pl
from jax.experimental.pallas import tpu as pltpu
from jax.sharding import PartitionSpec as P

CX = 16
CY = 128
CT = 4
CZ = 8
OV = 2
SWEEPS = 4
CHEB = 8
LANES = 128
NEAR = 4
WINDOW = 16
TURN = 5
EARLY = (5, 7, 6, 4, 3, 2, 1, 0)
LATE = (2, 7, 6, 5, 4, 3, 1, 0)

rate = 8.0
react = 0.5
damp = 0.9
theta = 0.8
delta = 0.6

F32 = jnp.float32
PLANE = (CX, CY)
VMEM = pl.BlockSpec(memory_space=pltpu.VMEM)


def beside(v):
    total = pltpu.roll(v, 1, 0) + pltpu.roll(v, CX - 1, 0)
    return total + (pltpu.roll(v, 1, 1) + pltpu.roll(v, CY - 1, 1))


def swept(v, first, scale, near, before):
    total = beside(v)
    for plane in near:
        if plane is not None:
            total = total + plane
    if before is not None:
        total = total + rate * before
    return (1.0 - damp) * v + first + scale * total


def by_parity(body, first, second):
    odd = at_ref[0] & 1

    @pl.when(odd == 0)
    def _():
        body(first, second)

    @pl.when(odd == 1)
    def _():
        body(second, first)


def by_parity(body, first, second):
    odd = lax.axis_index("space") & 1

    @pl.when(odd == 0)
    def _():
        body(first, second)

    @pl.when(odd == 1)
    def _():
        body(second, first)


def first_kernel(loaded_ref, own_ref, outer_ref, inner_ref):
    def body(low_ref, high_ref):
        for t in range(CT):
            for z in range(CZ):
                rhs, s = loaded_ref[0, t, z], loaded_ref[1, t, z]
                diag = (rate + 6.0 - react) + (3.0 * react) * (s * s)
                scale = damp / diag
                first = scale * rhs
                for which, value in enumerate((scale, first, diag, rhs)):
                    own_ref[which, t, z] = value
                if z < OV:
                    low_ref[0, t, z], low_ref[1, t, z] = scale, first
                if z >= CZ - OV:
                    high_ref[0, t, z - (CZ - OV)] = scale
                    high_ref[1, t, z - (CZ - OV)] = first

    by_parity(body, outer_ref, inner_ref)


def reader(which, own_ref, low_ref, high_ref):
    def read(t, z):
        if z < 0:
            return low_ref[which, t, z + OV]
        if z >= CZ:
            return high_ref[which, t, z - CZ]
        return own_ref[which, t, z]

    return read


def inner_kernel(own_ref, out_ref):
    a, b = CT - 2, CT - 1

    def scale(t, z):
        return own_ref[0, t, z]

    def first(t, z):
        return own_ref[1, t, z]

    for z in range(CZ):
        out_ref[z] = first(b, z)
    for z in range(1, CZ - 1):
        v = first(b, z)
        near = (first(b, z - 1), first(b, z + 1))
        out_ref[CZ + z - 1] = swept(v, v, scale(b, z), near, first(a, z))
    for z in range(2, CZ - 2):
        v = first(a, z)
        second = swept(v, v, scale(a, z), (first(a, z - 1), first(a, z + 1)), None)
        near = (out_ref[CZ + z - 2], out_ref[CZ + z])
        out_ref[2 * CZ + z - 4] = swept(
            out_ref[CZ + z - 1], first(b, z), scale(b, z), near, second
        )


FIRST_ENDS = (-2, -1, CZ, CZ + 1)
SECOND_ENDS = (-1, 0, CZ - 1, CZ)
THIRD_ENDS = (0, 1, CZ - 2, CZ - 1)


def earlier_step(inside_ref, ends_ref):
    def first(z):
        return ends_ref[FIRST_ENDS.index(z)] if z in FIRST_ENDS else inside_ref[z]

    def second(z):
        if z in SECOND_ENDS:
            return ends_ref[4 + SECOND_ENDS.index(z)]
        return inside_ref[CZ + z - 1]

    def third(z):
        if z in THIRD_ENDS:
            return ends_ref[8 + THIRD_ENDS.index(z)]
        return inside_ref[2 * CZ + z - 4]

    return first, second, third


def later_kernel(own_ref, outer_ref, inner_ref, inside_ref, out_ref):
    a, b = CT - 2, CT - 1

    def body(low_ref, high_ref):
        scale = reader(0, own_ref, low_ref, high_ref)
        first = reader(1, own_ref, low_ref, high_ref)
        _, second, _ = earlier_step(inside_ref, out_ref)
        for k, z in enumerate(FIRST_ENDS):
            out_ref[k] = first(b, z)
        for k, z in enumerate(SECOND_ENDS):
            v = first(b, z)
            near = (first(b, z - 1), first(b, z + 1))
            out_ref[4 + k] = swept(v, v, scale(b, z), near, first(a, z))
        for k, z in enumerate(THIRD_ENDS):
            v = first(a, z)
            before = swept(v, v, scale(a, z), (first(a, z - 1), first(a, z + 1)), None)
            near = (second(z - 1), second(z + 1))
            out_ref[8 + k] = swept(second(z), first(b, z), scale(b, z), near, before)

    by_parity(body, outer_ref, inner_ref)


def fold_matrix(rows, columns, fine_first):
    i = lax.broadcasted_iota(jnp.int32, (rows, columns), 0)
    k = lax.broadcasted_iota(jnp.int32, (rows, columns), 1)
    fine, lane = (i, k) if fine_first else (k, i)
    return jnp.where(lax.shift_right_logical(fine, 2) == (lane & (CY // 4 - 1)), 1.0, 0.0)


def x_mask():
    x = lax.broadcasted_iota(jnp.int32, PLANE, 0)
    lane = lax.broadcasted_iota(jnp.int32, PLANE, 1)
    return jnp.where(lax.shift_right_logical(x, 2) == lax.shift_right_logical(lane, 5), 1.0, 0.0)


def early_kernel(own_ref, outer_ref, inner_ref, v2_ref, v3_ref, v4_ref, rest_ref):
    def body(low_ref, high_ref):
        scale = reader(0, own_ref, low_ref, high_ref)
        first = reader(1, own_ref, low_ref, high_ref)
        for t in range(CT):
            for z in range(-2, CZ + 2):
                v = first(t, z)
                near = [first(t, q) for q in (z - 1, z + 1) if -2 <= q < CZ + 2]
                before = first(t - 1, z) if t > 0 else None
                v2_ref[t, z + 2] = swept(v, v, scale(t, z), near, before)
        for t in range(1, CT):
            for z in range(-1, CZ + 1):
                near = (v2_ref[t, z + 1], v2_ref[t, z + 3])
                before = v2_ref[t - 1, z + 2] if t > 1 else None
                v3_ref[t - 1, z + 1] = swept(
                    v2_ref[t, z + 2], first(t, z), scale(t, z), near, before
                )
        for t in range(2, CT):
            for z in range(CZ):
                near = (v3_ref[t - 1, z], v3_ref[t - 1, z + 2])
                before = v3_ref[t - 2, z + 1] if t > 2 else None
                v4_ref[t - 2, z] = swept(
                    v3_ref[t - 1, z + 1], first(t, z), scale(t, z), near, before
                )

    by_parity(body, outer_ref, inner_ref)
    for z in range(CZ):
        rest = own_ref[3, 0, z] - own_ref[2, CT - 1, z] * v4_ref[1, z]
        for t in range(1, CT):
            rest = rest + own_ref[3, t, z]
        rest_ref[z] = rest


def exact_dot(x, ones):
    parts = []
    for _ in range(3):
        part = x.astype(jnp.bfloat16)
        parts.append(part)
        x = x - part.astype(F32)
    ones = ones.astype(jnp.bfloat16)
    high, mid, low = (jnp.dot(part, ones, preferred_element_type=F32) for part in parts)
    return high + (mid + low)


def fold(planes):
    folded = exact_dot(planes.reshape(-1, CY), fold_matrix(CY, LANES, True))
    return jnp.sum(folded.reshape(-1, CX, LANES) * x_mask()[None], axis=1)


def coef_kernel(own_ref, out_ref, stack):
    stack[...] = jnp.zeros_like(stack)
    for b in range(2):
        total = None
        for t in range(CT):
            for z in range(4 * b, 4 * b + 4):
                diag = own_ref[2, t, z]
                total = diag if total is None else total + diag
        stack[4 + b] = (total - 4 * CT * (rate + 6.0)) * (1.0 / react)
    out_ref[...] = fold(stack[...])


def main_kernel(
    own_ref,
    outer_ref,
    inner_ref,
    v2_ref,
    v3_ref,
    v4_ref,
    rest_ref,
    inside_ref,
    ends_ref,
    lp_ref,
    sums_ref,
    v2,
    v3,
    stack,
):
    first_before, second_before, third_before = earlier_step(inside_ref, ends_ref)

    def body(low_ref, high_ref):
        scale = reader(0, own_ref, low_ref, high_ref)
        own = reader(1, own_ref, low_ref, high_ref)
        for z in range(-2, CZ + 2):
            v2[z + 2] = v2_ref[0, z + 2] + rate * scale(0, z) * first_before(z)
        for z in range(-1, CZ + 1):
            near = (v2[z + 1], v2[z + 3])
            before = second_before(z)
            v3[0, z + 1] = swept(v2[z + 2], own(0, z), scale(0, z), near, before)
            v3[1, z + 1] = v3_ref[0, z + 1] + rate * scale(1, z) * v2[z + 2]

    by_parity(body, outer_ref, inner_ref)

    rest = []
    planes = []
    for z in range(CZ):
        part = rest_ref[z]
        early = None
        for t in range(CT - 1):
            scale = own_ref[0, t, z]
            if t < 2:
                before = third_before(z) if t == 0 else v3[0, z + 1]
                near = (v3[t, z], v3[t, z + 2])
                value = swept(v3[t, z + 1], own_ref[1, t, z], scale, near, before)
            else:
                value = v4_ref[0, z] + rate * scale * v3[1, z + 1]
            lp_ref[t, z] = value
            part = part - own_ref[2, t, z] * value
            early = value if early is None else early + value
        value = v4_ref[1, z]
        lp_ref[CT - 1, z] = value
        rest.append(part + rate * early)
        planes.append(early + value)
    odd = (lax.axis_index("tm") & 1) == 1
    for b in range(2):
        z = 4 * b
        total = planes[z] + planes[z + 1] + planes[z + 2] + planes[z + 3]
        inner = planes[z] + planes[z + 3] + 2.0 * (planes[z + 1] + planes[z + 2])
        inner = inner + (planes[4] if b == 0 else planes[3])
        value = rest[z] + rest[z + 1] + rest[z + 2] + rest[z + 3]
        value = value + beside(total) + inner
        last = v4_ref[1, z] + v4_ref[1, z + 1]
        last = rate * (last + (v4_ref[1, z + 2] + v4_ref[1, z + 3]))
        stack[b] = jnp.where(odd, value, value + last)
        stack[4 + b] = jnp.where(odd, last, 0.0)
    stack[2] = planes[0]
    stack[3] = planes[CZ - 1]
    none = jnp.zeros((2, LANES), F32)
    sums_ref[...] = jnp.concatenate([fold(stack[...]), none], axis=0)


def share_kernel(sums_ref, coef_ref, other_coef_ref, out_ref):
    odd = (lax.axis_index("tm") & 1) == 1
    sums = sums_ref[...] + jnp.where(odd, 0.0, coef_ref[...] + other_coef_ref[...])
    out_ref[...] = jnp.broadcast_to(sums[None], out_ref.shape)


def window_kernel(all_ref, out_ref, rows):
    plane = lax.axis_index("space")
    count = all_ref.shape[0]
    parts = [all_ref[lax.rem(plane + (2 * count - TURN - NEAR + k), count)] for k in range(2 * NEAR + 1)]
    for k, part in enumerate(parts):
        low, high = part[0:1], part[1:2]
        if k > 0:
            low = low + parts[k - 1][3:4]
        if k < 2 * NEAR:
            high = high + parts[k + 1][2:3]
        if k > 0:
            rows[0, 2 * k - 1 : 2 * k] = low
            rows[1, 2 * k - 1 : 2 * k] = part[4:5]
        if k < 2 * NEAR:
            rows[0, 2 * k : 2 * k + 1] = high
            rows[1, 2 * k : 2 * k + 1] = part[5:6]
    value = rows[...]
    for k in range(out_ref.shape[0]):
        out_ref[k] = value


def coarse_steps(all_ref, bound_ref):
    lane = lax.broadcasted_iota(jnp.int32, (WINDOW, LANES), 1) & (CY // 4 - 1)
    width = CY // 4
    is_first, is_last = lane == 0, lane == width - 1

    def around(f):
        total = pltpu.roll(f, width, 1) + pltpu.roll(f, LANES - width, 1)
        after = jnp.where(is_last, pltpu.roll(f, width - 1, 1), pltpu.roll(f, LANES - 1, 1))
        before = jnp.where(is_first, pltpu.roll(f, LANES - width + 1, 1), pltpu.roll(f, 1, 1))
        return (total + (pltpu.roll(f, 1, 0) + pltpu.roll(f, WINDOW - 1, 0))) + (after + before)

    slots = all_ref.shape[0] // 2
    order = EARLY if bound_ref is None else LATE

    def slab(k, which):
        return all_ref[order.index(k), which]

    inverse = []
    resid = []
    for k in range(slots):
        rhs = slab(2 * k, 0) + slab(2 * k + 1, 0)
        if k > 0:
            rhs = rhs + slab(2 * k - 1, 1)
        elif bound_ref is not None:
            rhs = rhs + handed(bound_ref, 4)
        coef = slab(2 * k, 1)
        inv = 1.0 / (1.375 + (react / 512.0) * coef)
        inverse.append(inv)
        resid.append((rhs * (1.0 / 512.0)) * inv)
    step = [r * (1.0 / theta) for r in resid]
    sol = list(step)
    rho = delta / theta
    last = []
    beside = [i * (1.0 / 16.0) for i in inverse]
    for m in range(1, CHEB):
        nxt = 1.0 / (2.0 * theta / delta - rho)
        last.append(step[-1])
        known = []
        for k in range(slots):
            value = resid[k] - step[k]
            if k > 0:
                value = value + step[k - 1] * inverse[k]
            elif bound_ref is not None:
                value = value + handed(bound_ref, m - 1 if m <= 4 else m) * inverse[k]
            known.append(value)
        for k in range(slots):
            resid[k] = known[k] + around(step[k]) * beside[k]
        for k in range(slots):
            step[k] = (nxt * rho) * step[k] + (2.0 * nxt / delta) * resid[k]
            sol[k] = sol[k] + step[k]
        rho = nxt
    return sol, last


def swapped(v):
    return jnp.concatenate([v[WINDOW // 2 :], v[: WINDOW // 2]], axis=0)


def handed(bound_ref, k):
    if k == 3:
        none = jnp.zeros((WINDOW // 4, LANES), F32)
        return jnp.concatenate([none, bound_ref[6], none], axis=0)
    at = (0, 2, 4, None, 7, 4, 2, 0)[k]
    both = (bound_ref[at], bound_ref[at + 1])
    return jnp.concatenate(both if k <= 4 else both[::-1], axis=0)


def bound_kernel(all_ref, out_ref, mine_ref, found):
    @pl.when(lax.axis_index("tm") < all_ref.shape[0])
    def _():
        sol, last = coarse_steps(all_ref, None)
        row = lax.broadcasted_iota(jnp.int32, (WINDOW, LANES), 0)
        for m in range(3):
            used = (row > m) & (row < WINDOW - 1 - m)
            block = jnp.where(used, last[m], swapped(last[6 - m]))
            out_ref[2 * m], out_ref[2 * m + 1] = block[: WINDOW // 2], block[WINDOW // 2 :]
        out_ref[6] = last[3][WINDOW // 4 : 3 * WINDOW // 4]
        for h in range(2):
            half = pl.ds(h * WINDOW // 2, WINDOW // 2)
            out_ref[7 + h] = all_ref[EARLY.index(all_ref.shape[0] - 1), 1, half]
        mine_ref[...] = own_slot(sol, found)


def own_slot(sol, found):
    for k, value in enumerate(sol):
        found[k] = value
    return found[lax.rem(lax.axis_index("tm"), 2 * len(sol)) // 2]


def spread(window):
    mask = x_mask()
    mine = 2 * NEAR - 1
    both = [window[mine + b : mine + b + 1] * mask for b in range(2)]
    fine = exact_dot(jnp.concatenate(both, axis=0), fold_matrix(LANES, CY, False))
    return [fine[b * CX : (b + 1) * CX] for b in range(2)]


def result_kernel(lp_ref, mine_ref, out_ref):
    for b, value in enumerate(spread(mine_ref[...])):
        for t in range(CT):
            for z in range(4 * b, 4 * b + 4):
                out_ref[t, z] = lp_ref[t, z] + value


def second_half_kernel(lp_ref, all_ref, bound_ref, _, out_ref, found, result, sems):
    @pl.when(lax.axis_index("tm") >= all_ref.shape[0])
    def _():
        sol, _ = coarse_steps(all_ref, bound_ref)
        values = spread(own_slot(sol, found))
        copies = []
        for t in range(CT):
            for b, value in enumerate(values):
                for z in range(4 * b, 4 * b + 4):
                    result[t, z] = lp_ref[t, z] + value
                part = pl.ds(4 * b, 4)
                copy = pltpu.make_async_copy(
                    result.at[t, part], out_ref.at[t, part], sems.at[2 * t + b]
                )
                copy.start()
                copies.append(copy)
        for copy in copies:
            copy.wait()


def call(kernel, shapes, count, scratch=()):
    single = not isinstance(shapes, (list, tuple))
    return pl.pallas_call(
        kernel,
        out_shape=shapes if single else list(shapes),
        in_specs=[VMEM] * count,
        out_specs=VMEM if single else [VMEM] * len(shapes),
        scratch_shapes=list(scratch),
        compiler_params=pltpu.CompilerParams(vmem_limit_bytes=32 << 20),
    )


def arr(*shape):
    return jax.ShapeDtypeStruct(shape, F32)


def local(right_side, state):
    slabs = lax.axis_size("tm")
    planes = lax.axis_size("space")
    half = slabs // 2
    across = [(k, (k + 1) % planes) for k in range(1, planes, 2)]
    across += [(b, a) for a, b in across]
    within = [(k, k + 1) for k in range(0, planes, 2)]
    within += [(b, a) for a, b in within]
    onward = [(i, i + 1) for i in range(slabs - 1)]

    edge = arr(2, CT, OV, CX, CY)
    own, outer, inner = call(first_kernel, [arr(4, CT, CZ, CX, CY), edge, edge], 1)(
        jnp.stack([right_side, state])
    )
    outer = lax.ppermute(outer, "space", across)
    inner = lax.ppermute(inner, "space", within)
    inside = call(inner_kernel, arr(3 * CZ - 6, CX, CY), 1)(own)
    passed = lax.ppermute(inside, "tm", onward)
    sent = call(later_kernel, arr(12, CX, CY), 4)(own, outer, inner, inside)
    ends = lax.ppermute(sent, "tm", onward)
    v2, v3, v4, rest = call(
        early_kernel,
        [
            arr(CT, CZ + 4, CX, CY),
            arr(CT - 1, CZ + 2, CX, CY),
            arr(CT - 2, CZ, CX, CY),
            arr(CZ, CX, CY),
        ],
        3,
    )(own, outer, inner)
    coef = call(coef_kernel, arr(8, LANES), 1, [pltpu.VMEM((8, CX, CY), F32)])(own)
    other_coef = lax.ppermute(coef, "tm", [(i, i - 1) for i in range(1, slabs, 2)])
    lp, sums = call(
        main_kernel,
        [arr(CT, CZ, CX, CY), arr(8, LANES)],
        9,
        [
            pltpu.VMEM((CZ + 4, CX, CY), F32),
            pltpu.VMEM((2, CZ + 2, CX, CY), F32),
            pltpu.VMEM((6, CX, CY), F32),
        ],
    )(own, outer, inner, v2, v3, v4, rest, passed, ends)
    sums = call(share_kernel, arr(planes, 8, LANES), 3)(sums, coef, other_coef)
    column = lax.all_to_all(
        sums, "space", 0, 0, axis_index_groups=[[(p + TURN) % planes for p in range(planes)]]
    )
    window = call(
        window_kernel,
        arr(half, 2, WINDOW, LANES),
        1,
        [pltpu.VMEM((2, WINDOW, LANES), F32)],
    )(column)
    halves = [list(EARLY), [half + k for k in LATE]]
    every = lax.all_to_all(window, "tm", 0, 0, axis_index_groups=halves)
    found = pltpu.VMEM((half // 2, WINDOW, LANES), F32)
    last, mine = call(bound_kernel, [arr(9, WINDOW // 2, LANES), arr(WINDOW, LANES)], 1, [found])(every)
    quarter = half // 2
    order = (0, 2, 1, 3, 6, 5, 4, 7) if half == 8 else tuple(range(half))
    serve = [((quarter + k) % half, half + order[k]) for k in range(half)]
    bound = lax.ppermute(last, "tm", serve)
    shape = arr(CT, CZ, CX, CY)
    result = call(result_kernel, shape, 2)(lp, mine)
    anywhere = pl.BlockSpec(memory_space=pl.ANY)
    return pl.pallas_call(
        second_half_kernel,
        out_shape=shape,
        in_specs=[VMEM, VMEM, VMEM, anywhere],
        out_specs=anywhere,
        scratch_shapes=[
            found,
            pltpu.VMEM((CT, CZ, CX, CY), F32),
            pltpu.SemaphoreType.DMA((2 * CT,)),
        ],
        input_output_aliases={3: 0},
        compiler_params=pltpu.CompilerParams(vmem_limit_bytes=32 << 20),
    )(lp, every, bound, result)


def solution(mesh):
    return jax.shard_map(
        local,
        mesh=mesh,
        in_specs=(P("tm", "space", None, None), P("tm", "space", None, None)),
        out_specs=P("tm", "space", None, None),
        check_vma=False,
    )
```

```python
import jax
import jax.numpy as jnp
from jax import lax
from jax.experimental import pallas as pl
from jax.experimental.pallas import tpu as pltpu
from jax.sharding import PartitionSpec as P

CX = 16
CY = 128
CT = 4
CZ = 8
OV = 2
SWEEPS = 4
CHEB = 8
LANES = 128
NEAR = 4
WINDOW = 16
TURN = 5
EARLY = (5, 7, 6, 4, 3, 2, 1, 0)
LATE = (2, 7, 6, 5, 4, 3, 1, 0)

rate = 8.0
react = 0.5
damp = 0.9
theta = 0.8
delta = 0.6

F32 = jnp.float32
PLANE = (CX, CY)
VMEM = pl.BlockSpec(memory_space=pltpu.VMEM)


def beside(v):
    total = pltpu.roll(v, 1, 0) + pltpu.roll(v, CX - 1, 0)
    return total + (pltpu.roll(v, 1, 1) + pltpu.roll(v, CY - 1, 1))


def swept(v, first, scale, near, before):
    total = beside(v)
    for plane in near:
        if plane is not None:
            total = total + plane
    if before is not None:
        total = total + rate * before
    return (1.0 - damp) * v + first + scale * total


def by_parity(body, first, second):
    odd = at_ref[0] & 1

    @pl.when(odd == 0)
    def _():
        body(first, second)

    @pl.when(odd == 1)
    def _():
        body(second, first)


def by_parity(body, first, second):
    odd = lax.axis_index("space") & 1

    @pl.when(odd == 0)
    def _():
        body(first, second)

    @pl.when(odd == 1)
    def _():
        body(second, first)


def first_kernel(loaded_ref, own_ref, outer_ref, inner_ref):
    def body(low_ref, high_ref):
        for t in range(CT):
            for z in range(CZ):
                rhs, s = loaded_ref[0, t, z], loaded_ref[1, t, z]
                diag = (rate + 6.0 - react) + (3.0 * react) * (s * s)
                scale = damp / diag
                first = scale * rhs
                for which, value in enumerate((scale, first, diag, rhs)):
                    own_ref[which, t, z] = value
                if z < OV:
                    low_ref[0, t, z], low_ref[1, t, z] = scale, first
                if z >= CZ - OV:
                    high_ref[0, t, z - (CZ - OV)] = scale
                    high_ref[1, t, z - (CZ - OV)] = first

    by_parity(body, outer_ref, inner_ref)


def reader(which, own_ref, low_ref, high_ref):
    def read(t, z):
        if z < 0:
            return low_ref[which, t, z + OV]
        if z >= CZ:
            return high_ref[which, t, z - CZ]
        return own_ref[which, t, z]

    return read


def inner_kernel(own_ref, out_ref):
    a, b = CT - 2, CT - 1

    def scale(t, z):
        return own_ref[0, t, z]

    def first(t, z):
        return own_ref[1, t, z]

    for z in range(CZ):
        out_ref[z] = first(b, z)
    for z in range(1, CZ - 1):
        v = first(b, z)
        near = (first(b, z - 1), first(b, z + 1))
        out_ref[CZ + z - 1] = swept(v, v, scale(b, z), near, first(a, z))
    for z in range(2, CZ - 2):
        v = first(a, z)
        second = swept(v, v, scale(a, z), (first(a, z - 1), first(a, z + 1)), None)
        near = (out_ref[CZ + z - 2], out_ref[CZ + z])
        out_ref[2 * CZ + z - 4] = swept(
            out_ref[CZ + z - 1], first(b, z), scale(b, z), near, second
        )


FIRST_ENDS = (-2, -1, CZ, CZ + 1)
SECOND_ENDS = (-1, 0, CZ - 1, CZ)
THIRD_ENDS = (0, 1, CZ - 2, CZ - 1)


def earlier_step(inside_ref, ends_ref):
    def first(z):
        return ends_ref[FIRST_ENDS.index(z)] if z in FIRST_ENDS else inside_ref[z]

    def second(z):
        if z in SECOND_ENDS:
            return ends_ref[4 + SECOND_ENDS.index(z)]
        return inside_ref[CZ + z - 1]

    def third(z):
        if z in THIRD_ENDS:
            return ends_ref[8 + THIRD_ENDS.index(z)]
        return inside_ref[2 * CZ + z - 4]

    return first, second, third


def later_kernel(own_ref, outer_ref, inner_ref, inside_ref, out_ref):
    a, b = CT - 2, CT - 1

    def body(low_ref, high_ref):
        scale = reader(0, own_ref, low_ref, high_ref)
        first = reader(1, own_ref, low_ref, high_ref)
        _, second, _ = earlier_step(inside_ref, out_ref)
        for k, z in enumerate(FIRST_ENDS):
            out_ref[k] = first(b, z)
        for k, z in enumerate(SECOND_ENDS):
            v = first(b, z)
            near = (first(b, z - 1), first(b, z + 1))
            out_ref[4 + k] = swept(v, v, scale(b, z), near, first(a, z))
        for k, z in enumerate(THIRD_ENDS):
            v = first(a, z)
            before = swept(v, v, scale(a, z), (first(a, z - 1), first(a, z + 1)), None)
            near = (second(z - 1), second(z + 1))
            out_ref[8 + k] = swept(second(z), first(b, z), scale(b, z), near, before)

    by_parity(body, outer_ref, inner_ref)


def fold_matrix(rows, columns, fine_first):
    i = lax.broadcasted_iota(jnp.int32, (rows, columns), 0)
    k = lax.broadcasted_iota(jnp.int32, (rows, columns), 1)
    fine, lane = (i, k) if fine_first else (k, i)
    return jnp.where(lax.shift_right_logical(fine, 2) == (lane & (CY // 4 - 1)), 1.0, 0.0)


def x_mask():
    x = lax.broadcasted_iota(jnp.int32, PLANE, 0)
    lane = lax.broadcasted_iota(jnp.int32, PLANE, 1)
    return jnp.where(lax.shift_right_logical(x, 2) == lax.shift_right_logical(lane, 5), 1.0, 0.0)


def early_kernel(own_ref, outer_ref, inner_ref, v2_ref, v3_ref, v4_ref, rest_ref):
    def body(low_ref, high_ref):
        scale = reader(0, own_ref, low_ref, high_ref)
        first = reader(1, own_ref, low_ref, high_ref)
        for t in range(CT):
            for z in range(-2, CZ + 2):
                v = first(t, z)
                near = [first(t, q) for q in (z - 1, z + 1) if -2 <= q < CZ + 2]
                before = first(t - 1, z) if t > 0 else None
                v2_ref[t, z + 2] = swept(v, v, scale(t, z), near, before)
        for t in range(1, CT):
            for z in range(-1, CZ + 1):
                near = (v2_ref[t, z + 1], v2_ref[t, z + 3])
                before = v2_ref[t - 1, z + 2] if t > 1 else None
                v3_ref[t - 1, z + 1] = swept(
                    v2_ref[t, z + 2], first(t, z), scale(t, z), near, before
                )
        for t in range(2, CT):
            for z in range(CZ):
                near = (v3_ref[t - 1, z], v3_ref[t - 1, z + 2])
                before = v3_ref[t - 2, z + 1] if t > 2 else None
                v4_ref[t - 2, z] = swept(
                    v3_ref[t - 1, z + 1], first(t, z), scale(t, z), near, before
                )

    by_parity(body, outer_ref, inner_ref)
    for z in range(CZ):
        rest = own_ref[3, 0, z] - own_ref[2, CT - 1, z] * v4_ref[1, z]
        for t in range(1, CT):
            rest = rest + own_ref[3, t, z]
        rest_ref[z] = rest


def exact_dot(x, ones):
    parts = []
    for _ in range(3):
        part = x.astype(jnp.bfloat16)
        parts.append(part)
        x = x - part.astype(F32)
    ones = ones.astype(jnp.bfloat16)
    high, mid, low = (jnp.dot(part, ones, preferred_element_type=F32) for part in parts)
    return high + (mid + low)


def fold(planes):
    folded = exact_dot(planes.reshape(-1, CY), fold_matrix(CY, LANES, True))
    return jnp.sum(folded.reshape(-1, CX, LANES) * x_mask()[None], axis=1)


def coef_kernel(own_ref, out_ref, stack):
    for b in range(2):
        sums = []
        for t in range(CT):
            near = [own_ref[2, t, z] for z in range(4 * b, 4 * b + 4)]
            sums.append((near[0] + near[1]) + (near[2] + near[3]))
        total = (sums[0] + sums[1]) + (sums[2] + sums[3])
        stack[b] = (total - 4 * CT * (rate + 6.0)) * (1.0 / react)
    out_ref[...] = jnp.zeros_like(out_ref)
    out_ref[4:6] = fold(stack[...])


def main_kernel(
    own_ref,
    outer_ref,
    inner_ref,
    v2_ref,
    v3_ref,
    v4_ref,
    rest_ref,
    inside_ref,
    ends_ref,
    lp_ref,
    sums_ref,
    v2,
    v3,
    stack,
):
    first_before, second_before, third_before = earlier_step(inside_ref, ends_ref)

    def body(low_ref, high_ref):
        scale = reader(0, own_ref, low_ref, high_ref)
        own = reader(1, own_ref, low_ref, high_ref)
        for z in range(-2, CZ + 2):
            v2[z + 2] = v2_ref[0, z + 2] + rate * scale(0, z) * first_before(z)
        for z in range(-1, CZ + 1):
            near = (v2[z + 1], v2[z + 3])
            before = second_before(z)
            v3[0, z + 1] = swept(v2[z + 2], own(0, z), scale(0, z), near, before)
            v3[1, z + 1] = v3_ref[0, z + 1] + rate * scale(1, z) * v2[z + 2]

    by_parity(body, outer_ref, inner_ref)

    rest = []
    planes = []
    for z in range(CZ):
        part = rest_ref[z]
        early = None
        for t in range(CT - 1):
            scale = own_ref[0, t, z]
            if t < 2:
                before = third_before(z) if t == 0 else v3[0, z + 1]
                near = (v3[t, z], v3[t, z + 2])
                value = swept(v3[t, z + 1], own_ref[1, t, z], scale, near, before)
            else:
                value = v4_ref[0, z] + rate * scale * v3[1, z + 1]
            lp_ref[t, z] = value
            part = part - own_ref[2, t, z] * value
            early = value if early is None else early + value
        value = v4_ref[1, z]
        lp_ref[CT - 1, z] = value
        rest.append(part + rate * early)
        planes.append(early + value)
    odd = (lax.axis_index("tm") & 1) == 1
    for b in range(2):
        z = 4 * b
        total = planes[z] + planes[z + 1] + planes[z + 2] + planes[z + 3]
        inner = planes[z] + planes[z + 3] + 2.0 * (planes[z + 1] + planes[z + 2])
        inner = inner + (planes[4] if b == 0 else planes[3])
        value = rest[z] + rest[z + 1] + rest[z + 2] + rest[z + 3]
        value = value + beside(total) + inner
        last = v4_ref[1, z] + v4_ref[1, z + 1]
        last = rate * (last + (v4_ref[1, z + 2] + v4_ref[1, z + 3]))
        stack[b] = jnp.where(odd, value, value + last)
        stack[4 + b] = jnp.where(odd, last, 0.0)
    stack[2] = planes[0]
    stack[3] = planes[CZ - 1]
    none = jnp.zeros((2, LANES), F32)
    sums_ref[...] = jnp.concatenate([fold(stack[...]), none], axis=0)


def share_kernel(sums_ref, coef_ref, other_coef_ref, out_ref):
    odd = (lax.axis_index("tm") & 1) == 1
    sums = sums_ref[...] + jnp.where(odd, 0.0, coef_ref[...] + other_coef_ref[...])
    out_ref[...] = jnp.broadcast_to(sums[None], out_ref.shape)


def window_kernel(all_ref, out_ref, rows):
    plane = lax.axis_index("space")
    count = all_ref.shape[0]
    parts = [all_ref[lax.rem(plane + (2 * count - TURN - NEAR + k), count)] for k in range(2 * NEAR + 1)]
    for k, part in enumerate(parts):
        low, high = part[0:1], part[1:2]
        if k > 0:
            low = low + parts[k - 1][3:4]
        if k < 2 * NEAR:
            high = high + parts[k + 1][2:3]
        if k > 0:
            rows[0, 2 * k - 1 : 2 * k] = low
            rows[1, 2 * k - 1 : 2 * k] = part[4:5]
        if k < 2 * NEAR:
            rows[0, 2 * k : 2 * k + 1] = high
            rows[1, 2 * k : 2 * k + 1] = part[5:6]
    value = rows[...]
    for k in range(out_ref.shape[0]):
        out_ref[k] = value


def coarse_steps(all_ref, bound_ref):
    lane = lax.broadcasted_iota(jnp.int32, (WINDOW, LANES), 1) & (CY // 4 - 1)
    width = CY // 4
    is_first, is_last = lane == 0, lane == width - 1

    def around(f):
        total = pltpu.roll(f, width, 1) + pltpu.roll(f, LANES - width, 1)
        after = jnp.where(is_last, pltpu.roll(f, width - 1, 1), pltpu.roll(f, LANES - 1, 1))
        before = jnp.where(is_first, pltpu.roll(f, LANES - width + 1, 1), pltpu.roll(f, 1, 1))
        return (total + (pltpu.roll(f, 1, 0) + pltpu.roll(f, WINDOW - 1, 0))) + (after + before)

    slots = all_ref.shape[0] // 2
    order = EARLY if bound_ref is None else LATE

    def slab(k, which):
        return all_ref[order.index(k), which]

    inverse = []
    resid = []
    for k in range(slots):
        rhs = slab(2 * k, 0) + slab(2 * k + 1, 0)
        if k > 0:
            rhs = rhs + slab(2 * k - 1, 1)
        elif bound_ref is not None:
            rhs = rhs + handed(bound_ref, 4)
        coef = slab(2 * k, 1)
        inv = 1.0 / (1.375 + (react / 512.0) * coef)
        inverse.append(inv)
        resid.append((rhs * (1.0 / 512.0)) * inv)
    step = [r * (1.0 / theta) for r in resid]
    sol = list(step)
    rho = delta / theta
    last = []
    beside = [i * (1.0 / 16.0) for i in inverse]
    for m in range(1, CHEB):
        nxt = 1.0 / (2.0 * theta / delta - rho)
        last.append(step[-1])
        known = []
        for k in range(slots):
            value = resid[k] - step[k]
            if k > 0:
                value = value + step[k - 1] * inverse[k]
            elif bound_ref is not None:
                value = value + handed(bound_ref, m - 1 if m <= 4 else m) * inverse[k]
            known.append(value)
        for k in range(slots):
            resid[k] = known[k] + around(step[k]) * beside[k]
        for k in range(slots):
            step[k] = (nxt * rho) * step[k] + (2.0 * nxt / delta) * resid[k]
            sol[k] = sol[k] + step[k]
        rho = nxt
    return sol, last


def swapped(v):
    return jnp.concatenate([v[WINDOW // 2 :], v[: WINDOW // 2]], axis=0)


def handed(bound_ref, k):
    if k == 3:
        none = jnp.zeros((WINDOW // 4, LANES), F32)
        return jnp.concatenate([none, bound_ref[6], none], axis=0)
    at = (0, 2, 4, None, 7, 4, 2, 0)[k]
    both = (bound_ref[at], bound_ref[at + 1])
    return jnp.concatenate(both if k <= 4 else both[::-1], axis=0)


def bound_kernel(all_ref, out_ref, mine_ref, found):
    @pl.when(lax.axis_index("tm") < all_ref.shape[0])
    def _():
        sol, last = coarse_steps(all_ref, None)
        row = lax.broadcasted_iota(jnp.int32, (WINDOW, LANES), 0)
        for m in range(3):
            used = (row > m) & (row < WINDOW - 1 - m)
            block = jnp.where(used, last[m], swapped(last[6 - m]))
            out_ref[2 * m], out_ref[2 * m + 1] = block[: WINDOW // 2], block[WINDOW // 2 :]
        out_ref[6] = last[3][WINDOW // 4 : 3 * WINDOW // 4]
        for h in range(2):
            half = pl.ds(h * WINDOW // 2, WINDOW // 2)
            out_ref[7 + h] = all_ref[EARLY.index(all_ref.shape[0] - 1), 1, half]
        mine_ref[...] = own_slot(sol, found)


def own_slot(sol, found):
    for k, value in enumerate(sol):
        found[k] = value
    return found[lax.rem(lax.axis_index("tm"), 2 * len(sol)) // 2]


def spread(window):
    mask = x_mask()
    mine = 2 * NEAR - 1
    both = [window[mine + b : mine + b + 1] * mask for b in range(2)]
    fine = exact_dot(jnp.concatenate(both, axis=0), fold_matrix(LANES, CY, False))
    return [fine[b * CX : (b + 1) * CX] for b in range(2)]


def result_kernel(lp_ref, mine_ref, out_ref):
    for b, value in enumerate(spread(mine_ref[...])):
        for t in range(CT):
            for z in range(4 * b, 4 * b + 4):
                out_ref[t, z] = lp_ref[t, z] + value


def second_half_kernel(lp_ref, all_ref, bound_ref, _, out_ref, found, result, sems):
    @pl.when(lax.axis_index("tm") >= all_ref.shape[0])
    def _():
        sol, _ = coarse_steps(all_ref, bound_ref)
        values = spread(own_slot(sol, found))
        copies = []
        for t in range(CT):
            for b, value in enumerate(values):
                for z in range(4 * b, 4 * b + 4):
                    result[t, z] = lp_ref[t, z] + value
                part = pl.ds(4 * b, 4)
                copy = pltpu.make_async_copy(
                    result.at[t, part], out_ref.at[t, part], sems.at[2 * t + b]
                )
                copy.start()
                copies.append(copy)
        for copy in copies:
            copy.wait()


def call(kernel, shapes, count, scratch=()):
    single = not isinstance(shapes, (list, tuple))
    return pl.pallas_call(
        kernel,
        out_shape=shapes if single else list(shapes),
        in_specs=[VMEM] * count,
        out_specs=VMEM if single else [VMEM] * len(shapes),
        scratch_shapes=list(scratch),
        compiler_params=pltpu.CompilerParams(vmem_limit_bytes=32 << 20),
    )


def arr(*shape):
    return jax.ShapeDtypeStruct(shape, F32)


def local(right_side, state):
    slabs = lax.axis_size("tm")
    planes = lax.axis_size("space")
    half = slabs // 2
    across = [(k, (k + 1) % planes) for k in range(1, planes, 2)]
    across += [(b, a) for a, b in across]
    within = [(k, k + 1) for k in range(0, planes, 2)]
    within += [(b, a) for a, b in within]
    onward = [(i, i + 1) for i in range(slabs - 1)]

    edge = arr(2, CT, OV, CX, CY)
    own, outer, inner = call(first_kernel, [arr(4, CT, CZ, CX, CY), edge, edge], 1)(
        jnp.stack([right_side, state])
    )
    outer = lax.ppermute(outer, "space", across)
    inner = lax.ppermute(inner, "space", within)
    inside = call(inner_kernel, arr(3 * CZ - 6, CX, CY), 1)(own)
    passed = lax.ppermute(inside, "tm", onward)
    sent = call(later_kernel, arr(12, CX, CY), 4)(own, outer, inner, inside)
    ends = lax.ppermute(sent, "tm", onward)
    v2, v3, v4, rest = call(
        early_kernel,
        [
            arr(CT, CZ + 4, CX, CY),
            arr(CT - 1, CZ + 2, CX, CY),
            arr(CT - 2, CZ, CX, CY),
            arr(CZ, CX, CY),
        ],
        3,
    )(own, outer, inner)
    coef = call(coef_kernel, arr(8, LANES), 1, [pltpu.VMEM((2, CX, CY), F32)])(own)
    other_coef = lax.ppermute(coef, "tm", [(i, i - 1) for i in range(1, slabs, 2)])
    lp, sums = call(
        main_kernel,
        [arr(CT, CZ, CX, CY), arr(8, LANES)],
        9,
        [
            pltpu.VMEM((CZ + 4, CX, CY), F32),
            pltpu.VMEM((2, CZ + 2, CX, CY), F32),
            pltpu.VMEM((6, CX, CY), F32),
        ],
    )(own, outer, inner, v2, v3, v4, rest, passed, ends)
    sums = call(share_kernel, arr(planes, 8, LANES), 3)(sums, coef, other_coef)
    column = lax.all_to_all(
        sums, "space", 0, 0, axis_index_groups=[[(p + TURN) % planes for p in range(planes)]]
    )
    window = call(
        window_kernel,
        arr(half, 2, WINDOW, LANES),
        1,
        [pltpu.VMEM((2, WINDOW, LANES), F32)],
    )(column)
    halves = [list(EARLY), [half + k for k in LATE]]
    every = lax.all_to_all(window, "tm", 0, 0, axis_index_groups=halves)
    found = pltpu.VMEM((half // 2, WINDOW, LANES), F32)
    last, mine = call(bound_kernel, [arr(9, WINDOW // 2, LANES), arr(WINDOW, LANES)], 1, [found])(every)
    quarter = half // 2
    order = (0, 2, 1, 3, 6, 5, 4, 7) if half == 8 else tuple(range(half))
    serve = [((quarter + k) % half, half + order[k]) for k in range(half)]
    bound = lax.ppermute(last, "tm", serve)
    shape = arr(CT, CZ, CX, CY)
    result = call(result_kernel, shape, 2)(lp, mine)
    anywhere = pl.BlockSpec(memory_space=pl.ANY)
    return pl.pallas_call(
        second_half_kernel,
        out_shape=shape,
        in_specs=[VMEM, VMEM, VMEM, anywhere],
        out_specs=anywhere,
        scratch_shapes=[
            found,
            pltpu.VMEM((CT, CZ, CX, CY), F32),
            pltpu.SemaphoreType.DMA((2 * CT,)),
        ],
        input_output_aliases={3: 0},
        compiler_params=pltpu.CompilerParams(vmem_limit_bytes=32 << 20),
    )(lp, every, bound, result)


def solution(mesh):
    return jax.shard_map(
        local,
        mesh=mesh,
        in_specs=(P("tm", "space", None, None), P("tm", "space", None, None)),
        out_specs=P("tm", "space", None, None),
        check_vma=False,
    )
```

```python
import jax
import jax.numpy as jnp
from jax import lax
from jax.experimental import pallas as pl
from jax.experimental.pallas import tpu as pltpu
from jax.sharding import PartitionSpec as P

CX = 16
CY = 128
CT = 4
CZ = 8
OV = 2
SWEEPS = 4
CHEB = 8
LANES = 128
NEAR = 4
WINDOW = 16
TURN = 5
EARLY = (5, 7, 6, 4, 3, 2, 1, 0)
LATE = (2, 3, 4, 5, 6, 7, 1, 0)

rate = 8.0
react = 0.5
damp = 0.9
theta = 0.8
delta = 0.6

F32 = jnp.float32
PLANE = (CX, CY)
VMEM = pl.BlockSpec(memory_space=pltpu.VMEM)


def beside(v):
    total = pltpu.roll(v, 1, 0) + pltpu.roll(v, CX - 1, 0)
    return total + (pltpu.roll(v, 1, 1) + pltpu.roll(v, CY - 1, 1))


def swept(v, first, scale, near, before):
    total = beside(v)
    for plane in near:
        if plane is not None:
            total = total + plane
    if before is not None:
        total = total + rate * before
    return (1.0 - damp) * v + first + scale * total


def by_parity(body, first, second):
    odd = at_ref[0] & 1

    @pl.when(odd == 0)
    def _():
        body(first, second)

    @pl.when(odd == 1)
    def _():
        body(second, first)


def by_parity(body, first, second):
    odd = lax.axis_index("space") & 1

    @pl.when(odd == 0)
    def _():
        body(first, second)

    @pl.when(odd == 1)
    def _():
        body(second, first)


def first_kernel(loaded_ref, own_ref, outer_ref, inner_ref):
    def body(low_ref, high_ref):
        for t in range(CT):
            for z in range(CZ):
                rhs, s = loaded_ref[0, t, z], loaded_ref[1, t, z]
                diag = (rate + 6.0 - react) + (3.0 * react) * (s * s)
                scale = damp / diag
                first = scale * rhs
                for which, value in enumerate((scale, first, diag, rhs)):
                    own_ref[which, t, z] = value
                if z < OV:
                    low_ref[0, t, z], low_ref[1, t, z] = scale, first
                if z >= CZ - OV:
                    high_ref[0, t, z - (CZ - OV)] = scale
                    high_ref[1, t, z - (CZ - OV)] = first

    by_parity(body, outer_ref, inner_ref)


def reader(which, own_ref, low_ref, high_ref):
    def read(t, z):
        if z < 0:
            return low_ref[which, t, z + OV]
        if z >= CZ:
            return high_ref[which, t, z - CZ]
        return own_ref[which, t, z]

    return read


def inner_kernel(own_ref, out_ref):
    a, b = CT - 2, CT - 1

    def scale(t, z):
        return own_ref[0, t, z]

    def first(t, z):
        return own_ref[1, t, z]

    for z in range(CZ):
        out_ref[z] = first(b, z)
    for z in range(1, CZ - 1):
        v = first(b, z)
        near = (first(b, z - 1), first(b, z + 1))
        out_ref[CZ + z - 1] = swept(v, v, scale(b, z), near, first(a, z))
    for z in range(2, CZ - 2):
        v = first(a, z)
        second = swept(v, v, scale(a, z), (first(a, z - 1), first(a, z + 1)), None)
        near = (out_ref[CZ + z - 2], out_ref[CZ + z])
        out_ref[2 * CZ + z - 4] = swept(
            out_ref[CZ + z - 1], first(b, z), scale(b, z), near, second
        )


FIRST_ENDS = (-2, -1, CZ, CZ + 1)
SECOND_ENDS = (-1, 0, CZ - 1, CZ)
THIRD_ENDS = (0, 1, CZ - 2, CZ - 1)


def earlier_step(inside_ref, ends_ref):
    def first(z):
        return ends_ref[FIRST_ENDS.index(z)] if z in FIRST_ENDS else inside_ref[z]

    def second(z):
        if z in SECOND_ENDS:
            return ends_ref[4 + SECOND_ENDS.index(z)]
        return inside_ref[CZ + z - 1]

    def third(z):
        if z in THIRD_ENDS:
            return ends_ref[8 + THIRD_ENDS.index(z)]
        return inside_ref[2 * CZ + z - 4]

    return first, second, third


def later_kernel(own_ref, outer_ref, inner_ref, inside_ref, out_ref):
    a, b = CT - 2, CT - 1

    def body(low_ref, high_ref):
        scale = reader(0, own_ref, low_ref, high_ref)
        first = reader(1, own_ref, low_ref, high_ref)
        _, second, _ = earlier_step(inside_ref, out_ref)
        for k, z in enumerate(FIRST_ENDS):
            out_ref[k] = first(b, z)
        for k, z in enumerate(SECOND_ENDS):
            v = first(b, z)
            near = (first(b, z - 1), first(b, z + 1))
            out_ref[4 + k] = swept(v, v, scale(b, z), near, first(a, z))
        for k, z in enumerate(THIRD_ENDS):
            v = first(a, z)
            before = swept(v, v, scale(a, z), (first(a, z - 1), first(a, z + 1)), None)
            near = (second(z - 1), second(z + 1))
            out_ref[8 + k] = swept(second(z), first(b, z), scale(b, z), near, before)

    by_parity(body, outer_ref, inner_ref)


def fold_matrix(rows, columns, fine_first):
    i = lax.broadcasted_iota(jnp.int32, (rows, columns), 0)
    k = lax.broadcasted_iota(jnp.int32, (rows, columns), 1)
    fine, lane = (i, k) if fine_first else (k, i)
    return jnp.where(lax.shift_right_logical(fine, 2) == (lane & (CY // 4 - 1)), 1.0, 0.0)


def x_mask():
    x = lax.broadcasted_iota(jnp.int32, PLANE, 0)
    lane = lax.broadcasted_iota(jnp.int32, PLANE, 1)
    return jnp.where(lax.shift_right_logical(x, 2) == lax.shift_right_logical(lane, 5), 1.0, 0.0)


def early_kernel(own_ref, outer_ref, inner_ref, v2_ref, v3_ref, v4_ref, rest_ref):
    def body(low_ref, high_ref):
        scale = reader(0, own_ref, low_ref, high_ref)
        first = reader(1, own_ref, low_ref, high_ref)
        for t in range(CT):
            for z in range(-2, CZ + 2):
                v = first(t, z)
                near = [first(t, q) for q in (z - 1, z + 1) if -2 <= q < CZ + 2]
                before = first(t - 1, z) if t > 0 else None
                v2_ref[t, z + 2] = swept(v, v, scale(t, z), near, before)
        for t in range(1, CT):
            for z in range(-1, CZ + 1):
                near = (v2_ref[t, z + 1], v2_ref[t, z + 3])
                before = v2_ref[t - 1, z + 2] if t > 1 else None
                v3_ref[t - 1, z + 1] = swept(
                    v2_ref[t, z + 2], first(t, z), scale(t, z), near, before
                )
        for t in range(2, CT):
            for z in range(CZ):
                near = (v3_ref[t - 1, z], v3_ref[t - 1, z + 2])
                before = v3_ref[t - 2, z + 1] if t > 2 else None
                v4_ref[t - 2, z] = swept(
                    v3_ref[t - 1, z + 1], first(t, z), scale(t, z), near, before
                )

    by_parity(body, outer_ref, inner_ref)
    for z in range(CZ):
        rest = own_ref[3, 0, z] - own_ref[2, CT - 1, z] * v4_ref[1, z]
        for t in range(1, CT):
            rest = rest + own_ref[3, t, z]
        rest_ref[z] = rest


def exact_dot(x, ones):
    parts = []
    for _ in range(3):
        part = x.astype(jnp.bfloat16)
        parts.append(part)
        x = x - part.astype(F32)
    ones = ones.astype(jnp.bfloat16)
    high, mid, low = (jnp.dot(part, ones, preferred_element_type=F32) for part in parts)
    return high + (mid + low)


def fold(planes):
    folded = exact_dot(planes.reshape(-1, CY), fold_matrix(CY, LANES, True))
    return jnp.sum(folded.reshape(-1, CX, LANES) * x_mask()[None], axis=1)


def coef_kernel(own_ref, out_ref, stack):
    for b in range(2):
        sums = []
        for t in range(CT):
            near = [own_ref[2, t, z] for z in range(4 * b, 4 * b + 4)]
            sums.append((near[0] + near[1]) + (near[2] + near[3]))
        total = (sums[0] + sums[1]) + (sums[2] + sums[3])
        stack[b] = (total - 4 * CT * (rate + 6.0)) * (1.0 / react)
    out_ref[...] = jnp.zeros_like(out_ref)
    out_ref[4:6] = fold(stack[...])


def main_kernel(
    own_ref,
    outer_ref,
    inner_ref,
    v2_ref,
    v3_ref,
    v4_ref,
    rest_ref,
    inside_ref,
    ends_ref,
    lp_ref,
    sums_ref,
    v2,
    v3,
    stack,
):
    first_before, second_before, third_before = earlier_step(inside_ref, ends_ref)

    def body(low_ref, high_ref):
        scale = reader(0, own_ref, low_ref, high_ref)
        own = reader(1, own_ref, low_ref, high_ref)
        for z in range(-2, CZ + 2):
            v2[z + 2] = v2_ref[0, z + 2] + rate * scale(0, z) * first_before(z)
        for z in range(-1, CZ + 1):
            near = (v2[z + 1], v2[z + 3])
            before = second_before(z)
            v3[0, z + 1] = swept(v2[z + 2], own(0, z), scale(0, z), near, before)
            v3[1, z + 1] = v3_ref[0, z + 1] + rate * scale(1, z) * v2[z + 2]

    by_parity(body, outer_ref, inner_ref)

    rest = []
    planes = []
    for z in range(CZ):
        part = rest_ref[z]
        early = None
        for t in range(CT - 1):
            scale = own_ref[0, t, z]
            if t < 2:
                before = third_before(z) if t == 0 else v3[0, z + 1]
                near = (v3[t, z], v3[t, z + 2])
                value = swept(v3[t, z + 1], own_ref[1, t, z], scale, near, before)
            else:
                value = v4_ref[0, z] + rate * scale * v3[1, z + 1]
            lp_ref[t, z] = value
            part = part - own_ref[2, t, z] * value
            early = value if early is None else early + value
        value = v4_ref[1, z]
        lp_ref[CT - 1, z] = value
        rest.append(part + rate * early)
        planes.append(early + value)
    odd = (lax.axis_index("tm") & 1) == 1
    for b in range(2):
        z = 4 * b
        total = planes[z] + planes[z + 1] + planes[z + 2] + planes[z + 3]
        inner = planes[z] + planes[z + 3] + 2.0 * (planes[z + 1] + planes[z + 2])
        inner = inner + (planes[4] if b == 0 else planes[3])
        value = rest[z] + rest[z + 1] + rest[z + 2] + rest[z + 3]
        value = value + beside(total) + inner
        last = v4_ref[1, z] + v4_ref[1, z + 1]
        last = rate * (last + (v4_ref[1, z + 2] + v4_ref[1, z + 3]))
        stack[b] = jnp.where(odd, value, value + last)
        stack[4 + b] = jnp.where(odd, last, 0.0)
    stack[2] = planes[0]
    stack[3] = planes[CZ - 1]
    none = jnp.zeros((2, LANES), F32)
    sums_ref[...] = jnp.concatenate([fold(stack[...]), none], axis=0)


def share_kernel(sums_ref, coef_ref, other_coef_ref, out_ref):
    odd = (lax.axis_index("tm") & 1) == 1
    sums = sums_ref[...] + jnp.where(odd, 0.0, coef_ref[...] + other_coef_ref[...])
    out_ref[...] = jnp.broadcast_to(sums[None], out_ref.shape)


def window_kernel(all_ref, out_ref, rows):
    plane = lax.axis_index("space")
    count = all_ref.shape[0]
    parts = [all_ref[lax.rem(plane + (2 * count - TURN - NEAR + k), count)] for k in range(2 * NEAR + 1)]
    for k, part in enumerate(parts):
        low, high = part[0:1], part[1:2]
        if k > 0:
            low = low + parts[k - 1][3:4]
        if k < 2 * NEAR:
            high = high + parts[k + 1][2:3]
        if k > 0:
            rows[0, 2 * k - 1 : 2 * k] = low
            rows[1, 2 * k - 1 : 2 * k] = part[4:5]
        if k < 2 * NEAR:
            rows[0, 2 * k : 2 * k + 1] = high
            rows[1, 2 * k : 2 * k + 1] = part[5:6]
    value = rows[...]
    for k in range(out_ref.shape[0]):
        out_ref[k] = value


def coarse_steps(all_ref, bound_ref):
    lane = lax.broadcasted_iota(jnp.int32, (WINDOW, LANES), 1) & (CY // 4 - 1)
    width = CY // 4
    is_first, is_last = lane == 0, lane == width - 1

    def around(f):
        total = pltpu.roll(f, width, 1) + pltpu.roll(f, LANES - width, 1)
        after = jnp.where(is_last, pltpu.roll(f, width - 1, 1), pltpu.roll(f, LANES - 1, 1))
        before = jnp.where(is_first, pltpu.roll(f, LANES - width + 1, 1), pltpu.roll(f, 1, 1))
        return (total + (pltpu.roll(f, 1, 0) + pltpu.roll(f, WINDOW - 1, 0))) + (after + before)

    slots = all_ref.shape[0] // 2
    order = EARLY if bound_ref is None else LATE

    def slab(k, which):
        return all_ref[order.index(k), which]

    inverse = []
    resid = []
    for k in range(slots):
        rhs = slab(2 * k, 0) + slab(2 * k + 1, 0)
        if k > 0:
            rhs = rhs + slab(2 * k - 1, 1)
        elif bound_ref is not None:
            rhs = rhs + handed(bound_ref, 4)
        coef = slab(2 * k, 1)
        inv = 1.0 / (1.375 + (react / 512.0) * coef)
        inverse.append(inv)
        resid.append((rhs * (1.0 / 512.0)) * inv)
    step = [r * (1.0 / theta) for r in resid]
    sol = list(step)
    rho = delta / theta
    last = []
    beside = [i * (1.0 / 16.0) for i in inverse]
    for m in range(1, CHEB):
        nxt = 1.0 / (2.0 * theta / delta - rho)
        last.append(step[-1])
        known = []
        for k in range(slots):
            value = resid[k] - step[k]
            if k > 0:
                value = value + step[k - 1] * inverse[k]
            elif bound_ref is not None:
                value = value + handed(bound_ref, m - 1 if m <= 4 else m) * inverse[k]
            known.append(value)
        for k in range(slots):
            resid[k] = known[k] + around(step[k]) * beside[k]
        for k in range(slots):
            step[k] = (nxt * rho) * step[k] + (2.0 * nxt / delta) * resid[k]
            sol[k] = sol[k] + step[k]
        rho = nxt
    return sol, last


def swapped(v):
    return jnp.concatenate([v[WINDOW // 2 :], v[: WINDOW // 2]], axis=0)


def handed(bound_ref, k):
    if k == 3:
        none = jnp.zeros((WINDOW // 4, LANES), F32)
        return jnp.concatenate([none, bound_ref[6], none], axis=0)
    at = (0, 2, 4, None, 7, 4, 2, 0)[k]
    both = (bound_ref[at], bound_ref[at + 1])
    return jnp.concatenate(both if k <= 4 else both[::-1], axis=0)


def bound_kernel(all_ref, out_ref, mine_ref, found):
    @pl.when(lax.axis_index("tm") < all_ref.shape[0])
    def _():
        sol, last = coarse_steps(all_ref, None)
        row = lax.broadcasted_iota(jnp.int32, (WINDOW, LANES), 0)
        for m in range(3):
            used = (row > m) & (row < WINDOW - 1 - m)
            block = jnp.where(used, last[m], swapped(last[6 - m]))
            out_ref[2 * m], out_ref[2 * m + 1] = block[: WINDOW // 2], block[WINDOW // 2 :]
        out_ref[6] = last[3][WINDOW // 4 : 3 * WINDOW // 4]
        for h in range(2):
            half = pl.ds(h * WINDOW // 2, WINDOW // 2)
            out_ref[7 + h] = all_ref[EARLY.index(all_ref.shape[0] - 1), 1, half]
        mine_ref[...] = own_slot(sol, found)


def own_slot(sol, found):
    for k, value in enumerate(sol):
        found[k] = value
    return found[lax.rem(lax.axis_index("tm"), 2 * len(sol)) // 2]


def spread(window):
    mask = x_mask()
    mine = 2 * NEAR - 1
    both = [window[mine + b : mine + b + 1] * mask for b in range(2)]
    fine = exact_dot(jnp.concatenate(both, axis=0), fold_matrix(LANES, CY, False))
    return [fine[b * CX : (b + 1) * CX] for b in range(2)]


def result_kernel(lp_ref, mine_ref, out_ref):
    for b, value in enumerate(spread(mine_ref[...])):
        for t in range(CT):
            for z in range(4 * b, 4 * b + 4):
                out_ref[t, z] = lp_ref[t, z] + value


def second_half_kernel(lp_ref, all_ref, bound_ref, _, out_ref, found, result, sems):
    @pl.when(lax.axis_index("tm") >= all_ref.shape[0])
    def _():
        sol, _ = coarse_steps(all_ref, bound_ref)
        values = spread(own_slot(sol, found))
        copies = []
        for t in range(CT):
            for b, value in enumerate(values):
                for z in range(4 * b, 4 * b + 4):
                    result[t, z] = lp_ref[t, z] + value
                part = pl.ds(4 * b, 4)
                copy = pltpu.make_async_copy(
                    result.at[t, part], out_ref.at[t, part], sems.at[2 * t + b]
                )
                copy.start()
                copies.append(copy)
        for copy in copies:
            copy.wait()


def call(kernel, shapes, count, scratch=()):
    single = not isinstance(shapes, (list, tuple))
    return pl.pallas_call(
        kernel,
        out_shape=shapes if single else list(shapes),
        in_specs=[VMEM] * count,
        out_specs=VMEM if single else [VMEM] * len(shapes),
        scratch_shapes=list(scratch),
        compiler_params=pltpu.CompilerParams(vmem_limit_bytes=32 << 20),
    )


def arr(*shape):
    return jax.ShapeDtypeStruct(shape, F32)


def local(right_side, state):
    slabs = lax.axis_size("tm")
    planes = lax.axis_size("space")
    half = slabs // 2
    across = [(k, (k + 1) % planes) for k in range(1, planes, 2)]
    across += [(b, a) for a, b in across]
    within = [(k, k + 1) for k in range(0, planes, 2)]
    within += [(b, a) for a, b in within]
    onward = [(i, i + 1) for i in range(slabs - 1)]

    edge = arr(2, CT, OV, CX, CY)
    own, outer, inner = call(first_kernel, [arr(4, CT, CZ, CX, CY), edge, edge], 1)(
        jnp.stack([right_side, state])
    )
    outer = lax.ppermute(outer, "space", across)
    inner = lax.ppermute(inner, "space", within)
    inside = call(inner_kernel, arr(3 * CZ - 6, CX, CY), 1)(own)
    passed = lax.ppermute(inside, "tm", onward)
    sent = call(later_kernel, arr(12, CX, CY), 4)(own, outer, inner, inside)
    ends = lax.ppermute(sent, "tm", onward)
    v2, v3, v4, rest = call(
        early_kernel,
        [
            arr(CT, CZ + 4, CX, CY),
            arr(CT - 1, CZ + 2, CX, CY),
            arr(CT - 2, CZ, CX, CY),
            arr(CZ, CX, CY),
        ],
        3,
    )(own, outer, inner)
    coef = call(coef_kernel, arr(8, LANES), 1, [pltpu.VMEM((2, CX, CY), F32)])(own)
    other_coef = lax.ppermute(coef, "tm", [(i, i - 1) for i in range(1, slabs, 2)])
    lp, sums = call(
        main_kernel,
        [arr(CT, CZ, CX, CY), arr(8, LANES)],
        9,
        [
            pltpu.VMEM((CZ + 4, CX, CY), F32),
            pltpu.VMEM((2, CZ + 2, CX, CY), F32),
            pltpu.VMEM((6, CX, CY), F32),
        ],
    )(own, outer, inner, v2, v3, v4, rest, passed, ends)
    sums = call(share_kernel, arr(planes, 8, LANES), 3)(sums, coef, other_coef)
    column = lax.all_to_all(
        sums, "space", 0, 0, axis_index_groups=[[(p + TURN) % planes for p in range(planes)]]
    )
    window = call(
        window_kernel,
        arr(half, 2, WINDOW, LANES),
        1,
        [pltpu.VMEM((2, WINDOW, LANES), F32)],
    )(column)
    halves = [list(EARLY), [half + k for k in LATE]]
    every = lax.all_to_all(window, "tm", 0, 0, axis_index_groups=halves)
    found = pltpu.VMEM((half // 2, WINDOW, LANES), F32)
    last, mine = call(bound_kernel, [arr(9, WINDOW // 2, LANES), arr(WINDOW, LANES)], 1, [found])(every)
    quarter = half // 2
    order = (0, 2, 1, 3, 6, 5, 4, 7) if half == 8 else tuple(range(half))
    serve = [((quarter + k) % half, half + order[k]) for k in range(half)]
    bound = lax.ppermute(last, "tm", serve)
    shape = arr(CT, CZ, CX, CY)
    result = call(result_kernel, shape, 2)(lp, mine)
    anywhere = pl.BlockSpec(memory_space=pl.ANY)
    return pl.pallas_call(
        second_half_kernel,
        out_shape=shape,
        in_specs=[VMEM, VMEM, VMEM, anywhere],
        out_specs=anywhere,
        scratch_shapes=[
            found,
            pltpu.VMEM((CT, CZ, CX, CY), F32),
            pltpu.SemaphoreType.DMA((2 * CT,)),
        ],
        input_output_aliases={3: 0},
        compiler_params=pltpu.CompilerParams(vmem_limit_bytes=32 << 20),
    )(lp, every, bound, result)


def solution(mesh):
    return jax.shard_map(
        local,
        mesh=mesh,
        in_specs=(P("tm", "space", None, None), P("tm", "space", None, None)),
        out_specs=P("tm", "space", None, None),
        check_vma=False,
    )
```
